32 devices in a mesh: head: 4 (over x, core), batch: 8 (over z, y).
Axes of the slice: x: 2, y: 2, z: 4, core: 2. Of those that a mesh axis runs over, the one named last changes fastest.
Arguments:
- content: bfloat16 [8, 512, 768], P('batch', 'head'), may hold values from -6 to 6
- query_stream: bfloat16 [8, 96, 768], P('batch', 'head'), may hold values from -6 to 6
- memory: bfloat16 [8, 384, 768], P('batch', 'head'), may hold values from -6 to 6
- has_memory: int32 [8], P('batch'), may hold values 0 or 1
- order_rank: int32 [8, 512], P('batch'), may hold values from 0 to 511, as said below
- targets: int32 [8, 96], P('batch'), may hold values from 0 to 511, as said below
- segments: int32 [8, 512], P('batch'), may hold values from 0 to 1, never falling along the last dimension, each value on 1 to 384 neighbouring positions
- query_weight: bfloat16 [768, 768], P(None, 'head'), may hold values from -0.21875 to 0.21875
- key_weight: bfloat16 [768, 768], P(None, 'head'), may hold values from -0.21875 to 0.21875
- value_weight: bfloat16 [768, 768], P(None, 'head'), may hold values from -0.21875 to 0.21875
- output_weight: bfloat16 [768, 768], P('head'), may hold values from -3.5 to 3.5
- relative_weight: bfloat16 [768, 768], P(None, 'head'), may hold values from -0.21875 to 0.21875
- word_bias: bfloat16 [12, 64], P('head'), may hold values from -3 to 3
- position_bias: bfloat16 [12, 64], P('head'), may hold values from -3 to 3
- segment_bias: bfloat16 [12, 64], P('head'), may hold values from -3 to 3
- segment_embed: bfloat16 [2, 12, 64], P(None, 'head'), may hold values from -3 to 3
- first_gain: bfloat16 [768], replicated, may hold values from 0.5 to 1.5
- first_shift: bfloat16 [768], replicated, may hold values from -2 to 2
- inner_weight: bfloat16 [768, 3072], P(None, 'head'), may hold values from -0.21875 to 0.21875
- inner_bias: bfloat16 [3072], P('head'), may hold values from -2 to 2
- outer_weight: bfloat16 [3072, 768], P('head'), may hold values from -0.109375 to 0.109375
- outer_bias: bfloat16 [768], replicated, may hold values from -2 to 2
- second_gain: bfloat16 [768], replicated, may hold values from 0.5 to 1.5
- second_shift: bfloat16 [768], replicated, may hold values from -2 to 2
- content_cotangent: bfloat16 [8, 512, 768], P('batch', 'head'), may hold values from -6 to 6
- query_cotangent: bfloat16 [8, 96, 768], P('batch', 'head'), may hold values from -6 to 6
Outputs:
- content_out: bfloat16 [8, 512, 768], P('batch', 'head')
- query_out: bfloat16 [8, 96, 768], P('batch', 'head')
- content_grad: float32 [8, 512, 768], P('batch', 'head')
- query_grad: float32 [8, 96, 768], P('batch', 'head')
- query_weight_grad: float32 [768, 768], P(None, 'head')
- key_weight_grad: float32 [768, 768], P(None, 'head')
- value_weight_grad: float32 [768, 768], P(None, 'head')
- output_weight_grad: float32 [768, 768], P('head')
- relative_weight_grad: float32 [768, 768], P(None, 'head')
- word_bias_grad: float32 [12, 64], P('head')
- position_bias_grad: float32 [12, 64], P('head')
- segment_bias_grad: float32 [12, 64], P('head')
- segment_embed_grad: float32 [2, 12, 64], P(None, 'head')
- first_gain_grad: float32 [768], replicated
- first_shift_grad: float32 [768], replicated
- inner_weight_grad: float32 [768, 3072], P(None, 'head')
- inner_bias_grad: float32 [3072], P('head')
- outer_weight_grad: float32 [3072, 768], P('head')
- outer_bias_grad: float32 [768], replicated
- second_gain_grad: float32 [768], replicated
- second_shift_grad: float32 [768], replicated
The draws below stay inside these ranges and needn't reach their ends.
Inputs may be any that keep to these rules, and one draw needn't show every extreme that they name: `order_rank`: each row is a permutation of 0 to 511. `targets`: each row lists in ascending order the 96 positions whose order_rank is 416 or more. `segments`: never falling along a row.
All inputs are finite; a program needn't handle non-finite values. No bound on the sum of `has_memory` on one device may be relied on, other than what follows from the above.
Results may differ from the reference program's by a relative error of at most 0.023.
Values may be sent and summed in bfloat16 or wider, within the bound.
No kernel may reach another device: no remote copies, remote signals or barrier semaphores. Data moves between devices by JAX's collectives and lax.ppermute only.
A program may use at most 320 MiB of HBM per device.

```python
import math
import jax
import jax.numpy as jnp
import numpy as np
from jax import lax

D = 768
HEADS = 12
HEAD_DIM = 64
FF = 3072
LEN = 512
MEM = 384
PRED = 96
SEQS = 8


def ranking(key):
    seq_keys = jax.random.split(jax.random.fold_in(key, 7), SEQS)

    def draw_one(seq_key):
        return jax.random.permutation(seq_key, LEN)
    return jax.vmap(draw_one)(seq_keys).astype(jnp.int32)


def draw_order_rank(key, part):
    return ranking(key)


def draw_targets(key, part):
    ranks = ranking(key)
    by_rank = jnp.argsort(ranks, axis=1, stable=True)
    return jnp.sort(by_rank[:, LEN - PRED:], axis=1).astype(jnp.int32)


def plant(values, own_key, low, top_value):
    extent = values.shape
    spot = [jax.random.randint(jax.random.fold_in(own_key, axis), (), 0, extent[axis]) for axis in range(len(extent))]
    values = values.at[tuple(spot)].set(low)
    longest = extent.index(max(extent))
    spot[longest] = (spot[longest] + 1) % extent[longest]
    return values.at[tuple(spot)].set(top_value)


def block_levels(rng, extent, cuts, smallest, high):
    def one(position, shards_of):
        steps = jax.random.uniform(jax.random.fold_in(jax.random.fold_in(rng, 6), position), (shards_of,), jnp.float32, smallest / len(cuts), high / len(cuts))
        return jnp.repeat(jnp.exp(steps), extent[position] // shards_of).reshape((-1,) + (1,) * (len(extent) - position - 1))

    level = one(*cuts[0])
    for cut in cuts[1:]:
        level = level * one(*cut)
    return level


def split_up(number_of, total, bound, skew):
    weights = [(1 << 20) // math.isqrt(rank ** skew) + 1 for rank in range(2, number_of + 1)]
    surplus, holding = total - bound - (number_of - 1), [1] * (number_of - 1)
    while surplus > 0:
        candidates = [i for i in range(number_of - 1) if holding[i] < bound]
        pool, remaining = sum([weights[i] for i in candidates]), surplus
        for i in candidates:
            extra = min(bound - holding[i], max(1, remaining * weights[i] // pool), surplus)
            holding[i] = holding[i] + extra
            surplus = surplus - extra
    return np.array([bound] + holding)


def ragged_sizes(own_key, count, total, bound, slope):
    if count == 2:
        one = jax.random.randint(own_key, (), max(1, total - bound), min(bound, total - 1) + 1)
        return jnp.stack([one, total - one])
    sizes = jnp.asarray(split_up(count, total, bound, slope), jnp.int32)
    pairs = (count - 1) // 2
    giver, sink = sizes[1:1 + 2 * pairs:2], sizes[2:2 + 2 * pairs:2]
    room = jnp.minimum(giver - 1, bound - sink)
    shifted = jax.random.randint(jax.random.fold_in(own_key, 1), (pairs,), 0, 1 << 20) % (room + 1)
    sizes = sizes.at[1:1 + 2 * pairs:2].set(giver - shifted).at[2:2 + 2 * pairs:2].set(sink + shifted)
    return sizes[jax.random.permutation(jax.random.fold_in(own_key, 2), count)]


def bell_draw(key, dims, scale, bound, shards=(), kind=jnp.bfloat16):
    loudness = block_levels(key, dims, shards, -0.22, 0.18) if shards else 1.0
    drawn = jax.random.normal(key, dims, jnp.float32) * scale * loudness
    return jnp.minimum(jnp.maximum(drawn, -bound), bound).astype(kind)


def setup_inputs(seed: int = 0) -> dict:
    streams_of = jax.random.split(jax.random.key(seed), 27)
    content = bell_draw(streams_of[0], (SEQS, LEN, D), 1.0, 6.0, ((0, 8), (1, 4)))
    query_stream = bell_draw(streams_of[1], (SEQS, PRED, D), 1.0, 6.0, ((0, 8), (1, 4)))
    memory = bell_draw(streams_of[2], (SEQS, MEM, D), 1.0, 6.0, ((0, 8), (1, 4)))
    has_memory = plant((jax.random.randint(streams_of[3], (SEQS,), 0, 4) < 3).astype(jnp.int32), jax.random.fold_in(streams_of[3], 1), 0, 1)
    order_rank = draw_order_rank(jax.random.fold_in(streams_of[26], 71), 0)
    targets = draw_targets(jax.random.fold_in(streams_of[26], 71), 0)
    segments = jax.vmap(lambda own: jnp.searchsorted(jnp.cumsum(ragged_sizes(own, 2, LEN, LEN * 3 // 4, 0)), jnp.arange(LEN), side="right"))(jax.random.split(streams_of[6], SEQS)).reshape((SEQS, LEN)).astype(jnp.int32)
    query_weight = bell_draw(streams_of[7], (D, D), D ** -0.5, 0.21875, ((1, 4),))
    key_weight = bell_draw(streams_of[8], (D, D), D ** -0.5, 0.21875, ((1, 4),))
    value_weight = bell_draw(streams_of[9], (D, D), D ** -0.5, 0.21875, ((1, 4),))
    output_weight = bell_draw(streams_of[10], (D, D), (max(D // 256, 1)) ** -0.5, 3.5, ((0, 4),))
    relative_weight = bell_draw(streams_of[11], (D, D), D ** -0.5, 0.21875, ((1, 4),))
    word_bias = bell_draw(streams_of[12], (HEADS, HEAD_DIM), 0.5, 3.0, ((0, 4),))
    position_bias = bell_draw(streams_of[13], (HEADS, HEAD_DIM), 0.5, 3.0, ((0, 4),))
    segment_bias = bell_draw(streams_of[14], (HEADS, HEAD_DIM), 0.5, 3.0, ((0, 4),))
    segment_embed = bell_draw(streams_of[15], (2, HEADS, HEAD_DIM), 0.5, 3.0, ((1, 4),))
    first_gain = jnp.clip(1.0 + 0.1 * jax.random.normal(streams_of[16], (D,), jnp.float32), 0.5, 1.5).astype(jnp.bfloat16)
    first_shift = bell_draw(streams_of[17], (D,), 0.3, 2.0)
    inner_weight = bell_draw(streams_of[18], (D, FF), D ** -0.5, 0.21875, ((1, 4),))
    inner_bias = bell_draw(streams_of[19], (FF,), 0.3, 2.0, ((0, 4),))
    outer_weight = bell_draw(streams_of[20], (FF, D), FF ** -0.5, 0.109375, ((0, 4),))
    outer_bias = bell_draw(streams_of[21], (D,), 0.3, 2.0)
    second_gain = jnp.clip(1.0 + 0.1 * jax.random.normal(streams_of[22], (D,), jnp.float32), 0.5, 1.5).astype(jnp.bfloat16)
    second_shift = bell_draw(streams_of[23], (D,), 0.3, 2.0)
    content_cotangent = bell_draw(streams_of[24], (SEQS, LEN, D), 1.0, 6.0, ((0, 8), (1, 4)))
    query_cotangent = bell_draw(streams_of[25], (SEQS, PRED, D), 1.0, 6.0, ((0, 8), (1, 4)))
    return {"content": content, "query_stream": query_stream, "memory": memory, "has_memory": has_memory, "order_rank": order_rank, "targets": targets, "segments": segments, "query_weight": query_weight, "key_weight": key_weight, "value_weight": value_weight, "output_weight": output_weight, "relative_weight": relative_weight, "word_bias": word_bias, "position_bias": position_bias, "segment_bias": segment_bias, "segment_embed": segment_embed, "first_gain": first_gain, "first_shift": first_shift, "inner_weight": inner_weight, "inner_bias": inner_bias, "outer_weight": outer_weight, "outer_bias": outer_bias, "second_gain": second_gain, "second_shift": second_shift, "content_cotangent": content_cotangent, "query_cotangent": query_cotangent}


@jax.custom_vjp
def low(v):
    return lax.optimization_barrier(v.astype(jnp.bfloat16)).astype(jnp.float32)

@jax.custom_vjp
def low_back(v):
    return v

def low_keep(v):
    return (low(v), None)

def low_pass(kept, grad):
    return (grad,)

def back_keep(v):
    return (v, None)

def back_low(kept, grad):
    return (low(grad),)
low.defvjp(low_keep, low_pass)
low_back.defvjp(back_keep, back_low)
highest = lax.Precision.HIGHEST
score_scale = 0.125
masked_score = -1e+30
norm_eps = 1e-05
gelu_root = 0.7978845608028654
gelu_cubic = 0.044715

def both_ways(value):
    return low(low_back(value))

def matmul(left, right):
    return jnp.dot(left, right, precision=highest)

def layer_norm(values, gain, shift):
    center = values - lax.optimization_barrier(jnp.mean(values, axis=-1, keepdims=True))
    spread = lax.optimization_barrier(jnp.mean(center * center, axis=-1, keepdims=True))
    return center * lax.rsqrt(spread + norm_eps) * gain + shift

def gelu_tanh(values):
    return 0.5 * values * (1.0 + jnp.tanh(gelu_root * (values + gelu_cubic * values * values * values)))

def positions(key_count, length, width):
    steps = jnp.arange(key_count, -length, -1).astype(jnp.float32)
    freqs = 1.0 / 10000.0 ** (jnp.arange(0, width, 2).astype(jnp.float32) / width)
    angles = steps[:, None] * freqs[None, :]
    return jnp.concatenate([jnp.sin(angles), jnp.cos(angles)], axis=1)

def shift_rows(scores):
    heads, length, total = scores.shape
    return scores.reshape(heads, total, length)[:, 1:].reshape(heads, length, total - 1)[:, :, :total - length]

def slide_rows(scores, offsets, width):

    def one_row(row, start):
        return lax.dynamic_slice_in_dim(row, start, width)
    return jax.vmap(jax.vmap(one_row), in_axes=(0, None))(scores, offsets)

def masks(present, ranks, picks, labels, memory_rows):
    length = ranks.shape[0]
    picked = picks[:, None] == jnp.arange(length, dtype=jnp.int32)[None, :]
    pick_rank = lax.optimization_barrier(jnp.sum(jnp.where(picked, ranks[None, :], 0), axis=1)).astype(jnp.int32)
    pick_label = lax.optimization_barrier(jnp.sum(jnp.where(picked, labels[None, :], 0), axis=1)).astype(jnp.int32)
    limit = jnp.concatenate([ranks + 1, pick_rank])
    key_rank = jnp.concatenate([jnp.full((memory_rows,), -1, jnp.int32), ranks])
    is_memory = jnp.arange(memory_rows + length, dtype=jnp.int32) < memory_rows
    visible = jnp.where(is_memory[None, :], present > 0, key_rank[None, :] < limit[:, None])
    row_label = jnp.concatenate([labels, pick_label])
    key_label = jnp.concatenate([jnp.zeros((memory_rows,), jnp.int32), labels])
    differ = row_label[:, None] != key_label[None, :]
    offsets = (length - picks).astype(jnp.int32)
    return (visible, differ, offsets)

def sequence(params, inputs):
    query_weight, key_weight, value_weight, output_weight, relative_weight, word_bias, position_bias, segment_bias, segment_embed, first_gain, first_shift, inner_weight, inner_bias, outer_weight, outer_bias, second_gain, second_shift = params
    content, query_stream, memory, present, ranks, picks, labels = inputs
    length, width = content.shape
    memory_rows = memory.shape[0]
    heads, head_size = word_bias.shape
    key_count = memory_rows + length
    stream = jnp.concatenate([content, query_stream], axis=0)
    row_count = stream.shape[0]
    joined = jnp.concatenate([memory, content], axis=0)
    visible, differ, offsets = masks(present, ranks, picks, labels, memory_rows)
    query_full = low_back(matmul(stream, query_weight)).reshape(row_count, heads, head_size)
    query_word = low(query_full + word_bias)
    query_place = low(query_full + position_bias)
    query_label = query_full + segment_bias
    keys = both_ways(matmul(joined, key_weight)).reshape(key_count, heads, head_size)
    values = both_ways(matmul(joined, value_weight)).reshape(key_count, heads, head_size)
    table = low(positions(key_count, length, width))
    relative_keys = both_ways(matmul(table, relative_weight)).reshape(key_count + length, heads, head_size)
    content_term = jnp.einsum('ihd,jhd->hij', query_word, keys, precision=highest)
    relative_all = jnp.einsum('ihd,rhd->hir', query_place, relative_keys, precision=highest)
    place_term = jnp.concatenate([shift_rows(relative_all[:, :length]), slide_rows(relative_all[:, length:], offsets, key_count)], axis=1)
    label_same = jnp.einsum('ihd,hd->hi', query_label, segment_embed[0], precision=highest)
    label_other = jnp.einsum('ihd,hd->hi', query_label, segment_embed[1], precision=highest)
    label_term = jnp.where(differ[None], label_other[:, :, None], label_same[:, :, None])
    scores = low_back(jnp.where(visible[None], (content_term + place_term + label_term) * score_scale, masked_score))
    soft_weights = low(jax.nn.softmax(scores, axis=-1))
    attended = both_ways(jnp.einsum('hij,jhd->ihd', soft_weights, values, precision=highest)).reshape(row_count, heads * head_size)
    attention_out = low_back(matmul(attended, output_weight))
    hidden = layer_norm(stream + attention_out, first_gain, first_shift)
    inner = low_back(matmul(low(hidden), inner_weight) + inner_bias)
    outer = low_back(matmul(low(gelu_tanh(inner)), outer_weight) + outer_bias)
    result = layer_norm(hidden + outer, second_gain, second_shift)
    return (result[:length], result[length:])

def reference(content, query_stream, memory, has_memory, order_rank, targets, segments, query_weight, key_weight, value_weight, output_weight, relative_weight, word_bias, position_bias, segment_bias, segment_embed, first_gain, first_shift, inner_weight, inner_bias, outer_weight, outer_bias, second_gain, second_shift, content_cotangent, query_cotangent):
    params = tuple((weight.astype(jnp.float32) for weight in (query_weight, key_weight, value_weight, output_weight, relative_weight, word_bias, position_bias, segment_bias, segment_embed, first_gain, first_shift, inner_weight, inner_bias, outer_weight, outer_bias, second_gain, second_shift)))
    memory_in = memory.astype(jnp.float32)

    def forward(content_in, query_in, weights):

        def step(inputs):
            return sequence(weights, inputs)
        return lax.map(jax.checkpoint(step), (content_in, query_in, memory_in, has_memory, order_rank, targets, segments))
    outputs, pullback = jax.vjp(forward, content.astype(jnp.float32), query_stream.astype(jnp.float32), params)
    content_grad, query_grad, grads = pullback((content_cotangent.astype(jnp.float32), query_cotangent.astype(jnp.float32)))
    return (outputs[0].astype(jnp.bfloat16), outputs[1].astype(jnp.bfloat16), content_grad, query_grad, grads[0], grads[1], grads[2], grads[3], grads[4], grads[5], grads[6], grads[7], grads[8], grads[9], grads[10], grads[11], grads[12], grads[13], grads[14], grads[15], grads[16])
```

```python
import functools
import jax
import jax.numpy as jnp
import numpy as np
from jax import lax
from jax.experimental import pallas as pl
from jax.experimental.pallas import tpu as pltpu
from jax.sharding import PartitionSpec as P

masked_score = -1e30
norm_eps = 1e-05
gelu_root = 0.7978845608028654
gelu_cubic = 0.044715
hidden_key = 1 << 20
F32 = jnp.float32
BF16 = jnp.bfloat16
MIB = 1024 * 1024


def dot_nt(a, b):
    return lax.dot_general(a, b, (((1,), (1,)), ((), ())), preferred_element_type=F32)


def dot_nn(a, b):
    return lax.dot_general(a, b, (((1,), (0,)), ((), ())), preferred_element_type=F32)


def dot_tn(a, b):
    return lax.dot_general(a, b, (((0,), (0,)), ((), ())), preferred_element_type=F32)


def position_rows(key_count, length, width):
    steps = key_count - 1 - np.arange(key_count + length, dtype=np.float64)
    freqs = 10000.0 ** (-np.arange(0, width, 2, dtype=np.float64) / width)
    angles = steps[:, None] * freqs[None, :]
    return np.concatenate([np.sin(angles), np.cos(angles)], axis=1).astype(jnp.bfloat16)


def whole(shape):
    return pl.BlockSpec(shape, lambda *_: (0,) * len(shape))


def call(kernel, name, grid, ins, in_specs, outs, out_specs, scratch=()):
    return pl.pallas_call(
        kernel,
        grid=grid,
        in_specs=in_specs,
        out_specs=out_specs,
        out_shape=[jax.ShapeDtypeStruct(s, t) for s, t in outs],
        scratch_shapes=list(scratch),
        compiler_params=pltpu.CompilerParams(vmem_limit_bytes=52 * MIB),
        name=name,
    )(*ins)


def attend_forward_kernel(
    blocks, head_size, length,
    stream_ref, joined_ref, wq_ref, wkv_ref, rel_ref, col_ref, row_ref, bias_ref, embed_ref, keycol_ref,
    p_ref, att_ref, qf_ref, kc_ref, v_ref, acc_ref,
):
    h = pl.program_id(0)
    keys = joined_ref.shape[0]
    wide = wq_ref.shape[1]

    @pl.when(h == 0)
    def _():
        qf_ref[...] = dot_nn(stream_ref[...], wq_ref[...])
        kv = dot_nn(joined_ref[...], wkv_ref[...])
        kc_ref[...] = (kv[:, :wide] + keycol_ref[...].astype(F32)).astype(BF16)
        v_ref[...] = kv[:, wide:].astype(BF16)
        acc_ref[...] = jnp.zeros_like(acc_ref)

    limit_row = row_ref[0:1, :]
    for start, size, position in blocks:
        blk = slice(start, start + size)
        lane = lax.broadcasted_iota(jnp.int32, (size, wide), 1)
        mine = (lane >= h * head_size) & (lane < (h + 1) * head_size)
        qf = qf_ref[blk, :]
        zero = jnp.zeros_like(qf)
        word = jnp.where(mine, (qf + bias_ref[0:1, :]).astype(BF16).astype(F32) * 0.125, zero)
        place = jnp.where(mine, qf + bias_ref[1:2, :], zero).astype(BF16) * 0.125
        label = jnp.where(mine, (qf + bias_ref[2:3, :]) * 0.125, zero)
        label_hi = label.astype(BF16)
        label_lo = (label - label_hi.astype(F32)).astype(BF16)
        both = dot_nn(label_hi, embed_ref[...]) + dot_nn(label_lo, embed_ref[...])
        row_label = col_ref[blk, 1:2]
        pair = jnp.where(row_label == 0, both[:, :wide], both[:, wide:])
        pair_hi = pair.astype(BF16).astype(F32)
        first = wide - head_size
        hi_lane = (lane == first) | (lane == first + 2)
        lo_lane = (lane == first + 1) | (lane == first + 3)
        query = jnp.where(hi_lane, pair_hi, jnp.where(lo_lane, pair - pair_hi, word)).astype(BF16)
        scores = dot_nt(query, kc_ref[...])
        if position is not None:
            base = length - position - size
            width = keys + size
            rel = dot_nt(place, rel_ref[base : base + width, :])
            rel = pltpu.roll(rel, width - (size - 1), 1, stride=1, stride_axis=0)
        else:
            rel = dot_nt(place, rel_ref[...])
            total = rel.shape[1]
            shift = col_ref[blk, 2:3]
            bit = 0
            while (1 << bit) < length:
                rel = jnp.where(((shift >> bit) & 1) == 1, pltpu.roll(rel, total - (1 << bit), 1), rel)
                bit += 1
        scores = scores + rel[:, :keys]
        limit = col_ref[blk, 0:1]
        scores = jnp.where(limit_row < limit, scores, masked_score)
        top = jnp.max(scores, axis=-1, keepdims=True)
        powers = jnp.exp(scores - top)
        total = jnp.sum(powers, axis=-1, keepdims=True)
        soft = (powers * (1.0 / total)).astype(BF16)
        p_ref[0, blk, :] = soft
        att = dot_nn(soft, v_ref[...])
        acc_ref[blk, :] = jnp.where(mine, att, acc_ref[blk, :])

    @pl.when(h == pl.num_programs(0) - 1)
    def _():
        att_ref[...] = acc_ref[:, : att_ref.shape[1]].astype(BF16)


def attend_forward(blocks, stream, joined, wq, wkv, rel, col, row, bias, embed, keycol, heads, head_size, length):
    rows, keys, wide = stream.shape[0], joined.shape[0], wq.shape[1]
    ins = (stream, joined, wq, wkv, rel, col, row, bias, embed, keycol)
    outs = [
        ((heads, rows, keys), BF16),
        ((rows, heads * head_size), BF16),
        ((rows, wide), F32),
        ((keys, wide), BF16),
        ((keys, wide), BF16),
    ]
    out_specs = [pl.BlockSpec((1, rows, keys), lambda h: (h, 0, 0))] + [whole(s) for s, _ in outs[1:]]
    return call(
        functools.partial(attend_forward_kernel, blocks, head_size, length),
        "attend_forward", (heads,), ins, [whole(x.shape) for x in ins], outs, out_specs,
        [pltpu.VMEM((rows, wide), F32)],
    )


def attend_backward_kernel(
    blocks, head_size, length,
    p_ref, dat_ref, da_ref, qf_ref, qft_ref, kc_ref, v_ref, rel_ref, col_ref, bias_ref, biast_ref, embed_ref,
    dq_ref, kg_ref, vg_ref, rg_ref, small_ref, word_acc, place_acc, label_acc, s_scr, rg_acc,
):
    h = pl.program_id(0)
    keys = kc_ref.shape[0]
    wide = kc_ref.shape[1]
    total_rel = rel_ref.shape[0]
    heads = pl.num_programs(0)
    local = da_ref.shape[1]

    @pl.when(h == 0)
    def _():
        word_acc[...] = jnp.zeros_like(word_acc)
        place_acc[...] = jnp.zeros_like(place_acc)
        label_acc[...] = jnp.zeros_like(label_acc)
        small_ref[...] = jnp.zeros_like(small_ref)

    qft = qft_ref[...]
    word_t = (qft + biast_ref[:, 0:1]).astype(BF16) * 0.125
    place_t = (qft + biast_ref[:, 1:2]).astype(BF16) * 0.125
    rg_acc[...] = jnp.zeros_like(rg_acc)
    first = wide - head_size
    vg_ref[...] = dot_nn(dat_ref[...], p_ref[0]).astype(BF16)
    for start, size, position in blocks:
        blk = slice(start, start + size)
        lane = lax.broadcasted_iota(jnp.int32, (size, wide), 1)
        mine = (lane >= h * head_size) & (lane < (h + 1) * head_size)
        soft = p_ref[0, blk, :].astype(F32)
        grad = jnp.where(mine[:, :local], da_ref[blk, :], 0)
        chance = dot_nt(grad, v_ref[:, :local])
        inner = jnp.sum(chance * soft, axis=-1, keepdims=True)
        score = (soft * (chance - inner)).astype(BF16)
        s_scr[blk, :] = score
        word = dot_nn(score, kc_ref[...]) * 0.125
        word_acc[blk, :] = jnp.where(mine, word, word_acc[blk, :])
        if position is not None:
            base = length - position - size
            width = keys + size
            left = (size - 1) - lax.broadcasted_iota(jnp.int32, (size, 1), 0)
            reach = size
        else:
            base = 0
            width = total_rel
            left = col_ref[blk, 2:3]
            reach = length
        wider = jnp.concatenate([score.astype(F32), jnp.zeros((size, width - keys), F32)], axis=1)
        bit = 0
        while (1 << bit) < reach:
            wider = jnp.where(((left >> bit) & 1) == 1, pltpu.roll(wider, 1 << bit, 1), wider)
            bit += 1
        wider = wider.astype(BF16)
        placed = dot_nn(wider, rel_ref[base : base + width, :]) * 0.125
        place_acc[blk, :] = jnp.where(mine, placed, place_acc[blk, :])
        rg_acc[:, base : base + width] += dot_nn(place_t[:, blk], wider)
        zero_key = word[:, first : first + 1]
        one_key = word[:, first + 2 : first + 3]
        row_label = col_ref[blk, 1:2]
        same = jnp.where(row_label == 0, zero_key, one_key)
        other = jnp.where(row_label == 0, one_key, zero_key)
        label = same * embed_ref[0:1, :] + other * embed_ref[1:2, :]
        label_acc[blk, :] = jnp.where(mine, label, label_acc[blk, :])
        query_label = qf_ref[blk, :] + bias_ref[2:3, :]
        on = mine[0:1, :]
        small_ref[3:4, :] += jnp.where(on, jnp.sum(query_label * same, axis=0, keepdims=True), 0.0)
        small_ref[4:5, :] += jnp.where(on, jnp.sum(query_label * other, axis=0, keepdims=True), 0.0)
    kg_ref[...] = dot_nn(word_t, s_scr[...]).astype(BF16)
    rg_ref[...] = rg_acc[...].astype(BF16)

    @pl.when(h == heads - 1)
    def _():
        word, place, label = word_acc[...], place_acc[...], label_acc[...]
        dq_ref[...] = (word + place + label)[:, :local].astype(BF16)
        small_ref[0:1, :] = jnp.sum(word, axis=0, keepdims=True)
        small_ref[1:2, :] = jnp.sum(place, axis=0, keepdims=True)
        small_ref[2:3, :] = jnp.sum(label, axis=0, keepdims=True)


def attend_backward(blocks, p, dat, da, qf, qft, kc, v, rel, col, bias, biast, embed, head_size, length):
    heads, rows, keys = p.shape
    wide = qf.shape[1]
    local = heads * head_size
    total_rel = rel.shape[0]
    ins = (p, dat, da, qf, qft, kc, v, rel, col, bias, biast, embed)
    specs = [whole(x.shape) for x in ins]
    specs[0] = pl.BlockSpec((1, rows, keys), lambda h: (h, 0, 0))
    specs[1] = pl.BlockSpec((head_size, rows), lambda h: (h, 0))
    specs[4] = pl.BlockSpec((head_size, rows), lambda h: (h, 0))
    specs[10] = pl.BlockSpec((head_size, biast.shape[1]), lambda h: (h, 0))
    outs = [
        ((rows, local), BF16),
        ((local, keys), BF16),
        ((local, keys), BF16),
        ((local, total_rel), BF16),
        ((8, wide), F32),
    ]
    out_specs = [whole((rows, local))]
    out_specs += [pl.BlockSpec((head_size, n), lambda h: (h, 0)) for n in (keys, keys, total_rel)]
    out_specs += [whole((8, wide))]
    return call(
        functools.partial(attend_backward_kernel, blocks, head_size, length),
        "attend_backward", (heads,), ins, specs, outs, out_specs,
        [pltpu.VMEM((rows, wide), F32)] * 3
        + [pltpu.VMEM((rows, keys), BF16), pltpu.VMEM((head_size, total_rel), F32)],
    )


def norm_parts(x):
    center = x - jnp.mean(x, axis=-1, keepdims=True)
    scale = lax.rsqrt(jnp.mean(center * center, axis=-1, keepdims=True) + norm_eps)
    return center * scale, scale


def norm_back(grad, gain, unit, scale):
    along = grad * gain
    return scale * (
        along
        - jnp.mean(along, axis=-1, keepdims=True)
        - unit * jnp.mean(along * unit, axis=-1, keepdims=True)
    )


def feed_forward_kernel(
    core_ref, a0_ref, a1_ref, a2_ref, a3_ref, w0_ref, w1_ref, w2_ref, w3_ref, stream_ref, vec_ref,
    wi_ref, bi_ref, wo_ref,
    hid_ref, act_ref, gp_ref, mixed_ref, mine_ref, other_ref,
):
    half = mine_ref.shape[0]
    core = core_ref[0]
    for step in range(2):
        rows = pl.ds(pl.multiple_of((core if step else 1 - core) * half, 16), half)
        out = dot_nn(a0_ref[rows, :], w0_ref[...]) + dot_nn(a1_ref[rows, :], w1_ref[...])
        out = out + dot_nn(a2_ref[rows, :], w2_ref[...]) + dot_nn(a3_ref[rows, :], w3_ref[...])
        mixed = stream_ref[rows, :].astype(F32) + out
        if step:
            mixed_ref[...] = mixed
        unit, _ = norm_parts(mixed)
        hidden = (unit * vec_ref[0:1, :] + vec_ref[1:2, :]).astype(BF16)
        hid_ref[rows, :] = hidden
        inner = dot_nn(hidden, wi_ref[...]) + bi_ref[0:1, :]
        square = inner * inner
        turn = jnp.tanh(gelu_root * (inner + gelu_cubic * square * inner))
        lift = 0.5 * (1.0 + turn)
        slope = lift + 0.5 * inner * (1.0 - turn * turn) * (gelu_root * (1.0 + 3.0 * gelu_cubic * square))
        active = (inner * lift).astype(BF16)
        act_ref[rows, :] = active
        gp_ref[rows, :] = slope.astype(BF16)
        part = dot_nn(active, wo_ref[...]).astype(BF16)
        if step:
            mine_ref[...] = part
        else:
            other_ref[...] = part


def feed_forward(core, atts, wos, stream, vec, wi, bi, wo):
    rows, width = stream.shape
    units = wi.shape[1]
    half = rows // 2
    ins = (core, *atts, *wos, stream, vec, wi, bi, wo)
    outs = [
        ((rows, width), BF16),
        ((rows, units), BF16),
        ((rows, units), BF16),
        ((half, width), F32),
        ((half, width), BF16),
        ((half, width), BF16),
    ]
    specs = [pl.BlockSpec(memory_space=pltpu.SMEM)] + [whole(x.shape) for x in ins[1:]]
    return call(feed_forward_kernel, "feed_forward", (1,), ins, specs, outs, [whole(s) for s, _ in outs])


def second_norm_kernel(a_ref, b_ref, mixed_ref, cot_ref, vec_ref, out_ref, og_ref, sg_ref, sums_ref):
    unit, _ = norm_parts(mixed_ref[...])
    hidden = unit * vec_ref[0:1, :] + vec_ref[1:2, :]
    total = a_ref[...].astype(F32) + b_ref[...].astype(F32)
    unit, scale = norm_parts(hidden + total + vec_ref[2:3, :])
    out_ref[...] = (unit * vec_ref[3:4, :] + vec_ref[4:5, :]).astype(BF16)
    cot = cot_ref[...].astype(F32)
    grad = norm_back(cot, vec_ref[3:4, :], unit, scale)
    low = grad.astype(BF16)
    og_ref[...] = low
    sg_ref[...] = grad
    sums_ref[...] = jnp.zeros_like(sums_ref)
    sums_ref[0:1, :] = jnp.sum(low.astype(F32), axis=0, keepdims=True)
    sums_ref[1:2, :] = jnp.sum(cot * unit, axis=0, keepdims=True)
    sums_ref[2:3, :] = jnp.sum(cot, axis=0, keepdims=True)


def second_norm(a, b, mixed, cot, vec):
    ins = (a, b, mixed, cot, vec)
    shape = a.shape
    outs = [(shape, BF16), (shape, BF16), (shape, F32), ((8, shape[1]), F32)]
    return call(
        second_norm_kernel, "second_norm", (1,), ins, [whole(x.shape) for x in ins], outs,
        [whole(s) for s, _ in outs],
    )


def feed_backward_kernel(
    core_ref, mine_ref, other_ref, gp_ref, wi_ref, wo_ref, ig_ref, og_ref, bm_ref, bo_ref, sums_ref
):
    half = mine_ref.shape[0]
    core = core_ref[0]
    sums_ref[...] = jnp.zeros_like(sums_ref)
    for step in range(2):
        rows = pl.ds(pl.multiple_of((core if step else 1 - core) * half, 16), half)
        og = mine_ref[...] if step else other_ref[...]
        og_ref[rows, :] = og
        grad = (dot_nt(og, wo_ref[...]) * gp_ref[rows, :].astype(F32)).astype(BF16)
        ig_ref[rows, :] = grad
        sums_ref[0:1, :] += jnp.sum(grad.astype(F32), axis=0, keepdims=True)
        part = dot_nt(grad, wi_ref[...]).astype(BF16)
        if step:
            bm_ref[...] = part
        else:
            bo_ref[...] = part


def feed_backward(core, mine, other, gp, wi, wo):
    rows, units = gp.shape
    half, width = mine.shape
    ins = (core, mine, other, gp, wi, wo)
    outs = [
        ((rows, units), BF16),
        ((rows, width), BF16),
        ((half, width), BF16),
        ((half, width), BF16),
        ((8, units), F32),
    ]
    specs = [pl.BlockSpec(memory_space=pltpu.SMEM)] + [whole(x.shape) for x in ins[1:]]
    return call(feed_backward_kernel, "feed_backward", (1,), ins, specs, outs, [whole(s) for s, _ in outs])


def first_norm_kernel(a_ref, b_ref, sg_ref, mixed_ref, vec_ref, mg_ref, ag_ref, sums_ref):
    grad = sg_ref[...] + a_ref[...].astype(F32) + b_ref[...].astype(F32)
    unit, scale = norm_parts(mixed_ref[...])
    out = norm_back(grad, vec_ref[0:1, :], unit, scale)
    mg_ref[...] = out
    ag_ref[...] = out.astype(BF16)
    sums_ref[...] = jnp.zeros_like(sums_ref)
    sums_ref[0:1, :] = jnp.sum(grad * unit, axis=0, keepdims=True)
    sums_ref[1:2, :] = jnp.sum(grad, axis=0, keepdims=True)


def first_norm(a, b, sg, mixed, vec):
    ins = (a, b, sg, mixed, vec)
    shape = a.shape
    outs = [(shape, F32), (shape, BF16), ((8, shape[1]), F32)]
    return call(
        first_norm_kernel, "first_norm", (1,), ins, [whole(x.shape) for x in ins], outs,
        [whole(s) for s, _ in outs],
    )


def add_kernel(a_ref, b_ref, o_ref):
    o_ref[...] = (a_ref[...].astype(F32) + b_ref[...].astype(F32)).astype(BF16)


def on_device(
    content, query_stream, memory, has_memory, order_rank, targets, segments,
    query_weight, key_weight, value_weight, output_weight, relative_weight,
    word_bias, position_bias, segment_bias, segment_embed, first_gain, first_shift,
    inner_weight, inner_bias, outer_weight, outer_bias, second_gain, second_shift,
    content_cotangent, query_cotangent,
):
    parts = lax.axis_size("head")
    me = lax.axis_index("head")
    core = me % 2
    core_perm = [(i, i ^ 1) for i in range(parts)]
    x_perm = [(i, i ^ 2) for i in range(parts)]

    def swap_core(x):
        return lax.ppermute(x, "head", core_perm)

    def swap_x(x):
        return lax.ppermute(x, "head", x_perm)

    own, width = content.shape[1:]
    own_picks, own_memory = query_stream.shape[1], memory.shape[1]
    length, picks_n, mem = own * parts, own_picks * parts, own_memory * parts
    keys = mem + length
    heads, head_size = word_bias.shape
    local = heads * head_size
    wide = local + head_size
    half = 2 * (own + own_picks)
    rows = 2 * half

    gathered = lax.all_gather(
        jnp.concatenate([content[0], query_stream[0], memory[0]], axis=0), "head", axis=0, tiled=False
    )
    con, pik, mems = (
        gathered[:, :own],
        gathered[:, own : own + own_picks],
        gathered[:, own + own_picks :],
    )
    order = (0, 2, 1, 3)

    def lay(a, b):
        return jnp.concatenate([a[0], a[2], b[0], b[2], a[1], a[3], b[1], b[3]], axis=0)

    stream = lay(con, pik)
    joined = jnp.concatenate([mems.reshape(mem, width), con.reshape(length, width)], axis=0)
    blocks = (
        (0, own, 0),
        (own, own, 2 * own),
        (2 * own, 2 * own_picks, None),
        (half, own, own),
        (half + own, own, 3 * own),
        (half + 2 * own, 2 * own_picks, None),
    )

    ranks, picks, labels = order_rank[0], targets[0], segments[0]
    picked = picks[:, None] == jnp.arange(length, dtype=jnp.int32)[None, :]
    pick_rank = jnp.sum(jnp.where(picked, ranks[None, :], 0), axis=1)
    pick_label = jnp.sum(jnp.where(picked, labels[None, :], 0), axis=1)

    def lay_column(a, b):
        return lay(a.reshape(parts, own), b.reshape(parts, own_picks))

    limit = lay_column(ranks + 1, pick_rank)
    row_label = lay_column(labels, pick_label)
    shift = lay_column(jnp.zeros_like(ranks), length - 1 - picks)
    col = jnp.stack([limit, row_label, shift] + [shift] * 5, axis=1)
    memory_rank = jnp.where(has_memory[0] > 0, -1, hidden_key).astype(jnp.int32)
    row = jnp.broadcast_to(jnp.concatenate([jnp.full((mem,), memory_rank), ranks])[None], (8, keys))
    key_label = jnp.concatenate([jnp.zeros((mem,), jnp.int32), labels])
    lane = jnp.arange(wide)[None]
    zero_lane = (lane == local) | (lane == local + 1)
    one_lane = (lane == local + 2) | (lane == local + 3)
    keycol = jnp.where(
        zero_lane, (1 - key_label)[:, None], jnp.where(one_lane, key_label[:, None], 0)
    ).astype(BF16)
    bias = jnp.pad(
        jnp.stack([word_bias.reshape(-1), position_bias.reshape(-1), segment_bias.reshape(-1)]).astype(F32),
        ((0, 5), (0, wide - local)),
    )
    flat_embed = jnp.pad(segment_embed.reshape(2, local), ((0, 0), (0, wide - local)))

    def embed_lanes(a, b):
        return jnp.where(zero_lane, a[:, None], jnp.where(one_lane, b[:, None], 0))

    embed = jnp.concatenate(
        [embed_lanes(flat_embed[0], flat_embed[1]), embed_lanes(flat_embed[1], flat_embed[0])], axis=1
    ).astype(BF16)

    def widen(w):
        return jnp.pad(w, ((0, 0), (0, wide - local)))

    table = jnp.asarray(position_rows(keys, length, width))
    rel = jnp.dot(table, widen(relative_weight), preferred_element_type=F32).astype(BF16)
    wkv = jnp.concatenate([widen(key_weight), widen(value_weight)], axis=1)

    wo_core = swap_core(output_weight)
    wo_x = swap_x(output_weight)
    wo_diag = swap_core(wo_x)
    cot_own = jnp.concatenate([content_cotangent[0], query_cotangent[0]], axis=0)
    cot_x = swap_x(cot_own)
    first_x = me < 2
    cot_0 = jnp.where(first_x, cot_own, cot_x)
    cot_1 = jnp.where(first_x, cot_x, cot_own)
    cot = jnp.concatenate([cot_0[:own], cot_1[:own], cot_0[own:], cot_1[own:]], axis=0)

    p, att, qf, kc, v = attend_forward(
        blocks, stream, joined, widen(query_weight), wkv, rel, col, row, bias, embed, keycol,
        heads, head_size, length,
    )
    att_core = swap_core(att)
    att_x = swap_x(att)
    att_diag = swap_core(att_x)

    vec = jnp.stack(
        [first_gain, first_shift, outer_bias, second_gain, second_shift] + [second_shift] * 3
    ).astype(F32)
    bi = jnp.broadcast_to(inner_bias.astype(F32)[None], (8, inner_bias.shape[0]))
    core_id = core.astype(jnp.int32).reshape(1)
    hid, act, gp, mixed, part_mine, part_other = feed_forward(
        core_id, (att, att_core, att_x, att_diag), (output_weight, wo_core, wo_x, wo_diag), stream, vec,
        inner_weight, bi, outer_weight,
    )

    def add(a, b):
        return call(add_kernel, "add", (1,), (a, b), [whole(a.shape)] * 2, [(a.shape, BF16)], [whole(a.shape)])[0]

    chip_part = add(part_mine, swap_core(part_other))
    out_half, og_half, sg_half, sums2 = second_norm(chip_part, swap_x(chip_part), mixed, cot, vec)
    ig, og, back_mine, back_other, inner_sums = feed_backward(
        core_id, og_half, swap_core(og_half), gp, inner_weight, outer_weight
    )
    chip_back = add(back_mine, swap_core(back_other))
    outer_weight_part = dot_tn(act, og).astype(BF16)
    inner_weight_part = dot_tn(hid, ig).astype(BF16)
    mg_half, ag_half, sums1 = first_norm(chip_back, swap_x(chip_back), sg_half, mixed, vec)
    ag_other = swap_core(ag_half)
    ag = jnp.where(
        core == 0,
        jnp.concatenate([ag_half, ag_other], axis=0),
        jnp.concatenate([ag_other, ag_half], axis=0),
    )
    da = dot_nt(ag, output_weight).astype(BF16)
    dat = dot_nt(output_weight, ag).astype(BF16)
    dq, kg, vg, rg, small = attend_backward(
        blocks, p, dat, da, qf, qf[:, :local].T, kc, v, rel, col, bias, bias[:, :local].T,
        flat_embed.astype(F32), head_size, length,
    )

    row_part = dot_nt(dq, query_weight)
    key_part = dot_tn(
        jnp.concatenate([kg[:, mem:], vg[:, mem:]], axis=0),
        jnp.concatenate([key_weight, value_weight], axis=1).T,
    )
    zeros = jnp.zeros((parts, own_picks, width), F32)
    row_part = row_part + lay(key_part.reshape(parts, own, width), zeros)
    low_rows = row_part.astype(BF16)
    row_mine = jnp.where(core == 0, low_rows[:half], low_rows[half:])
    row_other = jnp.where(core == 0, low_rows[half:], low_rows[:half])
    chip_row = add(row_mine, swap_core(row_other))

    def pick(a, which):
        first_half = jnp.concatenate([a[:own], a[2 * own : 2 * own + own_picks]], axis=0)
        second_half = jnp.concatenate([a[own : 2 * own], a[2 * own + own_picks :]], axis=0)
        return jnp.where(which == 0, first_half, second_half)

    side = me // 2
    row_sum = pick(chip_row, side).astype(F32) + swap_x(pick(chip_row, 1 - side)).astype(F32)
    row_grad = pick(mg_half, side) + row_sum
    outs = pick(out_half, side)

    query_weight_part = dot_tn(stream, dq).astype(BF16)
    key_weight_part = dot_nn(kg, joined).astype(BF16)
    value_weight_part = dot_nn(vg, joined).astype(BF16)
    relative_weight_part = dot_nn(rg, table).astype(BF16)
    output_weight_part = dot_tn(att, ag).astype(BF16)
    norm_sums = sums2[:3], sums1[:2]
    norm_sums = jnp.concatenate(norm_sums, axis=0)
    norm_sums = norm_sums + swap_core(norm_sums)
    ff = lax.psum((outer_weight_part, inner_weight_part, inner_sums[0]), "batch")
    rest = lax.psum(
        (
            query_weight_part,
            key_weight_part,
            value_weight_part,
            relative_weight_part,
            output_weight_part,
            small[:5, :local],
            norm_sums,
        ),
        "batch",
    )
    small_sum, norm_sum = rest[5], rest[6]

    def per_head(a):
        return a.reshape(heads, head_size)

    return (
        outs[None, :own],
        outs[None, own:],
        row_grad[None, :own],
        row_grad[None, own:],
        rest[0].astype(F32),
        rest[1].astype(F32).T,
        rest[2].astype(F32).T,
        rest[4].astype(F32),
        rest[3].astype(F32).T,
        per_head(small_sum[0]),
        per_head(small_sum[1]),
        per_head(small_sum[2]),
        small_sum[3:5].reshape(2, heads, head_size),
        norm_sum[3],
        norm_sum[4],
        ff[1].astype(F32),
        ff[2],
        ff[0].astype(F32),
        norm_sum[0],
        norm_sum[1],
        norm_sum[2],
    )


def solution(mesh):
    rows = P("batch", "head", None)
    ids = P("batch", None)
    columns = P(None, "head")
    by_head = P("head", None)
    table = P(None, "head", None)
    return jax.shard_map(
        on_device,
        mesh=mesh,
        in_specs=(
            rows, rows, rows, P("batch"), ids, ids, ids,
            columns, columns, columns, by_head, columns,
            by_head, by_head, by_head, table, P(), P(),
            columns, P("head"), by_head, P(), P(), P(), rows, rows,
        ),
        out_specs=(
            rows, rows, rows, rows,
            columns, columns, columns, by_head, columns,
            by_head, by_head, by_head, table, P(), P(),
            columns, P("head"), by_head, P(), P(), P(),
        ),
        check_vma=False,
    )
```

```python
import functools
import jax
import jax.numpy as jnp
import numpy as np
from jax import lax
from jax.experimental import pallas as pl
from jax.experimental.pallas import tpu as pltpu
from jax.sharding import PartitionSpec as P

masked_score = -1e30
norm_eps = 1e-05
gelu_root = 0.7978845608028654
gelu_cubic = 0.044715
hidden_key = 1e6
F32 = jnp.float32
BF16 = jnp.bfloat16
MIB = 1024 * 1024
SMEM_SPEC = pl.BlockSpec(memory_space=pltpu.SMEM)


def dot_nt(a, b):
    return lax.dot_general(a, b, (((1,), (1,)), ((), ())), preferred_element_type=F32)


def dot_nn(a, b):
    return lax.dot_general(a, b, (((1,), (0,)), ((), ())), preferred_element_type=F32)


def dot_tn(a, b):
    return lax.dot_general(a, b, (((0,), (0,)), ((), ())), preferred_element_type=F32)


def position_rows(key_count, length, width):
    steps = key_count - 1 - np.arange(key_count + length, dtype=np.float64)
    freqs = 10000.0 ** (-np.arange(0, width, 2, dtype=np.float64) / width)
    angles = steps[:, None] * freqs[None, :]
    return np.concatenate([np.sin(angles), np.cos(angles)], axis=1).astype(jnp.bfloat16)


def whole(shape):
    return pl.BlockSpec(shape, lambda *_: (0,) * len(shape))


def call(kernel, name, ins, outs, scratch=(), grid=(1,), in_specs=None, out_specs=None, smem=(), limit=24):
    specs = [whole(x.shape) for x in ins]
    for i in smem:
        specs[i] = SMEM_SPEC
    for i, spec in (in_specs or {}).items():
        specs[i] = spec
    to = [whole(s) for s, _ in outs]
    for i, spec in (out_specs or {}).items():
        to[i] = spec
    return pl.pallas_call(
        kernel,
        grid=grid,
        in_specs=specs,
        out_specs=to,
        out_shape=[jax.ShapeDtypeStruct(s, t) for s, t in outs],
        scratch_shapes=list(scratch),
        compiler_params=pltpu.CompilerParams(vmem_limit_bytes=limit * MIB),
        cost_estimate=pl.CostEstimate(flops=0, bytes_accessed=0, transcendentals=0),
        name=name,
    )(*ins)


def at16(i, n):
    return pl.ds(pl.multiple_of(i, 16), n)


def row_sum(x):
    return jnp.sum(x, axis=0, keepdims=True)


def pack_kernel(con_ref, mem_ref, pick_ref, out_ref, cot_ref, pcot_ref, rows_ref, late_ref):
    for to, parts in ((rows_ref, (con_ref, mem_ref, pick_ref)), (late_ref, (out_ref, cot_ref, pcot_ref))):
        start = 0
        for part in parts:
            to[start : start + part.shape[0], :] = part[...]
            start += part.shape[0]


def pack(*ins):
    width = ins[0].shape[1]
    outs = [((sum(x.shape[0] for x in part), width), BF16) for part in (ins[:3], ins[3:])]
    return call(pack_kernel, "pack", ins, outs, limit=60)


def relative_kernel(table_ref, w_ref, rel_ref):
    local = w_ref.shape[0]
    rel_ref[...] = jnp.zeros_like(rel_ref)
    rel_ref[:, :local] = dot_nt(table_ref[...], w_ref[...]).astype(BF16)


def relative_rows(table, w, wide):
    return call(relative_kernel, "relative", (table, w), [((table.shape[0], wide), BF16)], limit=60)[0]


def attend_forward_kernel(
    blocks, head_size, mem,
    ids_ref, present_ref, rank_ref, pick_ref, seg_ref, wb_ref, pb_ref, sb_ref, se_ref,
    g0_ref, g1_ref, g2_ref, g3_ref,
    wq_ref, wk_ref, wv_ref, rel_ref,
    p_ref, att_ref, qf_ref, kc_ref, v_ref, stream_ref, joined_ref, col_ref, bias_ref,
    acc_ref, row_ref, embed_ref,
):
    h = pl.program_id(0)
    keys, wide = kc_ref.shape
    local = wq_ref.shape[0]
    length = keys - mem
    own, own_mem = length // 4, mem // 4
    own_picks = g0_ref.shape[0] - own - own_mem
    half = stream_ref.shape[0] // 2

    @pl.when(h == 0)
    def _():
        core, side = ids_ref[1], ids_ref[2]
        cores = (core, 1 - core, core, 1 - core)
        sides = (side, side, 1 - side, 1 - side)
        gathered = (g0_ref, g1_ref, g2_ref, g3_ref)
        for i in range(4):
            owner = 2 * sides[i] + cores[i]
            rows = gathered[i][:own, :]
            stream_ref[at16(cores[i] * half + sides[i] * own, own), :] = rows
            joined_ref[at16(mem + owner * own, own), :] = rows
            joined_ref[at16(owner * own_mem, own_mem), :] = gathered[i][own : own + own_mem, :]
        for i in range(2):
            a = gathered[i][own + own_mem :, :].astype(F32)
            b = gathered[i + 2][own + own_mem :, :].astype(F32)
            first = jnp.where(side == 0, a, b)
            second = jnp.where(side == 0, b, a)
            both = jnp.concatenate([first, second], axis=0).astype(BF16)
            stream_ref[at16(cores[i] * half + 2 * own, 2 * own_picks), :] = both

        bias_ref[...] = jnp.zeros_like(bias_ref)
        sources = (wb_ref[...], pb_ref[...], sb_ref[...], se_ref[0], se_ref[1])
        for i, source in enumerate(sources):
            source = source.astype(F32)
            for k in range(source.shape[0]):
                bias_ref[i : i + 1, k * head_size : (k + 1) * head_size] = source[k : k + 1, :]
        turned = bias_ref[...].T
        lane = lax.broadcasted_iota(jnp.int32, embed_ref.shape, 1)
        left = lane < wide
        lane = jnp.where(left, lane, lane - wide)
        same, other = turned[:, 3:4], turned[:, 4:5]
        a = jnp.where(left, same, other)
        b = jnp.where(left, other, same)
        is_zero = (lane == local) | (lane == local + 1)
        is_one = (lane == local + 2) | (lane == local + 3)
        embed_ref[...] = jnp.where(is_zero, a, jnp.where(is_one, b, 0.0)).astype(BF16)

        ranks = rank_ref[...].astype(F32)
        labels = seg_ref[...].astype(F32)
        row = lax.broadcasted_iota(jnp.int32, (8, length), 0)
        content_col = jnp.where(row == 0, ranks + 1.0, jnp.where(row == 1, labels, 0.0)).T
        pick_row = jnp.broadcast_to(pick_ref[...].astype(F32), (8, pick_ref.shape[1]))
        picks = pick_row.T[:, 0:1]
        spot = lax.broadcasted_iota(jnp.int32, (picks.shape[0], length), 1).astype(F32)
        hit = spot == picks
        pick_rank = jnp.sum(jnp.where(hit, ranks, 0.0), axis=1, keepdims=True)
        pick_label = jnp.sum(jnp.where(hit, labels, 0.0), axis=1, keepdims=True)
        lane8 = lax.broadcasted_iota(jnp.int32, (picks.shape[0], 8), 1)
        shift = (length - 1.0) - picks
        pick_col = jnp.where(
            lane8 == 0, pick_rank, jnp.where(lane8 == 1, pick_label, jnp.where(lane8 == 2, shift, 0.0))
        )
        for c in range(2):
            for x in range(2):
                owner = 2 * x + c
                to = c * half + x * own
                col_ref[to : to + own, :] = content_col[owner * own : (owner + 1) * own, :]
                to = c * half + 2 * own + x * own_picks
                col_ref[to : to + own_picks, :] = pick_col[owner * own_picks : (owner + 1) * own_picks, :]
        memory_rank = jnp.where(present_ref[0] > 0, -1.0, hidden_key)
        row_ref[:, :mem] = jnp.full((8, mem), memory_rank, F32)
        row_ref[:, mem:] = jnp.broadcast_to(ranks, (8, length))

        qf_ref[...] = jnp.zeros_like(qf_ref)
        qf_ref[:, :local] = dot_nt(stream_ref[...], wq_ref[...])
        v_ref[...] = jnp.zeros_like(v_ref)
        v_ref[:, :local] = dot_nt(joined_ref[...], wv_ref[...]).astype(BF16)
        key_label = jnp.concatenate([jnp.zeros((mem, 1), F32), content_col[:, 1:2]], axis=0)
        lane = lax.broadcasted_iota(jnp.int32, (keys, wide), 1)
        is_zero = (lane == local) | (lane == local + 1)
        is_one = (lane == local + 2) | (lane == local + 3)
        kc_ref[...] = jnp.where(is_zero, 1.0 - key_label, jnp.where(is_one, key_label, 0.0)).astype(BF16)
        kc_ref[:, :local] = dot_nt(joined_ref[...], wk_ref[...]).astype(BF16)
        acc_ref[...] = jnp.zeros_like(acc_ref)

    limit_row = row_ref[0:1, :]
    for start, size, position in blocks:
        blk = slice(start, start + size)
        lane = lax.broadcasted_iota(jnp.int32, (size, wide), 1)
        mine = (lane >= h * head_size) & (lane < (h + 1) * head_size)
        qf = qf_ref[blk, :]
        zero = jnp.zeros_like(qf)
        word = jnp.where(mine, (qf + bias_ref[0:1, :]).astype(BF16).astype(F32) * 0.125, zero)
        place = jnp.where(mine, qf + bias_ref[1:2, :], zero).astype(BF16) * 0.125
        label = jnp.where(mine, (qf + bias_ref[2:3, :]) * 0.125, zero)
        label_hi = label.astype(BF16)
        label_lo = (label - label_hi.astype(F32)).astype(BF16)
        both = dot_nn(label_hi, embed_ref[...]) + dot_nn(label_lo, embed_ref[...])
        row_label = col_ref[blk, 1:2]
        pair = jnp.where(row_label == 0, both[:, :wide], both[:, wide:])
        pair_hi = pair.astype(BF16).astype(F32)
        hi_lane = (lane == local) | (lane == local + 2)
        lo_lane = (lane == local + 1) | (lane == local + 3)
        query = jnp.where(hi_lane, pair_hi, jnp.where(lo_lane, pair - pair_hi, word)).astype(BF16)
        scores = dot_nt(query, kc_ref[...])
        if position is not None:
            base = length - position - size
            width = keys + size
            rel = dot_nt(place, rel_ref[base : base + width, :])
            rel = pltpu.roll(rel, width - (size - 1), 1, stride=1, stride_axis=0)
        else:
            rel = dot_nt(place, rel_ref[...])
            total = rel.shape[1]
            shift = col_ref[blk, 2:3].astype(jnp.int32)
            bit = 0
            while (1 << bit) < length:
                rel = jnp.where(((shift >> bit) & 1) == 1, pltpu.roll(rel, total - (1 << bit), 1), rel)
                bit += 1
        scores = scores + rel[:, :keys]
        limit = col_ref[blk, 0:1]
        scores = jnp.where(limit_row < limit, scores, masked_score)
        top = jnp.max(scores, axis=-1, keepdims=True)
        powers = jnp.exp(scores - top)
        total = jnp.sum(powers, axis=-1, keepdims=True)
        soft = (powers * (1.0 / total)).astype(BF16)
        p_ref[0, blk, :] = soft
        att = dot_nn(soft, v_ref[...])
        acc_ref[blk, :] = jnp.where(mine, att, acc_ref[blk, :])

    @pl.when(h == pl.num_programs(0) - 1)
    def _():
        att_ref[...] = acc_ref[:, :local].astype(BF16)


def attend_forward(blocks, ids, small, gathered, own, weights, rel, heads, head_size, mem, rows):
    width = gathered[0].shape[1]
    keys = 4 * own + mem
    wide = rel.shape[1]
    ins = (ids, *small, *gathered, *weights, rel)
    outs = [
        ((heads, rows, keys), BF16),
        ((rows, heads * head_size), BF16),
        ((rows, wide), F32),
        ((keys, wide), BF16),
        ((keys, wide), BF16),
        ((rows, width), BF16),
        ((keys, width), BF16),
        ((rows, 8), F32),
        ((8, wide), F32),
    ]
    return call(
        functools.partial(attend_forward_kernel, blocks, head_size, mem),
        "attend_forward", ins, outs,
        [pltpu.VMEM((rows, wide), F32), pltpu.VMEM((8, keys), F32), pltpu.VMEM((wide, 2 * wide), BF16)],
        grid=(heads,), smem=(0, 1), limit=60,
        out_specs={0: pl.BlockSpec((1, rows, keys), lambda h: (h, 0, 0))},
    )


def attend_backward_kernel(
    h, heads, blocks, head_size, length, *refs,
):
    refs = list(refs)
    ids_ref, p_hbm = refs[:2]
    far, refs = refs[2:9], refs[9:]
    col_ref, bias_ref = refs[:2]
    refs = refs[2:]
    if h == 0:
        ag_ref, ago_ref, wo_ref, att_ref = refs[:4]
        refs = refs[4:]
    else:
        da_ref, dat_ref, dq_in, small_in = refs[:4]
        refs = refs[4:]
    if h == heads - 1:
        norm_ref, norm_core_ref, inner_ref = refs[:3]
        refs = refs[3:]
    dq_ref, small_ref, kg_ref, vg_ref, mine_ref, other_ref = refs[:6]
    refs = refs[6:]
    if h == 0:
        da_ref, dat_ref = refs[:2]
        refs = refs[2:]
    s_scr, rg_acc, qt_scr, all_ref, extra_scr, ag_scr = refs[:6]
    p_ref, near, sems = refs[6], refs[7:14], refs[14]
    v_ref, kc_ref, rel_ref, qf_ref, joined_ref, stream_ref, table_ref = near
    copies = [pltpu.make_async_copy(p_hbm.at[h], p_ref, sems.at[7])]
    copies += [pltpu.make_async_copy(a, b, sems.at[i]) for i, (a, b) in enumerate(zip(far, near))]
    for copy in copies:
        copy.start()
    keys, wide = kc_ref.shape
    total_rel = rel_ref.shape[0]
    local = da_ref.shape[1]
    at = slice(h * head_size, (h + 1) * head_size)
    side = ids_ref[3]
    part = head_size // 2

    if h == 0:
        half = ag_ref.shape[0]
        core = ids_ref[1]
        ag_scr[at16(core * half, half), :] = ag_ref[...]
        ag_scr[at16((1 - core) * half, half), :] = ago_ref[...]
        ag = ag_scr[...]
        da_ref[...] = dot_nt(ag, wo_ref[...]).astype(BF16)
        dat_ref[...] = dot_nt(wo_ref[...], ag).astype(BF16)
        extra_scr[...] = dot_tn(att_ref[...], ag).astype(BF16)
    if h == heads - 1:
        extra_scr[...] = jnp.zeros_like(extra_scr)

    lane = lax.broadcasted_iota(jnp.int32, (1, wide), 1)
    mine = (lane >= h * head_size) & (lane < (h + 1) * head_size)
    copies[0].wait()
    vg = dot_nn(dat_ref[at, :], p_ref[...]).astype(BF16)
    vg_ref[...] = vg
    for copy in copies[1:5]:
        copy.wait()
    rg_acc[...] = jnp.zeros_like(rg_acc)
    sums = [jnp.zeros((1, wide), F32) for _ in range(5)]
    for start, size, position in blocks:
        blk = slice(start, start + size)
        soft = p_ref[blk, :].astype(F32)
        grad = jnp.where(mine[:, :local], da_ref[blk, :], 0)
        chance = dot_nt(grad, v_ref[:, :local])
        inner = jnp.sum(chance * soft, axis=-1, keepdims=True)
        score = (soft * (chance - inner)).astype(BF16)
        s_scr[blk, :] = score
        word = dot_nn(score, kc_ref[...]) * 0.125
        qf = qf_ref[blk, :]
        place = (qf + bias_ref[1:2, :]).astype(BF16) * 0.125
        if position is not None:
            base = length - position - size
            width = keys + size
            turn = (
                lax.broadcasted_iota(jnp.int32, (size, size), 0)
                + lax.broadcasted_iota(jnp.int32, (size, size), 1)
                == size - 1
            ).astype(F32).astype(BF16)
            wider = jnp.concatenate([dot_nn(turn, score), jnp.zeros((size, width - keys), F32)], axis=1)
            wider = pltpu.roll(wider, 0, 1, stride=1, stride_axis=0).astype(BF16)
            placed = dot_nn(wider, rel_ref[base : base + width, :]) * 0.125
            high = placed.astype(BF16)
            low = (placed - high.astype(F32)).astype(BF16)
            placed = dot_nn(turn, high) + dot_nn(turn, low)
            place = dot_nn(turn, place)
        else:
            base = 0
            width = total_rel
            left = col_ref[blk, 2:3].astype(jnp.int32)
            wider = jnp.concatenate([score.astype(F32), jnp.zeros((size, width - keys), F32)], axis=1)
            bit = 0
            while (1 << bit) < length:
                wider = jnp.where(((left >> bit) & 1) == 1, pltpu.roll(wider, 1 << bit, 1), wider)
                bit += 1
            wider = wider.astype(BF16)
            placed = dot_nn(wider, rel_ref[base : base + width, :]) * 0.125
            place = place.astype(F32)
        rg_acc[:, base : base + width] += dot_nn(place.T[at, :].astype(BF16), wider)
        zero_key = word[:, local : local + 1]
        one_key = word[:, local + 2 : local + 3]
        row_label = col_ref[blk, 1:2]
        same = jnp.where(row_label == 0, zero_key, one_key)
        other = jnp.where(row_label == 0, one_key, zero_key)
        label = same * bias_ref[3:4, :] + other * bias_ref[4:5, :]
        query_label = qf + bias_ref[2:3, :]
        terms = (word, placed, label, query_label * same, query_label * other)
        for i, term in enumerate(terms):
            sums[i] = sums[i] + row_sum(term)
        dq = jnp.where(mine, word + placed + label, 0.0)
        if h == 0:
            dq_ref[blk, :] = dq[:, :local].astype(BF16)
        else:
            dq_ref[blk, :] = dq_in[blk, :] + dq[:, :local].astype(BF16)
        qt_scr[:, blk] = dq.T[at, :].astype(BF16)
    small_ref[...] = jnp.zeros_like(small_ref) if h == 0 else small_in[...]
    for i in range(5):
        old = jnp.zeros((1, wide), F32) if h == 0 else small_in[i : i + 1, :]
        small_ref[i : i + 1, :] = jnp.where(mine, sums[i], old)
    word_q = (qf_ref[...] + bias_ref[0:1, :]).astype(BF16).astype(F32) * 0.125
    kg = dot_nn(word_q.T[at, :].astype(BF16), s_scr[...]).astype(BF16)
    kg_ref[...] = kg
    for copy in copies[5:]:
        copy.wait()
    all_ref[2] = dot_nn(vg, joined_ref[...]).astype(BF16)
    all_ref[0] = dot_nn(qt_scr[...], stream_ref[...]).astype(BF16)
    all_ref[1] = dot_nn(kg, joined_ref[...]).astype(BF16)
    all_ref[3] = dot_nn(rg_acc[...].astype(BF16), table_ref[...]).astype(BF16)
    if h == heads - 1:
        norm = norm_ref[...] + norm_core_ref[...]
        width = norm.shape[1]
        tail = jnp.concatenate([small_ref[...], jnp.zeros((8, width - wide), F32)], axis=1)
        row = lax.broadcasted_iota(jnp.int32, (8, width), 0)
        norm = jnp.where(row == 5, inner_ref[...], norm)
        extra_scr[0:16, :] = jnp.concatenate([norm, tail], axis=0).astype(BF16)
    extra = extra_scr.shape[0] // 2
    for i in range(4):
        to = slice(i * part, (i + 1) * part)
        mine_ref[to, :] = all_ref[i, at16(side * part, part), :]
        other_ref[to, :] = all_ref[i, at16((1 - side) * part, part), :]
    if mine_ref.shape[0] > 4 * part:
        to = slice(4 * part, 4 * part + extra)
        mine_ref[to, :] = extra_scr[at16(side * extra, extra), :]
        other_ref[to, :] = extra_scr[at16((1 - side) * extra, extra), :]


def attend_backward(h, blocks, ids, p, far, shared, first, carried, norms, head_size, length):
    heads, rows, keys = p.shape
    wide, total_rel = far[2].shape[1], far[2].shape[0]
    width = far[4].shape[1]
    local = heads * head_size
    last = h == heads - 1
    extra = local if h == 0 else 32 if last else 0
    part = (4 * head_size + extra) // 2
    ins = (ids, p, *far, *shared, *(first if h == 0 else carried), *(norms if last else ()))
    outs = [
        ((rows, local), BF16),
        ((8, wide), F32),
        ((head_size, keys), BF16),
        ((head_size, keys), BF16),
        ((part, width), BF16),
        ((part, width), BF16),
    ]
    if h == 0:
        outs += [((rows, local), BF16), ((local, rows), BF16)]
    return call(
        functools.partial(attend_backward_kernel, h, heads, blocks, head_size, length),
        f"attend_backward_{h}", ins, outs,
        [
            pltpu.VMEM((rows, keys), BF16),
            pltpu.VMEM((head_size, total_rel), F32),
            pltpu.VMEM((head_size, rows), BF16),
            pltpu.VMEM((4, head_size, width), BF16),
            pltpu.VMEM((max(extra, 32), width), BF16),
            pltpu.VMEM((rows if h == 0 else 16, width), BF16),
            pltpu.VMEM((rows, keys), BF16),
            *[pltpu.VMEM(x.shape, x.dtype) for x in far],
            pltpu.SemaphoreType.DMA((8,)),
        ],
        smem=(0,), limit=60,
        in_specs={i: pl.BlockSpec(memory_space=pl.ANY) for i in range(1, 2 + len(far))},
    )


def norm_parts(x):
    center = x - jnp.mean(x, axis=-1, keepdims=True)
    scale = lax.rsqrt(jnp.mean(center * center, axis=-1, keepdims=True) + norm_eps)
    return center * scale, scale


def norm_back(grad, gain, unit, scale):
    along = grad * gain
    return scale * (
        along
        - jnp.mean(along, axis=-1, keepdims=True)
        - unit * jnp.mean(along * unit, axis=-1, keepdims=True)
    )


def feed_forward_kernel(
    ids_ref, a0_ref, a1_ref, a2_ref, a3_ref, w0_ref, w1_ref, w2_ref, w3_ref, stream_ref,
    gain_ref, shift_ref, wi_ref, bi_ref, wo_ref,
    hid_ref, act_ref, gp_ref, mixed_ref, mine_ref, other_ref,
):
    half = mine_ref.shape[0]
    local = a0_ref.shape[1]
    core = ids_ref[1]
    gain, shift = gain_ref[...].astype(F32), shift_ref[...].astype(F32)
    for step in range(2):
        rows = at16((core if step else 1 - core) * half, half)
        out = dot_nn(a0_ref[rows, :], w0_ref[...]) + dot_nn(a1_ref[rows, :], w1_ref[...])
        out = out + dot_nn(a2_ref[rows, :], w2_ref[:local, :]) + dot_nn(a3_ref[rows, :], w3_ref[:local, :])
        mixed = stream_ref[rows, :].astype(F32) + out
        if step:
            mixed_ref[...] = mixed
        unit, _ = norm_parts(mixed)
        hidden = (unit * gain + shift).astype(BF16)
        hid_ref[rows, :] = hidden
        inner = dot_nn(hidden, wi_ref[...]) + bi_ref[...].astype(F32)
        square = inner * inner
        turn = jnp.tanh(gelu_root * (inner + gelu_cubic * square * inner))
        lift = 0.5 * (1.0 + turn)
        slope = lift + 0.5 * inner * (1.0 - turn * turn) * (gelu_root * (1.0 + 3.0 * gelu_cubic * square))
        active = (inner * lift).astype(BF16)
        act_ref[rows, :] = active
        gp_ref[rows, :] = slope.astype(BF16)
        part = dot_nn(active, wo_ref[...]).astype(BF16)
        if step:
            mine_ref[...] = part
        else:
            other_ref[...] = part


def feed_forward(ids, atts, wos, stream, gain, shift, wi, bi, wo):
    rows, width = stream.shape
    units = wi.shape[1]
    half = rows // 2
    ins = (ids, *atts, *wos, stream, gain, shift, wi, bi, wo)
    outs = [
        ((rows, width), BF16),
        ((rows, units), BF16),
        ((rows, units), BF16),
        ((half, width), F32),
        ((half, width), BF16),
        ((half, width), BF16),
    ]
    return call(feed_forward_kernel, "feed_forward", ins, outs, smem=(0,), limit=32)


def second_norm_kernel(
    ids_ref, a_ref, b_ref, mixed_ref, cot_ref, pcot_ref, late_ref, g1_ref, s1_ref, ob_ref, g2_ref, s2_ref,
    content_ref, pick_ref, og_ref, sg_ref, sums_ref, cot_scr, out_scr,
):
    own, picks = cot_ref.shape[0], pcot_ref.shape[0]
    side = ids_ref[2]
    skip = late_ref.shape[0] - own - picks
    cot_scr[at16(side * own, own), :] = cot_ref[...].astype(F32)
    cot_scr[at16((1 - side) * own, own), :] = late_ref[skip : skip + own, :].astype(F32)
    a = pcot_ref[...].astype(F32)
    b = late_ref[skip + own :, :].astype(F32)
    cot_scr[2 * own : 2 * own + picks, :] = jnp.where(side == 0, a, b)
    cot_scr[2 * own + picks :, :] = jnp.where(side == 0, b, a)
    gain = g2_ref[...].astype(F32)
    unit, _ = norm_parts(mixed_ref[...])
    hidden = unit * g1_ref[...].astype(F32) + s1_ref[...].astype(F32)
    total = a_ref[...].astype(F32) + b_ref[...].astype(F32)
    unit, scale = norm_parts(hidden + total + ob_ref[...].astype(F32))
    out_scr[...] = unit * gain + s2_ref[...].astype(F32)
    content_ref[...] = out_scr[at16(side * own, own), :].astype(BF16)
    pick_ref[...] = jnp.where(
        side == 0, out_scr[2 * own : 2 * own + picks, :], out_scr[2 * own + picks :, :]
    ).astype(BF16)
    cot = cot_scr[...]
    grad = norm_back(cot, gain, unit, scale)
    low = grad.astype(BF16)
    og_ref[...] = low
    sg_ref[...] = grad
    sums_ref[...] = jnp.zeros_like(sums_ref)
    sums_ref[0:1, :] = row_sum(low.astype(F32))
    sums_ref[1:2, :] = row_sum(cot * unit)
    sums_ref[2:3, :] = row_sum(cot)


def second_norm(ids, a, b, mixed, cot, pcot, late, vectors):
    ins = (ids, a, b, mixed, cot, pcot, late, *vectors)
    shape = a.shape
    outs = [(cot.shape, BF16), (pcot.shape, BF16), (shape, BF16), (shape, F32), ((8, shape[1]), F32)]
    return call(
        second_norm_kernel, "second_norm", ins, outs, [pltpu.VMEM(shape, F32)] * 2, smem=(0,), limit=24
    )


def feed_backward_kernel(
    ids_ref, mine_ref, other_ref, gp_ref, wi_ref, wo_ref, ig_ref, og_ref, bm_ref, bo_ref, sums_ref
):
    half = mine_ref.shape[0]
    core = ids_ref[1]
    total = jnp.zeros((1, gp_ref.shape[1]), F32)
    for step in range(2):
        rows = at16((core if step else 1 - core) * half, half)
        og = mine_ref[...] if step else other_ref[...]
        og_ref[rows, :] = og
        grad = (dot_nt(og, wo_ref[...]) * gp_ref[rows, :].astype(F32)).astype(BF16)
        ig_ref[rows, :] = grad
        total = total + row_sum(grad.astype(F32))
        part = dot_nt(grad, wi_ref[...]).astype(BF16)
        if step:
            bm_ref[...] = part
        else:
            bo_ref[...] = part
    sums_ref[...] = total


def feed_backward(ids, mine, other, gp, wi, wo):
    rows, units = gp.shape
    half, width = mine.shape
    ins = (ids, mine, other, gp, wi, wo)
    outs = [
        ((rows, units), BF16),
        ((rows, width), BF16),
        ((half, width), BF16),
        ((half, width), BF16),
        ((1, units), F32),
    ]
    return call(feed_backward_kernel, "feed_backward", ins, outs, smem=(0,), limit=24)


def first_norm_kernel(a_ref, b_ref, sg_ref, mixed_ref, gain_ref, sums_in, mg_ref, ag_ref, sums_ref):
    grad = sg_ref[...] + a_ref[...].astype(F32) + b_ref[...].astype(F32)
    unit, scale = norm_parts(mixed_ref[...])
    out = norm_back(grad, gain_ref[...].astype(F32), unit, scale)
    mg_ref[...] = out
    ag_ref[...] = out.astype(BF16)
    sums_ref[...] = sums_in[...]
    sums_ref[3:4, :] = row_sum(grad * unit)
    sums_ref[4:5, :] = row_sum(grad)


def first_norm(a, b, sg, mixed, gain, sums):
    ins = (a, b, sg, mixed, gain, sums)
    shape = a.shape
    outs = [(shape, F32), (shape, BF16), (sums.shape, F32)]
    return call(first_norm_kernel, "first_norm", ins, outs, limit=16)


def add_kernel(a_ref, b_ref, o_ref):
    o_ref[...] = (a_ref[...].astype(F32) + b_ref[...].astype(F32)).astype(BF16)


def add(a, b):
    return call(add_kernel, "add", (a, b), [(a.shape, BF16)], limit=8)[0]


def row_grad_kernel(heads, mem, ids_ref, dq_ref, *refs):
    kgs, vgs = refs[:heads], refs[heads : 2 * heads]
    wq_ref, wk_ref, wv_ref, mine_ref, other_ref, key_scr = refs[2 * heads :]
    half = mine_ref.shape[0]
    core = ids_ref[1]
    own = key_scr.shape[0] // 4
    kg = jnp.concatenate([k[:, mem:].astype(F32) for k in kgs], axis=0).T.astype(BF16)
    vg = jnp.concatenate([v[:, mem:].astype(F32) for v in vgs], axis=0).T.astype(BF16)
    key_scr[...] = dot_nn(kg, wk_ref[...]) + dot_nn(vg, wv_ref[...])
    for step in range(2):
        c = core if step else 1 - core
        part = dot_nn(dq_ref[at16(c * half, half), :], wq_ref[...])
        to = mine_ref if step else other_ref
        to[0:own, :] = (part[:own] + key_scr[at16(c * own, own), :]).astype(BF16)
        to[own : 2 * own, :] = (part[own : 2 * own] + key_scr[at16((2 + c) * own, own), :]).astype(BF16)
        to[2 * own :, :] = part[2 * own :].astype(BF16)


def row_grads(ids, dq, kgs, vgs, weights, mem):
    rows = dq.shape[0]
    heads, keys, width = len(kgs), kgs[0].shape[1], weights[0].shape[1]
    ins = (ids, dq, *kgs, *vgs, *weights)
    outs = [((rows // 2, width), BF16)] * 2
    return call(
        functools.partial(row_grad_kernel, heads, mem), "row_grads", ins, outs,
        [pltpu.VMEM((keys - mem, width), F32)], smem=(0,), limit=20,
    )


def row_split_kernel(own, picks, ids_ref, a_ref, b_ref, mg_ref, keep_ref, keep_pick_ref, send_ref, scr):
    side = ids_ref[2]
    scr[...] = (a_ref[...].astype(F32) + b_ref[...].astype(F32)).astype(BF16).astype(F32)
    first, second = scr[2 * own : 2 * own + picks, :], scr[2 * own + picks :, :]
    send_ref[0:own, :] = scr[at16((1 - side) * own, own), :].astype(BF16)
    send_ref[own:, :] = jnp.where(side == 0, second, first).astype(BF16)
    keep_ref[...] = scr[at16(side * own, own), :] + mg_ref[at16(side * own, own), :]
    grad = jnp.where(side == 0, mg_ref[2 * own : 2 * own + picks, :], mg_ref[2 * own + picks :, :])
    keep_pick_ref[...] = jnp.where(side == 0, first, second) + grad


def row_split(own, picks, ids, a, b, mg):
    width = a.shape[1]
    outs = [((own, width), F32), ((picks, width), F32), ((own + picks, width), BF16)]
    return call(
        functools.partial(row_split_kernel, own, picks), "row_split", (ids, a, b, mg), outs,
        [pltpu.VMEM(a.shape, F32)], smem=(0,), limit=12,
    )


def row_finish_kernel(keep_ref, keep_pick_ref, got_ref, content_ref, pick_ref):
    own = keep_ref.shape[0]
    content_ref[...] = keep_ref[...] + got_ref[:own, :].astype(F32)
    pick_ref[...] = keep_pick_ref[...] + got_ref[own:, :].astype(F32)


def row_finish(keep, keep_pick, got):
    outs = [(keep.shape, F32), (keep_pick.shape, F32)]
    return call(row_finish_kernel, "row_finish", (keep, keep_pick, got), outs, limit=8)


def pair_grad_kernel(ids_ref, a_ref, b_ref, mine_ref, other_ref):
    half = mine_ref.shape[0]
    side = ids_ref[3]
    for step in range(2):
        cols = pl.ds(pl.multiple_of((side if step else 1 - side) * half, 128), half)
        out = dot_tn(a_ref[:, cols], b_ref[...]).astype(BF16)
        if step:
            mine_ref[...] = out
        else:
            other_ref[...] = out


def pair_grads(ids, a, b):
    outs = [((a.shape[1] // 2, b.shape[1]), BF16)] * 2
    return call(pair_grad_kernel, "pair_grads", (ids, a, b), outs, smem=(0,), limit=16)


def outer_grad_kernel(a_ref, b_ref, o_ref):
    o_ref[...] = dot_tn(a_ref[...], b_ref[...]).astype(BF16)


def outer_grads(a, b):
    return call(outer_grad_kernel, "outer_grads", (a, b), [((a.shape[1], b.shape[1]), BF16)], limit=16)[0]


def widen_kernel(a_ref, o_ref):
    o_ref[...] = a_ref[...].astype(F32)


def batch_swap(x, bit):
    n = lax.axis_size("batch")
    return lax.ppermute(x, "batch", [(i, i ^ (1 << bit)) for i in range(n)])


def after(x, *others):
    return lax.optimization_barrier((x, *others))[0]


class BatchSum:
    def __init__(self, mine, other):
        self.bits = lax.axis_size("batch").bit_length() - 1
        self.me = lax.axis_index("batch")
        self.step, self.x, self.coming = 0, mine, None
        self.next, self.bit = other, 0

    def half(self, x, bit, stays):
        n = x.shape[0] // 2
        side = (self.me >> bit) & 1
        return lax.dynamic_slice_in_dim(x, (side if stays else 1 - side) * n, n, 0)

    def prepare(self, *deps):
        last = self.bits - 1
        if self.coming is None:
            return self.next
        if self.step == 2 * last:
            return None
        if deps:
            self.coming = after(self.coming, *deps)
        self.step += 1
        self.bit = self.step
        if self.step < last:
            total = self.x + self.coming
            self.x = self.half(total, self.step, True)
            return self.half(total, self.step, False)
        if self.step == last or self.step == last + 1:
            self.x = self.x + self.coming
        else:
            self.spread(2 * last + 1 - self.step)
        if self.step > last:
            self.bit = 2 * last - self.step
        self.next = self.x
        return self.x

    def launch(self, x):
        if self.next is self.x:
            self.x = x
        self.next = None
        self.coming = batch_swap(x, self.bit)

    def spread(self, bit):
        side = (self.me >> bit) & 1
        x, y = self.x, self.coming
        self.x = jnp.where(side == 0, jnp.concatenate([x, y]), jnp.concatenate([y, x]))

    def finished(self):
        return self.step == 2 * self.bits - 2

    def total(self):
        self.spread(0)
        return self.x


def round_of(chains, deps, *others):
    ready = [(c, c.prepare(*deps)) for c in chains]
    ready = [(c, x) for c, x in ready if x is not None]
    tied = lax.optimization_barrier((*[x for _, x in ready], *others))
    for (c, _), x in zip(ready, tied):
        c.launch(x)
    return tied[len(ready) :]


def finish_kernel(heads, head_size, ids_ref, *refs):
    pairs, refs = refs[: 2 * heads], refs[2 * heads :]
    qo, ko, vo, oo, ro, wb, pb, sb, se, vec, scr, small = refs
    side = ids_ref[3]
    part = head_size // 2
    local = heads * head_size
    for h in range(heads):
        for i in range(4):
            for s in range(2):
                source = pairs[2 * h + s][i * part : (i + 1) * part, :]
                place = side if s == 0 else 1 - side
                scr[i, at16(h * head_size + place * part, part), :] = source.astype(F32)
    for i, to in enumerate((qo, ko, vo, ro)):
        to[...] = scr[i]
    half = local // 2
    for s in range(2):
        place = side if s == 0 else 1 - side
        oo[at16(place * half, half), :] = pairs[s][4 * part :, :].astype(F32)
        small[at16(place * 16, 16), :] = pairs[2 * heads - 2 + s][4 * part :, :].astype(F32)
    vec[...] = small[0:8, :]
    for h in range(heads):
        at = slice(h * head_size, (h + 1) * head_size)
        for i, to in enumerate((wb, pb, sb)):
            to[h : h + 1, :] = small[8 + i : 9 + i, at]
        for c in range(2):
            se[c, h : h + 1, :] = small[11 + c : 12 + c, at]


def finish(ids, pairs, heads, head_size):
    width = pairs[0].shape[1]
    local = heads * head_size
    outs = [((local, width), F32)] * 5
    outs += [((heads, head_size), F32)] * 3 + [((2, heads, head_size), F32), ((8, width), F32)]
    return call(
        functools.partial(finish_kernel, heads, head_size), "finish", (ids, *pairs), outs,
        [pltpu.VMEM((4, local, width), F32), pltpu.VMEM((32, width), F32)], smem=(0,), limit=24,
    )


def on_device(
    content, query_stream, memory, has_memory, order_rank, targets, segments,
    query_weight, key_weight, value_weight, output_weight, relative_weight,
    word_bias, position_bias, segment_bias, segment_embed, first_gain, first_shift,
    inner_weight, inner_bias, outer_weight, outer_bias, second_gain, second_shift,
    content_cotangent, query_cotangent,
):
    parts = lax.axis_size("head")
    me = lax.axis_index("head")
    core_perm = [(i, i ^ 1) for i in range(parts)]
    x_perm = [(i, i ^ 2) for i in range(parts)]

    def swap_core(x):
        return lax.ppermute(x, "head", core_perm)

    def swap_x(x):
        return lax.ppermute(x, "head", x_perm)

    own, width = content.shape[1:]
    own_picks, own_memory = query_stream.shape[1], memory.shape[1]
    length, mem = own * parts, own_memory * parts
    keys = mem + length
    heads, head_size = word_bias.shape
    local = heads * head_size
    wide = local + head_size
    half = 2 * (own + own_picks)
    rows = 2 * half
    ids = jnp.stack([me, me % 2, me // 2, lax.axis_index("batch") % 2]).astype(jnp.int32)
    blocks = (
        (0, own, 0),
        (own, own, 2 * own),
        (2 * own, 2 * own_picks, None),
        (half, own, own),
        (half + own, own, 3 * own),
        (half + 2 * own, 2 * own_picks, None),
    )

    turned = (query_weight.T, key_weight.T, value_weight.T)
    own_rows, late = pack(
        content[0], memory[0], query_stream[0], output_weight, content_cotangent[0], query_cotangent[0]
    )
    x_rows = swap_x(own_rows)
    core_rows = swap_core(own_rows)
    diag_rows = swap_core(x_rows)
    table = jnp.asarray(position_rows(keys, length, width))
    rel = relative_rows(table, relative_weight.T, wide)
    late_x = swap_x(after(late, x_rows))
    wo_core = swap_core(output_weight)

    small_ins = (
        has_memory, order_rank, targets, segments, word_bias, position_bias, segment_bias, segment_embed
    )
    p, att, qf, kc, v, stream, joined, col, bias = attend_forward(
        blocks, ids, small_ins, (own_rows, core_rows, x_rows, diag_rows), own,
        turned, rel, heads, head_size, mem, rows,
    )
    att_x = swap_x(att)
    att_core = swap_core(att)
    late_diag = swap_core(late_x)
    att_diag = swap_core(att_x)

    def vector(x):
        return x.reshape(1, -1)

    hid, act, gp, mixed, part_mine, part_other = feed_forward(
        ids, (att, att_core, att_x, att_diag), (output_weight, wo_core, late_x, late_diag), stream,
        vector(first_gain), vector(first_shift), inner_weight, vector(inner_bias), outer_weight,
    )
    chip_part = add(part_mine, swap_core(part_other))
    vectors = [vector(x) for x in (first_gain, first_shift, outer_bias, second_gain, second_shift)]
    content_out, query_out, og_half, sg_half, sums = second_norm(
        ids, chip_part, swap_x(chip_part), mixed, content_cotangent[0], query_cotangent[0], late_x, vectors
    )
    ig, og, back_mine, back_other, inner_sums = feed_backward(
        ids, og_half, swap_core(og_half), gp, inner_weight, outer_weight
    )
    chip_back = add(back_mine, swap_core(back_other))
    back_x = swap_x(chip_back)
    outer_part = outer_grads(act, og)
    outer_sum = lax.psum_scatter(outer_part, "batch", scatter_dimension=0, tiled=True)
    inner_chain = BatchSum(*pair_grads(ids, hid, after(ig, chip_back)))
    round_of([inner_chain], ())
    mg_half, ag_half, sums = first_norm(chip_back, back_x, sg_half, mixed, vector(first_gain), after(sums, outer_part))
    ag_other = swap_core(ag_half)
    sums_core = swap_core(sums)

    far = (v, kc, rel, qf, joined, stream, table)
    chains, kgs, vgs = [inner_chain], [], []
    carried, tied = None, ids
    for h in range(heads):
        outs = attend_backward(
            h, blocks, tied, p, far, (col, bias), (ag_half, ag_other, output_weight, att), carried,
            (sums, sums_core, inner_sums), head_size, length,
        )
        dq, small, kg, vg, mine, other = outs[:6]
        if h == 0:
            grads_in = outs[6:]
        carried = (*grads_in, dq, small)
        kgs.append(kg)
        vgs.append(vg)
        chains.append(BatchSum(mine, other))
        if h < heads - 1:
            (tied,) = round_of(chains, (dq,), ids)
    row_mine, row_other = row_grads(ids, dq, kgs, vgs, turned, mem)
    row_other, outer_sum = round_of(chains, (dq,), row_other, outer_sum)
    outer_sum = lax.all_gather(outer_sum, "batch", axis=0, tiled=True)
    keep, keep_pick, send = row_split(own, own_picks, ids, row_mine, swap_core(row_other), mg_half)
    (send,) = round_of(chains, (), send)
    content_grad, query_grad = row_finish(keep, keep_pick, swap_x(send))
    round_of(chains, ())
    round_of(chains, ())
    while not chains[-1].finished():
        round_of(chains, ())
    outer_sum = after(outer_sum, chains[-1].coming)
    inner_sum = inner_chain.total()
    pairs = [half for c in chains[1:] for half in (c.x, c.coming)]
    q, k, v_, o, r, wb, pb, sb, se, vec = finish(ids, pairs, heads, head_size)
    return (
        content_out[None],
        query_out[None],
        content_grad[None],
        query_grad[None],
        q.T, k.T, v_.T, o, r.T, wb, pb, sb, se,
        vec[3],
        vec[4],
        inner_sum.astype(F32),
        vec[5],
        outer_sum.astype(F32),
        vec[0],
        vec[1],
        vec[2],
    )


def solution(mesh):
    rows = P("batch", "head", None)
    ids = P("batch", None)
    columns = P(None, "head")
    by_head = P("head", None)
    table = P(None, "head", None)
    return jax.shard_map(
        on_device,
        mesh=mesh,
        in_specs=(
            rows, rows, rows, P("batch"), ids, ids, ids,
            columns, columns, columns, by_head, columns,
            by_head, by_head, by_head, table, P(), P(),
            columns, P("head"), by_head, P(), P(), P(), rows, rows,
        ),
        out_specs=(
            rows, rows, rows, rows,
            columns, columns, columns, by_head, columns,
            by_head, by_head, by_head, table, P(), P(),
            columns, P("head"), by_head, P(), P(), P(),
        ),
        check_vma=False,
    )
```

```python
import functools
import jax
import jax.numpy as jnp
import numpy as np
from jax import lax
from jax.experimental import pallas as pl
from jax.experimental.pallas import tpu as pltpu
from jax.sharding import PartitionSpec as P

masked_score = -1e30
norm_eps = 1e-05
gelu_root = 0.7978845608028654
gelu_cubic = 0.044715
hidden_key = 1e6
F32 = jnp.float32
BF16 = jnp.bfloat16
MIB = 1024 * 1024
SMEM_SPEC = pl.BlockSpec(memory_space=pltpu.SMEM)


def dot_nt(a, b):
    return lax.dot_general(a, b, (((1,), (1,)), ((), ())), preferred_element_type=F32)


def dot_nn(a, b):
    return lax.dot_general(a, b, (((1,), (0,)), ((), ())), preferred_element_type=F32)


def dot_tn(a, b):
    return lax.dot_general(a, b, (((0,), (0,)), ((), ())), preferred_element_type=F32)


def position_rows(key_count, length, width):
    steps = key_count - 1 - np.arange(key_count + length, dtype=np.float64)
    freqs = 10000.0 ** (-np.arange(0, width, 2, dtype=np.float64) / width)
    angles = steps[:, None] * freqs[None, :]
    return np.concatenate([np.sin(angles), np.cos(angles)], axis=1).astype(jnp.bfloat16)


def whole(shape):
    return pl.BlockSpec(shape, lambda *_: (0,) * len(shape))


def call(kernel, name, ins, outs, scratch=(), grid=(), in_specs=None, out_specs=None, smem=(), limit=24):
    kept = pl.BlockSpec(memory_space=pltpu.VMEM)
    specs = [kept if grid == () else whole(x.shape) for x in ins]
    for i in smem:
        specs[i] = SMEM_SPEC
    for i, spec in (in_specs or {}).items():
        specs[i] = spec
    to = [kept if grid == () else whole(s) for s, _ in outs]
    for i, spec in (out_specs or {}).items():
        to[i] = spec
    return pl.pallas_call(
        kernel,
        grid=grid,
        in_specs=specs,
        out_specs=to,
        out_shape=[jax.ShapeDtypeStruct(s, t) for s, t in outs],
        scratch_shapes=list(scratch),
        compiler_params=pltpu.CompilerParams(vmem_limit_bytes=limit * MIB),
        cost_estimate=pl.CostEstimate(flops=0, bytes_accessed=0, transcendentals=0),
        name=name,
    )(*ins)


def at16(i, n):
    return pl.ds(pl.multiple_of(i, 16), n)


def row_sum(x):
    return jnp.sum(x, axis=0, keepdims=True)


def pack_kernel(*refs):
    start = 0
    for part in refs[:-1]:
        refs[-1][start : start + part.shape[0], :] = part[...]
        start += part.shape[0]


def pack(*ins):
    shape = (sum(x.shape[0] for x in ins), ins[0].shape[1])
    return call(pack_kernel, "pack", ins, [(shape, BF16)], limit=60)[0]


def prepare_kernel(
    own, own_picks, mem,
    present_ref, rank_ref, pick_ref, seg_ref, wb_ref, pb_ref, sb_ref, se_ref, table_ref, w_ref,
    rel_ref, col_ref, key_ref, bias_ref, embed_ref, row_ref,
):
    local, wide = w_ref.shape[0], rel_ref.shape[1]
    head_size = wb_ref.shape[1]
    length = rank_ref.shape[1]
    half = 2 * (own + own_picks)
    rel_ref[...] = jnp.zeros_like(rel_ref)
    rel_ref[:, :local] = dot_nt(table_ref[...], w_ref[...]).astype(BF16)

    bias_ref[...] = jnp.zeros_like(bias_ref)
    sources = (wb_ref[...], pb_ref[...], sb_ref[...], se_ref[0], se_ref[1])
    for i, source in enumerate(sources):
        source = source.astype(F32)
        for k in range(source.shape[0]):
            bias_ref[i : i + 1, k * head_size : (k + 1) * head_size] = source[k : k + 1, :]
    turned = bias_ref[...].T
    lane = lax.broadcasted_iota(jnp.int32, embed_ref.shape, 1)
    left = lane < wide
    lane = jnp.where(left, lane, lane - wide)
    same, other = turned[:, 3:4], turned[:, 4:5]
    a = jnp.where(left, same, other)
    b = jnp.where(left, other, same)
    is_zero = (lane == local) | (lane == local + 1)
    is_one = (lane == local + 2) | (lane == local + 3)
    embed_ref[...] = jnp.where(is_zero, a, jnp.where(is_one, b, 0.0)).astype(BF16)

    ranks = rank_ref[...].astype(F32)
    labels = seg_ref[...].astype(F32)
    row = lax.broadcasted_iota(jnp.int32, (8, length), 0)
    content_col = jnp.where(row == 0, ranks + 1.0, jnp.where(row == 1, labels, 0.0)).T
    key_ref[...] = content_col
    pick_row = jnp.broadcast_to(pick_ref[...].astype(F32), (8, pick_ref.shape[1]))
    picks = pick_row.T[:, 0:1]
    spot = lax.broadcasted_iota(jnp.int32, (picks.shape[0], length), 1).astype(F32)
    hit = spot == picks
    pick_rank = jnp.sum(jnp.where(hit, ranks, 0.0), axis=1, keepdims=True)
    pick_label = jnp.sum(jnp.where(hit, labels, 0.0), axis=1, keepdims=True)
    lane8 = lax.broadcasted_iota(jnp.int32, (picks.shape[0], 8), 1)
    shift = (length - 1.0) - picks
    pick_col = jnp.where(
        lane8 == 0, pick_rank, jnp.where(lane8 == 1, pick_label, jnp.where(lane8 == 2, shift, 0.0))
    )
    for c in range(2):
        for x in range(2):
            owner = 2 * x + c
            to = c * half + x * own
            col_ref[to : to + own, :] = content_col[owner * own : (owner + 1) * own, :]
            to = c * half + 2 * own + x * own_picks
            col_ref[to : to + own_picks, :] = pick_col[owner * own_picks : (owner + 1) * own_picks, :]
    memory_rank = jnp.where(present_ref[0] > 0, -1.0, hidden_key)
    row_ref[:, :mem] = jnp.full((8, mem), memory_rank, F32)
    row_ref[:, mem:] = jnp.broadcast_to(ranks, (8, length))


def prepare(small, table, w, own, own_picks, mem, wide):
    length = 4 * own
    outs = [
        ((table.shape[0], wide), BF16),
        ((4 * (own + own_picks), 8), F32),
        ((length, 8), F32),
        ((8, wide), F32),
        ((wide, 2 * wide), BF16),
        ((8, mem + length), F32),
    ]
    return call(
        functools.partial(prepare_kernel, own, own_picks, mem), "prepare", (*small, table, w), outs,
        smem=(0,), limit=60,
    )


def attend_forward_kernel(
    blocks, head_size, mem,
    ids_ref, g0_ref, g1_ref, g2_ref, g3_ref,
    wq_ref, wk_ref, wv_ref, rel_ref, col_in, key_ref, bias_ref, embed_ref, row_ref,
    p_ref, att_ref, qf_ref, kc_ref, v_ref, stream_ref, joined_ref, col_ref,
    acc_ref, score_scr, rel_scr, place_scr,
):
    h = pl.program_id(0)
    keys, wide = kc_ref.shape
    local = wq_ref.shape[0]
    length = keys - mem
    own, own_mem = length // 4, mem // 4
    own_picks = g0_ref.shape[0] - own - own_mem
    half = stream_ref.shape[0] // 2

    @pl.when(h == 0)
    def _():
        core, side = ids_ref[1], ids_ref[2]
        cores = (core, 1 - core, core, 1 - core)
        sides = (side, side, 1 - side, 1 - side)
        gathered = (g0_ref, g1_ref, g2_ref, g3_ref)
        for i in range(4):
            owner = 2 * sides[i] + cores[i]
            rows = gathered[i][:own, :]
            stream_ref[at16(cores[i] * half + sides[i] * own, own), :] = rows
            joined_ref[at16(mem + owner * own, own), :] = rows
            joined_ref[at16(owner * own_mem, own_mem), :] = gathered[i][own : own + own_mem, :]
        for i in range(2):
            a = gathered[i][own + own_mem :, :].astype(F32)
            b = gathered[i + 2][own + own_mem :, :].astype(F32)
            first = jnp.where(side == 0, a, b)
            second = jnp.where(side == 0, b, a)
            both = jnp.concatenate([first, second], axis=0).astype(BF16)
            stream_ref[at16(cores[i] * half + 2 * own, 2 * own_picks), :] = both

        col_ref[...] = col_in[...]
        qf_ref[...] = jnp.zeros_like(qf_ref)
        qf_ref[:, :local] = dot_nt(stream_ref[...], wq_ref[...])
        v_ref[...] = jnp.zeros_like(v_ref)
        v_ref[:, :local] = dot_nt(joined_ref[...], wv_ref[...]).astype(BF16)
        key_label = jnp.concatenate([jnp.zeros((mem, 1), F32), key_ref[:, 1:2]], axis=0)
        lane = lax.broadcasted_iota(jnp.int32, (keys, wide), 1)
        is_zero = (lane == local) | (lane == local + 1)
        is_one = (lane == local + 2) | (lane == local + 3)
        kc_ref[...] = jnp.where(is_zero, 1.0 - key_label, jnp.where(is_one, key_label, 0.0)).astype(BF16)
        kc_ref[:, :local] = dot_nt(joined_ref[...], wk_ref[...]).astype(BF16)
        acc_ref[...] = jnp.zeros_like(acc_ref)

    lane = lax.broadcasted_iota(jnp.int32, (1, wide), 1)
    mine = (lane >= h * head_size) & (lane < (h + 1) * head_size)
    hi_lane = (lane == local) | (lane == local + 2)
    lo_lane = (lane == local + 1) | (lane == local + 3)
    qf = qf_ref[...]
    word = jnp.where(mine, (qf + bias_ref[0:1, :]).astype(BF16).astype(F32) * 0.125, 0.0)
    place = jnp.where(mine, qf + bias_ref[1:2, :], 0.0).astype(BF16) * 0.125
    label = jnp.where(mine, (qf + bias_ref[2:3, :]) * 0.125, 0.0)
    label_hi = label.astype(BF16)
    label_lo = (label - label_hi.astype(F32)).astype(BF16)
    both = dot_nn(label_hi, embed_ref[...]) + dot_nn(label_lo, embed_ref[...])
    pair = jnp.where(col_ref[:, 1:2] == 0, both[:, :wide], both[:, wide:])
    pair_hi = pair.astype(BF16).astype(F32)
    query = jnp.where(hi_lane, pair_hi, jnp.where(lo_lane, pair - pair_hi, word)).astype(BF16)
    score_scr[...] = dot_nt(query, kc_ref[...])
    place_scr[...] = place

    limit_row = row_ref[0:1, :]
    for start, size, position in blocks:
        place = place_scr[start : start + size, :]
        if position is not None:
            base = length - position - size
            width = keys + size
            rel_scr[:size, :width] = dot_nt(place, rel_ref[base : base + width, :])
        else:
            rel_scr[:size, :] = dot_nt(place, rel_ref[...])
        chunk = 32 if size % 32 == 0 else 16
        for low in range(0, size, chunk):
            blk = slice(start + low, start + low + chunk)
            if position is not None:
                rel = rel_scr[low : low + chunk, :width]
                rel = pltpu.roll(rel, width - (size - 1) + low, 1, stride=1, stride_axis=0)
            else:
                rel = rel_scr[low : low + chunk, :]
                shift = col_ref[blk, 2:3].astype(jnp.int32)
                bit = (length - 1).bit_length()
                while bit > 0:
                    bit -= 1
                    far = 1 << bit
                    left = pltpu.roll(rel, rel.shape[1] - far, 1)
                    rel = jnp.where(((shift >> bit) & 1) == 1, left, rel)
                    rel = rel[:, : -(-(keys + far - 1) // 128) * 128]
            scores = score_scr[blk, :] + rel[:, :keys]
            scores = jnp.where(limit_row < col_ref[blk, 0:1], scores, masked_score)
            top = jnp.max(scores, axis=-1, keepdims=True)
            powers = jnp.exp(scores - top)
            total = jnp.sum(powers, axis=-1, keepdims=True)
            p_ref[0, blk, :] = powers.astype(BF16)
            lane8 = lax.broadcasted_iota(jnp.int32, (chunk, 8), 1)
            col_ref[blk, :] = jnp.where(lane8 == 4 + h, 1.0 / total, col_ref[blk, :])
    lane8 = lax.broadcasted_iota(jnp.int32, col_ref.shape, 1)
    inverse = jnp.sum(jnp.where(lane8 == 4 + h, col_ref[...], 0.0), axis=1, keepdims=True)
    att = dot_nn(p_ref[0], v_ref[...]) * inverse
    acc_ref[...] = jnp.where(mine, att, acc_ref[...])

    @pl.when(h == pl.num_programs(0) - 1)
    def _():
        att_ref[:, :local] = acc_ref[:half, :local].astype(BF16)
        att_ref[:, local:] = acc_ref[half:, :local].astype(BF16)


def attend_forward(blocks, ids, gathered, own, weights, rel, tables, heads, head_size, mem, rows):
    width = gathered[0].shape[1]
    keys = 4 * own + mem
    wide = rel.shape[1]
    ins = (ids, *gathered, *weights, rel, *tables)
    outs = [
        ((heads, rows, keys), BF16),
        ((rows // 2, 2 * heads * head_size), BF16),
        ((rows, wide), F32),
        ((keys, wide), BF16),
        ((keys, wide), BF16),
        ((rows, width), BF16),
        ((keys, width), BF16),
        ((rows, 8), F32),
    ]
    return call(
        functools.partial(attend_forward_kernel, blocks, head_size, mem),
        "attend_forward", ins, outs,
        [
            pltpu.VMEM((rows, wide), F32),
            pltpu.VMEM((rows, keys), F32),
            pltpu.VMEM((own, rel.shape[0]), F32),
            pltpu.VMEM((rows, wide), BF16),
        ],
        grid=(heads,), smem=(0,), limit=60,
        out_specs={0: pl.BlockSpec((1, rows, keys), lambda h: (h, 0, 0))},
    )


def second_half(packed):
    local = packed.shape[1] // 2
    return pltpu.roll(packed.astype(F32), local, 1)[:, :local].astype(BF16)


def attend_backward_kernel(
    h, heads, blocks, head_size, length, *refs,
):
    refs = list(refs)
    ids_ref, p_hbm = refs[:2]
    far, refs = refs[2:9], refs[9:]
    col_ref, bias_ref = refs[:2]
    refs = refs[2:]
    if h == 0:
        ag_ref, ago_ref, wo_ref, att_ref = refs[:4]
        refs = refs[4:]
    else:
        da_ref, dat_ref, dq_in, small_in = refs[:4]
        refs = refs[4:]
    if h == heads - 1:
        norm_ref, norm_core_ref, inner_ref = refs[:3]
        kgs, vgs = refs[3 : 2 + heads], refs[2 + heads : 1 + 2 * heads]
        weights_hbm = refs[1 + 2 * heads : 4 + 2 * heads]
        refs = refs[4 + 2 * heads :]
    dq_ref, small_ref, kg_ref, vg_ref, mine_ref, other_ref = refs[:6]
    refs = refs[6:]
    if h == 0:
        da_ref, dat_ref = refs[:2]
        refs = refs[2:]
    if h == heads - 1:
        row_mine, row_other = refs[:2]
        refs = refs[2:]
    s_scr, rg_acc, qt_scr, all_ref, extra_scr, ag_scr = refs[:6]
    p_ref, near, sems = refs[6], refs[7:14], refs[14]
    chance_scr, word_scr, place_scr, wide_scr = refs[15:19]
    v_ref, kc_ref, rel_ref, qf_ref, joined_ref, stream_ref, table_ref = near
    copies = [pltpu.make_async_copy(p_hbm.at[h], p_ref, sems.at[7])]
    copies += [pltpu.make_async_copy(a, b, sems.at[i]) for i, (a, b) in enumerate(zip(far, near))]
    if h == heads - 1:
        weights, key_scr = refs[19:22], refs[22]
        copies += [
            pltpu.make_async_copy(a, b, sems.at[8 + i]) for i, (a, b) in enumerate(zip(weights_hbm, weights))
        ]
    for copy in copies:
        copy.start()
    keys, wide = kc_ref.shape
    total_rel = rel_ref.shape[0]
    local = da_ref.shape[1]
    at = slice(h * head_size, (h + 1) * head_size)
    side = ids_ref[3]
    part = head_size // 2

    if h == 0:
        half = ag_ref.shape[0]
        core = ids_ref[1]
        ag_scr[at16(core * half, half), :] = ag_ref[...]
        ag_scr[at16((1 - core) * half, half), :] = ago_ref[...]
        ag = ag_scr[...]
        grads = dot_nt(ag, wo_ref[...]).astype(BF16).astype(F32)
        turned = dot_nt(wo_ref[...], ag).astype(BF16).astype(F32)
        inverse = col_ref[...].T
        lane = lax.broadcasted_iota(jnp.int32, (1, local), 1)
        factor = jnp.zeros((grads.shape[0], 1), F32)
        for k in range(heads):
            of = slice(k * head_size, (k + 1) * head_size)
            here = (lane >= k * head_size) & (lane < (k + 1) * head_size)
            factor = jnp.where(here, col_ref[:, 4 + k : 5 + k], factor)
            dat_ref[of, :] = (turned[of, :] * inverse[4 + k : 5 + k, :]).astype(BF16)
        da_ref[...] = (grads * factor).astype(BF16)
        packed = att_ref[...]
        extra = dot_tn(packed[:, :local], ag[:half, :]) + dot_tn(second_half(packed), ag[half:, :])
        extra_scr[...] = extra.astype(BF16)
    if h == heads - 1:
        extra_scr[...] = jnp.zeros_like(extra_scr)

    lane = lax.broadcasted_iota(jnp.int32, (1, wide), 1)
    mine = (lane >= h * head_size) & (lane < (h + 1) * head_size)
    copies[0].wait()
    vg = dot_nn(dat_ref[at, :], p_ref[...]).astype(BF16)
    vg_ref[...] = vg
    for copy in copies[1:5]:
        copy.wait()
    rg_acc[...] = jnp.zeros_like(rg_acc)
    sums = [jnp.zeros((1, wide), F32) for _ in range(5)]
    chance_scr[...] = dot_nt(jnp.where(mine[:, :local], da_ref[...], 0), v_ref[:, :local])
    step = 32
    for start in range(0, p_ref.shape[0], step):
        blk = slice(start, start + step)
        soft = p_ref[blk, :].astype(F32)
        chance = chance_scr[blk, :]
        inner = jnp.sum(chance * soft, axis=-1, keepdims=True) * col_ref[blk, 4 + h : 5 + h]
        s_scr[blk, :] = (soft * (chance - inner)).astype(BF16)
    word_scr[...] = dot_nn(s_scr[...], kc_ref[...]) * 0.125
    for start, size, position in blocks:
        blk = slice(start, start + size)
        score = s_scr[blk, :]
        place = (qf_ref[blk, :] + bias_ref[1:2, :]).astype(BF16) * 0.125
        if position is not None:
            base = length - position - size
            width = keys + size
            turn = (
                lax.broadcasted_iota(jnp.int32, (size, size), 0)
                + lax.broadcasted_iota(jnp.int32, (size, size), 1)
                == size - 1
            ).astype(F32).astype(BF16)
            wider = jnp.concatenate([dot_nn(turn, score), jnp.zeros((size, width - keys), F32)], axis=1)
            wider = pltpu.roll(wider, 0, 1, stride=1, stride_axis=0).astype(BF16)
            placed = dot_nn(wider, rel_ref[base : base + width, :]) * 0.125
            high = placed.astype(BF16)
            low = (placed - high.astype(F32)).astype(BF16)
            place_scr[blk, :] = dot_nn(turn, high) + dot_nn(turn, low)
            place = dot_nn(turn, place)
        else:
            base = 0
            width = total_rel
            for low in range(0, size, 16):
                to = slice(start + low, start + low + 16)
                left = col_ref[to, 2:3].astype(jnp.int32)
                moved = s_scr[to, :].astype(F32)
                bit = 0
                while (1 << bit) < length:
                    need = -(-(keys + (2 << bit) - 1) // 128) * 128
                    if need > moved.shape[1]:
                        moved = jnp.concatenate(
                            [moved, jnp.zeros((16, need - moved.shape[1]), F32)], axis=1
                        )
                    moved = jnp.where(((left >> bit) & 1) == 1, pltpu.roll(moved, 1 << bit, 1), moved)
                    bit += 1
                wide_scr[low : low + 16, :] = moved.astype(BF16)
            wider = wide_scr[...]
            place_scr[blk, :] = dot_nn(wider, rel_ref[...]) * 0.125
            place = place.astype(F32)
        rg_acc[:, base : base + width] += dot_nn(place.T[at, :].astype(BF16), wider)
    step = 152
    for start in range(0, p_ref.shape[0], step):
        blk = slice(start, start + step)
        word, placed = word_scr[blk, :], place_scr[blk, :]
        row_label = col_ref[blk, 1:2]
        zero_key = word[:, local : local + 1]
        one_key = word[:, local + 2 : local + 3]
        same = jnp.where(row_label == 0, zero_key, one_key)
        other = jnp.where(row_label == 0, one_key, zero_key)
        label = same * bias_ref[3:4, :] + other * bias_ref[4:5, :]
        query_label = qf_ref[blk, :] + bias_ref[2:3, :]
        terms = (word, placed, label, query_label * same, query_label * other)
        for i, term in enumerate(terms):
            sums[i] = sums[i] + row_sum(term)
        word_scr[blk, :] = jnp.where(mine, word + placed + label, 0.0)
    dq = word_scr[...]
    if h == 0:
        dq_ref[...] = dq[:, :local].astype(BF16)
    else:
        dq_ref[...] = dq_in[...] + dq[:, :local].astype(BF16)
    qt_scr[...] = dq.T[at, :].astype(BF16)
    small_ref[...] = jnp.zeros_like(small_ref) if h == 0 else small_in[...]
    for i in range(5):
        old = jnp.zeros((1, wide), F32) if h == 0 else small_in[i : i + 1, :]
        small_ref[i : i + 1, :] = jnp.where(mine, sums[i], old)
    word_q = (qf_ref[...] + bias_ref[0:1, :]).astype(BF16).astype(F32) * 0.125
    kg = dot_nn(word_q.T[at, :].astype(BF16), s_scr[...]).astype(BF16)
    kg_ref[...] = kg
    for copy in copies[5:8]:
        copy.wait()
    all_ref[2] = dot_nn(vg, joined_ref[...]).astype(BF16)
    all_ref[0] = dot_nn(qt_scr[...], stream_ref[...]).astype(BF16)
    all_ref[1] = dot_nn(kg, joined_ref[...]).astype(BF16)
    all_ref[3] = dot_nn(rg_acc[...].astype(BF16), table_ref[...]).astype(BF16)
    if h == heads - 1:
        for copy in copies[8:]:
            copy.wait()
        half = row_mine.shape[0]
        core = ids_ref[1]
        own = key_scr.shape[0] // 4
        mem = keys - key_scr.shape[0]
        wq_ref, wk_ref, wv_ref = weights
        key_grad = jnp.concatenate([k[:, mem:].astype(F32) for k in (*kgs, kg_ref)], axis=0).T.astype(BF16)
        value_grad = jnp.concatenate([k[:, mem:].astype(F32) for k in (*vgs, vg_ref)], axis=0).T.astype(BF16)
        key_scr[...] = dot_nn(key_grad, wk_ref[...]) + dot_nn(value_grad, wv_ref[...])
        for step in range(2):
            c = core if step else 1 - core
            rows_part = dot_nn(dq_ref[at16(c * half, half), :], wq_ref[...])
            to = row_mine if step else row_other
            to[0:own, :] = (rows_part[:own] + key_scr[at16(c * own, own), :]).astype(BF16)
            to[own : 2 * own, :] = (rows_part[own : 2 * own] + key_scr[at16((2 + c) * own, own), :]).astype(BF16)
            to[2 * own :, :] = rows_part[2 * own :].astype(BF16)
        norm = norm_ref[...] + norm_core_ref[...]
        width = norm.shape[1]
        tail = jnp.concatenate([small_ref[...], jnp.zeros((8, width - wide), F32)], axis=1)
        row = lax.broadcasted_iota(jnp.int32, (8, width), 0)
        norm = jnp.where(row == 5, inner_ref[...], norm)
        extra_scr[0:16, :] = jnp.concatenate([norm, tail], axis=0).astype(BF16)
    extra = extra_scr.shape[0] // 2
    for i in range(4):
        to = slice(i * part, (i + 1) * part)
        mine_ref[to, :] = all_ref[i, at16(side * part, part), :]
        other_ref[to, :] = all_ref[i, at16((1 - side) * part, part), :]
    if mine_ref.shape[0] > 4 * part:
        to = slice(4 * part, 4 * part + extra)
        mine_ref[to, :] = extra_scr[at16(side * extra, extra), :]
        other_ref[to, :] = extra_scr[at16((1 - side) * extra, extra), :]


def attend_backward(h, blocks, ids, p, far, shared, first, carried, final, head_size, length):
    heads, rows, keys = p.shape
    wide, total_rel = far[2].shape[1], far[2].shape[0]
    width = far[4].shape[1]
    local = heads * head_size
    last = h == heads - 1
    extra = local if h == 0 else 64 if last else 0
    part = (4 * head_size + extra) // 2
    ins = (ids, p, *far, *shared, *(first if h == 0 else carried), *(final if last else ()))
    outs = [
        ((rows, local), BF16),
        ((8, wide), F32),
        ((head_size, keys), BF16),
        ((head_size, keys), BF16),
        ((part, width), BF16),
        ((part, width), BF16),
    ]
    if h == 0:
        outs += [((rows, local), BF16), ((local, rows), BF16)]
    anywhere = pl.BlockSpec(memory_space=pl.ANY)
    in_specs = {i: anywhere for i in range(1, 2 + len(far))}
    scratch = []
    if last:
        outs += [((rows // 2, width), BF16)] * 2
        in_specs.update({len(ins) - 1 - i: anywhere for i in range(3)})
        scratch = [pltpu.VMEM((local, width), BF16)] * 3 + [pltpu.VMEM((length, width), F32)]
    return call(
        functools.partial(attend_backward_kernel, h, heads, blocks, head_size, length),
        f"attend_backward_{h}", ins, outs,
        [
            pltpu.VMEM((rows, keys), BF16),
            pltpu.VMEM((head_size, total_rel), F32),
            pltpu.VMEM((head_size, rows), BF16),
            pltpu.VMEM((4, head_size, width), BF16),
            pltpu.VMEM((max(extra, 64), width), BF16),
            pltpu.VMEM((rows if h == 0 else 16, width), BF16),
            pltpu.VMEM((rows, keys), BF16),
            *[pltpu.VMEM(x.shape, x.dtype) for x in far],
            pltpu.SemaphoreType.DMA((11,)),
            pltpu.VMEM((rows, keys), F32),
            pltpu.VMEM((rows, wide), F32),
            pltpu.VMEM((rows, wide), F32),
            pltpu.VMEM((blocks[2][1], total_rel), BF16),
            *scratch,
        ],
        smem=(0,), limit=60, in_specs=in_specs,
    )


def norm_parts(x):
    center = x - jnp.mean(x, axis=-1, keepdims=True)
    scale = lax.rsqrt(jnp.mean(center * center, axis=-1, keepdims=True) + norm_eps)
    return center * scale, scale


def norm_back(grad, gain, unit, scale):
    along = grad * gain
    return scale * (
        along
        - jnp.mean(along, axis=-1, keepdims=True)
        - unit * jnp.mean(along * unit, axis=-1, keepdims=True)
    )


def stage_kernel(*refs):
    n = len(refs) // 2
    for a, b in zip(refs[:n], refs[n:]):
        b[...] = a[...]


def stage(*arrays):
    return call(stage_kernel, "stage", arrays, [(x.shape, x.dtype) for x in arrays], limit=10)


def feed_forward_kernel(
    ids_ref, a0_ref, a1_ref, a2_ref, a3_ref, w0_ref, w1_ref, w2_ref, w3_ref, stream_ref,
    gain_ref, shift_ref, wi_ref, bi_ref, wo_ref,
    hid_ref, act_ref, gp_ref, mixed_ref, mine_ref, other_ref,
):
    half = mine_ref.shape[0]
    local = w0_ref.shape[0]
    core = ids_ref[1]
    gain, shift = gain_ref[...].astype(F32), shift_ref[...].astype(F32)
    packed = [a[...].astype(F32) for a in (a0_ref, a1_ref, a2_ref, a3_ref)]
    turned = [pltpu.roll(a, local, 1)[:, :local] for a in packed]
    for step in range(2):
        rows = at16((core if step else 1 - core) * half, half)
        first = core == (0 if step else 1)
        att = [jnp.where(first, a[:, :local], b).astype(BF16) for a, b in zip(packed, turned)]
        out = dot_nn(att[0], w0_ref[...]) + dot_nn(att[1], w1_ref[...])
        out = out + dot_nn(att[2], w2_ref[:local, :]) + dot_nn(att[3], w3_ref[:local, :])
        mixed = stream_ref[rows, :].astype(F32) + out
        if step:
            mixed_ref[...] = mixed
        unit, _ = norm_parts(mixed)
        hidden = (unit * gain + shift).astype(BF16)
        hid_ref[rows, :] = hidden
        inner = dot_nn(hidden, wi_ref[...]) + bi_ref[...].astype(F32)
        square = inner * inner
        turn = jnp.tanh(gelu_root * (inner + gelu_cubic * square * inner))
        lift = 0.5 * (1.0 + turn)
        slope = lift + 0.5 * inner * (1.0 - turn * turn) * (gelu_root * (1.0 + 3.0 * gelu_cubic * square))
        active = (inner * lift).astype(BF16)
        act_ref[rows, :] = active
        gp_ref[rows, :] = slope.astype(BF16)
        part = dot_nn(active, wo_ref[...]).astype(BF16)
        if step:
            mine_ref[...] = part
        else:
            other_ref[...] = part


def feed_forward(ids, atts, wos, stream, gain, shift, wi, bi, wo):
    rows, width = stream.shape
    units = wi.shape[1]
    half = rows // 2
    ins = (ids, *atts, *wos, stream, gain, shift, wi, bi, wo)
    outs = [
        ((rows, width), BF16),
        ((rows, units), BF16),
        ((rows, units), BF16),
        ((half, width), F32),
        ((half, width), BF16),
        ((half, width), BF16),
    ]
    return call(feed_forward_kernel, "feed_forward", ins, outs, smem=(0,), limit=32)


def second_norm_kernel(
    ids_ref, a_ref, b_ref, mixed_ref, cot_ref, pcot_ref, late_ref, g1_ref, s1_ref, ob_ref, g2_ref, s2_ref,
    content_ref, pick_ref, og_ref, sg_ref, sums_ref, cot_scr, out_scr,
):
    own, picks = cot_ref.shape[0], pcot_ref.shape[0]
    side = ids_ref[2]
    skip = late_ref.shape[0] - own - picks
    cot_scr[at16(side * own, own), :] = cot_ref[...].astype(F32)
    cot_scr[at16((1 - side) * own, own), :] = late_ref[skip : skip + own, :].astype(F32)
    a = pcot_ref[...].astype(F32)
    b = late_ref[skip + own :, :].astype(F32)
    cot_scr[2 * own : 2 * own + picks, :] = jnp.where(side == 0, a, b)
    cot_scr[2 * own + picks :, :] = jnp.where(side == 0, b, a)
    gain = g2_ref[...].astype(F32)
    unit, _ = norm_parts(mixed_ref[...])
    hidden = unit * g1_ref[...].astype(F32) + s1_ref[...].astype(F32)
    total = a_ref[...].astype(F32) + b_ref[...].astype(F32)
    unit, scale = norm_parts(hidden + total + ob_ref[...].astype(F32))
    out_scr[...] = unit * gain + s2_ref[...].astype(F32)
    content_ref[...] = out_scr[at16(side * own, own), :].astype(BF16)
    pick_ref[...] = jnp.where(
        side == 0, out_scr[2 * own : 2 * own + picks, :], out_scr[2 * own + picks :, :]
    ).astype(BF16)
    cot = cot_scr[...]
    grad = norm_back(cot, gain, unit, scale)
    low = grad.astype(BF16)
    og_ref[...] = low
    sg_ref[...] = grad
    sums_ref[...] = jnp.zeros_like(sums_ref)
    sums_ref[0:1, :] = row_sum(low.astype(F32))
    sums_ref[1:2, :] = row_sum(cot * unit)
    sums_ref[2:3, :] = row_sum(cot)


def second_norm(ids, a, b, mixed, cot, pcot, late, vectors):
    ins = (ids, a, b, mixed, cot, pcot, late, *vectors)
    shape = a.shape
    outs = [(cot.shape, BF16), (pcot.shape, BF16), (shape, BF16), (shape, F32), ((8, shape[1]), F32)]
    return call(
        second_norm_kernel, "second_norm", ins, outs, [pltpu.VMEM(shape, F32)] * 2, smem=(0,), limit=24
    )


def feed_backward_kernel(
    ids_ref, mine_ref, other_ref, gp_ref, wi_ref, wo_ref, ig_ref, og_ref, bm_ref, bo_ref, sums_ref
):
    half = mine_ref.shape[0]
    core = ids_ref[1]
    total = jnp.zeros((1, gp_ref.shape[1]), F32)
    for step in range(2):
        rows = at16((core if step else 1 - core) * half, half)
        og = mine_ref[...] if step else other_ref[...]
        og_ref[rows, :] = og
        grad = (dot_nt(og, wo_ref[...]) * gp_ref[rows, :].astype(F32)).astype(BF16)
        ig_ref[rows, :] = grad
        total = total + row_sum(grad.astype(F32))
        part = dot_nt(grad, wi_ref[...]).astype(BF16)
        if step:
            bm_ref[...] = part
        else:
            bo_ref[...] = part
    sums_ref[...] = total


def feed_backward(ids, mine, other, gp, wi, wo):
    rows, units = gp.shape
    half, width = mine.shape
    ins = (ids, mine, other, gp, wi, wo)
    outs = [
        ((rows, units), BF16),
        ((rows, width), BF16),
        ((half, width), BF16),
        ((half, width), BF16),
        ((1, units), F32),
    ]
    return call(feed_backward_kernel, "feed_backward", ins, outs, smem=(0,), limit=24)


def first_norm_kernel(a_ref, b_ref, sg_ref, mixed_ref, gain_ref, sums_in, mg_ref, ag_ref, sums_ref):
    grad = sg_ref[...] + a_ref[...].astype(F32) + b_ref[...].astype(F32)
    unit, scale = norm_parts(mixed_ref[...])
    out = norm_back(grad, gain_ref[...].astype(F32), unit, scale)
    mg_ref[...] = out
    ag_ref[...] = out.astype(BF16)
    sums_ref[...] = sums_in[...]
    sums_ref[3:4, :] = row_sum(grad * unit)
    sums_ref[4:5, :] = row_sum(grad)


def first_norm(a, b, sg, mixed, gain, sums):
    ins = (a, b, sg, mixed, gain, sums)
    shape = a.shape
    outs = [(shape, F32), (shape, BF16), (sums.shape, F32)]
    return call(first_norm_kernel, "first_norm", ins, outs, limit=16)


def add_kernel(a_ref, b_ref, o_ref):
    o_ref[...] = (a_ref[...].astype(F32) + b_ref[...].astype(F32)).astype(BF16)


def add(a, b):
    return call(add_kernel, "add", (a, b), [(a.shape, BF16)], limit=8)[0]


def row_split_kernel(own, picks, ids_ref, a_ref, b_ref, mg_ref, keep_ref, keep_pick_ref, send_ref, scr):
    side = ids_ref[2]
    scr[...] = (a_ref[...].astype(F32) + b_ref[...].astype(F32)).astype(BF16).astype(F32)
    first, second = scr[2 * own : 2 * own + picks, :], scr[2 * own + picks :, :]
    send_ref[0:own, :] = scr[at16((1 - side) * own, own), :].astype(BF16)
    send_ref[own:, :] = jnp.where(side == 0, second, first).astype(BF16)
    keep_ref[...] = scr[at16(side * own, own), :] + mg_ref[at16(side * own, own), :]
    grad = jnp.where(side == 0, mg_ref[2 * own : 2 * own + picks, :], mg_ref[2 * own + picks :, :])
    keep_pick_ref[...] = jnp.where(side == 0, first, second) + grad


def row_split(own, picks, ids, a, b, mg):
    width = a.shape[1]
    outs = [((own, width), F32), ((picks, width), F32), ((own + picks, width), BF16)]
    return call(
        functools.partial(row_split_kernel, own, picks), "row_split", (ids, a, b, mg), outs,
        [pltpu.VMEM(a.shape, F32)], smem=(0,), limit=12,
    )


def row_finish_kernel(keep_ref, keep_pick_ref, got_ref, content_ref, pick_ref):
    own = keep_ref.shape[0]
    content_ref[...] = keep_ref[...] + got_ref[:own, :].astype(F32)
    pick_ref[...] = keep_pick_ref[...] + got_ref[own:, :].astype(F32)


def row_finish(keep, keep_pick, got):
    outs = [(keep.shape, F32), (keep_pick.shape, F32)]
    return call(row_finish_kernel, "row_finish", (keep, keep_pick, got), outs, limit=8)


def pair_grad_kernel(bit, ids_ref, a_ref, b_ref, mine_ref, other_ref):
    half = mine_ref.shape[0]
    side = ids_ref[3 + bit]
    for step in range(2):
        cols = pl.ds(pl.multiple_of((side if step else 1 - side) * half, 128), half)
        out = dot_tn(a_ref[:, cols], b_ref[...]).astype(BF16)
        if step:
            mine_ref[...] = out
        else:
            other_ref[...] = out


def pair_grads(ids, a, b, bit):
    outs = [((a.shape[1] // 2, b.shape[1]), BF16)] * 2
    return call(functools.partial(pair_grad_kernel, bit), "pair_grads", (ids, a, b), outs, smem=(0,), limit=16)


def batch_swap(x, bit):
    n = lax.axis_size("batch")
    return lax.ppermute(x, "batch", [(i, i ^ (1 << bit)) for i in range(n)])


def after(x, *others):
    return lax.optimization_barrier((x, *others))[0]


class BatchSum:
    def __init__(self, mine, other, turn=0):
        self.bits = lax.axis_size("batch").bit_length() - 1
        self.order = [(i + turn) % self.bits for i in range(self.bits)]
        self.step, self.x, self.first = 0, mine, other
        self.coming, self.start, self.tied = None, 0, False

    def next_step(self):
        last = self.bits - 1
        if self.coming is None:
            return "first", 0, self.order[0]
        if self.step == 2 * last:
            return None
        self.step += 1
        step = self.step
        if step < last:
            return "split", self.order[step], self.order[step]
        if step == last:
            return "add", 0, self.order[last]
        bit = self.order[2 * last - step]
        if step == last + 1:
            return "add", 0, bit
        return "spread", self.order[2 * last + 1 - step], bit

    def got(self):
        return lax.slice_in_dim(self.coming, self.start, self.start + self.x.shape[0], axis=0)

    def finished(self):
        return self.step == 2 * self.bits - 2

    def total(self):
        side = (lax.axis_index("batch") >> self.order[0]) & 1
        x, y = self.x, self.got()
        return jnp.where(side == 0, jnp.concatenate([x, y]), jnp.concatenate([y, x]))


def up16(n):
    return -(-n // 16) * 16


def step_kernel(jobs, sizes, ids_ref, *refs):
    ins, outs = refs[: len(refs) - len(sizes)], refs[len(refs) - len(sizes) :]
    for kind, bit, x_at, got_at, start, to, sent, place in jobs:
        x = ins[x_at][...].astype(F32)
        if kind != "first":
            n = x.shape[0]
            side = ids_ref[3 + bit]
            y = ins[got_at][start : start + up16(n), :].astype(F32)[:n, :]
            if kind == "spread":
                low, high = jnp.where(side == 0, x, y), jnp.where(side == 0, y, x)
                x = jnp.concatenate([low, high], axis=0)
            else:
                x = (x + y).astype(BF16).astype(F32)
            if kind == "split":
                low, high = x[: n // 2, :], x[n // 2 :, :]
                outs[to][...] = jnp.where(side == 0, low, high).astype(BF16)
                x = jnp.where(side == 0, high, low)
            elif to is not None:
                outs[to][...] = x.astype(BF16)
        if sent is not None:
            n = x.shape[0]
            if n % 16:
                x = jnp.concatenate([x, jnp.zeros((up16(n) - n, x.shape[1]), F32)], axis=0)
            outs[sent][place : place + up16(n), :] = x.astype(BF16)


def round_of(chains, ids, *others):
    todo = []
    for c in chains:
        step = c.next_step()
        if step is not None:
            kind, half_bit, bit = step
            n = c.first.shape[0] if kind == "first" else c.x.shape[0]
            n = {"split": n // 2, "spread": 2 * n}.get(kind, n)
            todo.append((c, kind, half_bit, bit, n))
    groups = {}
    for item in todo:
        groups.setdefault(item[3], []).append(item)
    plain = all(item[4] % 8 == 0 and item[0].x.shape[0] % 8 == 0 for item in todo)
    width = chains[0].x.shape[1]
    sends = {}
    if plain:
        jobs, ins, outs = [], [ids], []

        def source(x):
            ins.append(x)
            return len(ins) - 2

        results = []
        for bit, items in groups.items():
            shared = len(items) > 1
            sent, place = None, 0
            if shared or items[0][1] == "split":
                outs.append(sum(up16(item[4]) for item in items))
                sent = len(outs) - 1
            for c, kind, half_bit, _, n in items:
                job_sent = sent
                if kind == "first":
                    if shared:
                        jobs.append((kind, 0, source(c.first), 0, 0, None, sent, place))
                    results.append((c, None, bit, sent, place, c.first))
                else:
                    outs.append(n)
                    to = len(outs) - 1
                    jobs.append((kind, half_bit, source(c.x), source(c.coming), c.start, to, sent, place))
                    results.append((c, to, bit, sent, place, None))
                place += up16(n)
        made = ()
        if jobs:
            shapes = [((n, width), BF16) for n in outs]
            made = call(functools.partial(step_kernel, jobs, outs), "step", ins, shapes, smem=(0,), limit=14)
        for c, to, bit, sent, place, first in results:
            if to is not None:
                c.x = made[to]
            c.start = place
            sends[bit] = made[sent] if sent is not None else (first if to is None else c.x)
    else:
        me = lax.axis_index("batch")
        for c, kind, half_bit, bit, n in todo:
            x = c.first
            if kind != "first":
                side = (me >> half_bit) & 1
                y = c.got()
                if kind == "spread":
                    c.x = jnp.where(side == 0, jnp.concatenate([c.x, y]), jnp.concatenate([y, c.x]))
                else:
                    c.x = c.x + y
                x = c.x
            if kind == "split":
                c.x = lax.dynamic_slice_in_dim(x, side * n, n, 0)
                x = lax.dynamic_slice_in_dim(x, (1 - side) * n, n, 0)
            c.start = 0
            if bit in sends:
                c.start = up16(sends[bit].shape[0])
                gap = jnp.zeros((c.start - sends[bit].shape[0], width), BF16)
                x = jnp.concatenate([sends[bit], gap, x])
            sends[bit] = x
    settled = [c for c in chains if c.finished() and not c.tied and all(c is not item[0] for item in todo)]
    bits = list(sends)
    tied = lax.optimization_barrier((*[sends[b] for b in bits], *[c.coming for c in settled], *others))
    for c, x in zip(settled, tied[len(bits) :]):
        c.coming, c.tied = x, True
    arrived = {b: batch_swap(x, b) for b, x in zip(bits, tied)}
    for c, _, _, bit, _ in todo:
        c.coming = arrived[bit]
    return tied[len(bits) + len(settled) :]


def finish_kernel(heads, head_size, starts, ids_ref, *refs):
    pairs, refs = refs[: 2 * heads], refs[2 * heads :]
    qo, ko, vo, oo, ro, wb, pb, sb, se, vec, scr, small = refs
    side = ids_ref[3]
    part = head_size // 2
    local = heads * head_size
    for h in range(heads):
        for i in range(4):
            for s in range(2):
                start = i * part + (starts[h] if s else 0)
                source = pairs[2 * h + s][start : start + part, :]
                place = side if s == 0 else 1 - side
                scr[i, at16(h * head_size + place * part, part), :] = source.astype(F32)
    for i, to in enumerate((qo, ko, vo, ro)):
        to[...] = scr[i]
    half = local // 2
    for s in range(2):
        place = side if s == 0 else 1 - side
        start = 4 * part + (starts[0] if s else 0)
        oo[at16(place * half, half), :] = pairs[s][start : start + half, :].astype(F32)
        start = 4 * part + (starts[-1] if s else 0)
        small[at16(place * 16, 16), :] = pairs[2 * heads - 2 + s][start : start + 16, :].astype(F32)
    vec[...] = small[0:8, :]
    for h in range(heads):
        at = slice(h * head_size, (h + 1) * head_size)
        for i, to in enumerate((wb, pb, sb)):
            to[h : h + 1, :] = small[8 + i : 9 + i, at]
        for c in range(2):
            se[c, h : h + 1, :] = small[11 + c : 12 + c, at]


def finish(ids, pairs, starts, heads, head_size):
    width = pairs[0].shape[1]
    local = heads * head_size
    outs = [((local, width), F32)] * 5
    outs += [((heads, head_size), F32)] * 3 + [((2, heads, head_size), F32), ((8, width), F32)]
    return call(
        functools.partial(finish_kernel, heads, head_size, starts), "finish", (ids, *pairs), outs,
        [pltpu.VMEM((4, local, width), F32), pltpu.VMEM((32, width), F32)], smem=(0,), limit=24,
    )


def on_device(
    content, query_stream, memory, has_memory, order_rank, targets, segments,
    query_weight, key_weight, value_weight, output_weight, relative_weight,
    word_bias, position_bias, segment_bias, segment_embed, first_gain, first_shift,
    inner_weight, inner_bias, outer_weight, outer_bias, second_gain, second_shift,
    content_cotangent, query_cotangent,
):
    parts = lax.axis_size("head")
    me = lax.axis_index("head")
    core_perm = [(i, i ^ 1) for i in range(parts)]
    x_perm = [(i, i ^ 2) for i in range(parts)]

    def swap_core(x):
        return lax.ppermute(x, "head", core_perm)

    def swap_x(x):
        return lax.ppermute(x, "head", x_perm)

    own, width = content.shape[1:]
    own_picks, own_memory = query_stream.shape[1], memory.shape[1]
    length, mem = own * parts, own_memory * parts
    keys = mem + length
    heads, head_size = word_bias.shape
    local = heads * head_size
    wide = local + head_size
    half = 2 * (own + own_picks)
    rows = 2 * half
    bits = lax.axis_size("batch").bit_length() - 1
    group = lax.axis_index("batch")
    ids = jnp.stack([me, me % 2, me // 2, *[(group >> i) & 1 for i in range(bits)]]).astype(jnp.int32)
    blocks = (
        (0, own, 0),
        (own, own, 2 * own),
        (2 * own, 2 * own_picks, None),
        (half, own, own),
        (half + own, own, 3 * own),
        (half + 2 * own, 2 * own_picks, None),
    )

    turned = (query_weight.T, key_weight.T, value_weight.T)
    own_rows = pack(content[0], memory[0], query_stream[0])
    x_rows = swap_x(own_rows)
    core_rows = swap_core(own_rows)
    table = jnp.asarray(position_rows(keys, length, width))
    small_ins = (
        has_memory, order_rank, targets, segments, word_bias, position_bias, segment_bias, segment_embed
    )
    rel, *tables = prepare(small_ins, table, relative_weight.T, own, own_picks, mem, wide)
    late = pack(output_weight, content_cotangent[0], after(query_cotangent[0], own_rows))
    x_rows, ids = lax.optimization_barrier((x_rows, ids, rel, late))[:2]
    diag_rows = swap_core(x_rows)
    late_x = swap_x(after(late, rel))
    wo_core = swap_core(output_weight)
    p, att, qf, kc, v, stream, joined, col = attend_forward(
        blocks, ids, (own_rows, core_rows, x_rows, diag_rows), own, turned, rel, tables,
        heads, head_size, mem, rows,
    )
    bias = tables[2]
    att_x = swap_x(att)
    att_core = swap_core(att)
    late_diag = swap_core(after(late_x, att))
    wi, wo = stage(after(inner_weight, att), after(outer_weight, att))
    att_x = after(att_x, wi)
    att_diag = swap_core(att_x)

    def vector(x):
        return x.reshape(1, -1)

    hid, act, gp, mixed, part_mine, part_other = feed_forward(
        ids, (att, att_core, att_x, att_diag), (output_weight, wo_core, late_x, late_diag), stream,
        vector(first_gain), vector(first_shift), wi, vector(inner_bias), wo,
    )
    chip_part = add(part_mine, swap_core(part_other))
    vectors = [vector(x) for x in (first_gain, first_shift, outer_bias, second_gain, second_shift)]
    content_out, query_out, og_half, sg_half, sums = second_norm(
        ids, chip_part, swap_x(chip_part), mixed, content_cotangent[0], query_cotangent[0], late_x, vectors
    )
    ig, og, back_mine, back_other, inner_sums = feed_backward(
        ids, og_half, swap_core(og_half), gp, wi, wo
    )
    chip_back = add(back_mine, swap_core(back_other))
    back_x = swap_x(chip_back)
    outer_chain = BatchSum(*pair_grads(ids, act, after(og, chip_back), 0))
    inner_chain = BatchSum(*pair_grads(ids, hid, after(ig, chip_back), 1), 1)
    ff_chains = [outer_chain, inner_chain]
    round_of(ff_chains, ids)
    mg_half, ag_half, sums = first_norm(chip_back, back_x, sg_half, mixed, vector(first_gain), sums)
    ag_other = swap_core(ag_half)
    sums_core = swap_core(sums)

    far = (v, kc, rel, qf, joined, stream, table)
    chains, kgs, vgs = list(ff_chains), [], []
    carried = None
    (tied,) = round_of(ff_chains, after(ids, ag_half), ids)
    for h in range(heads):
        outs = attend_backward(
            h, blocks, tied, p, far, (col, bias), (ag_half, ag_other, output_weight, att), carried,
            (sums, sums_core, inner_sums, *kgs, *vgs, *turned), head_size, length,
        )
        dq, small, kg, vg, mine, other = outs[:6]
        if h == 0:
            grads_in = outs[6:]
        carried = (*grads_in, dq, small)
        kgs.append(kg)
        vgs.append(vg)
        chains.append(BatchSum(mine, other))
        if h < heads - 1:
            (tied,) = round_of(chains, after(ids, dq), ids)
    row_mine, row_other = outs[6:]
    (row_other,) = round_of(chains, after(ids, dq), row_other)
    keep, keep_pick, send = row_split(own, own_picks, ids, row_mine, swap_core(row_other), mg_half)
    (send,) = round_of(chains, ids, send)
    got = swap_x(send)
    totals = []
    while not chains[-1].finished():
        carried = [got] if isinstance(got, jax.Array) else list(got)
        if not totals and all(c.finished() for c in ff_chains):
            totals = [c.total().astype(F32) for c in ff_chains]
        mixed_out = round_of(chains, ids, *carried, *totals)
        totals = list(mixed_out[len(carried) :])
        got = mixed_out[: len(carried)]
        if len(got) == 1:
            got = row_finish(keep, keep_pick, got[0])
    content_grad, query_grad = got
    outer_sum, inner_sum = totals
    pairs = [half for c in chains[2:] for half in (c.x, c.coming)]
    q, k, v_, o, r, wb, pb, sb, se, vec = finish(ids, pairs, [c.start for c in chains[2:]], heads, head_size)
    return (
        content_out[None],
        query_out[None],
        content_grad[None],
        query_grad[None],
        q.T, k.T, v_.T, o, r.T, wb, pb, sb, se,
        vec[3],
        vec[4],
        inner_sum,
        vec[5],
        outer_sum,
        vec[0],
        vec[1],
        vec[2],
    )


def solution(mesh):
    rows = P("batch", "head", None)
    ids = P("batch", None)
    columns = P(None, "head")
    by_head = P("head", None)
    table = P(None, "head", None)
    return jax.shard_map(
        on_device,
        mesh=mesh,
        in_specs=(
            rows, rows, rows, P("batch"), ids, ids, ids,
            columns, columns, columns, by_head, columns,
            by_head, by_head, by_head, table, P(), P(),
            columns, P("head"), by_head, P(), P(), P(), rows, rows,
        ),
        out_specs=(
            rows, rows, rows, rows,
            columns, columns, columns, by_head, columns,
            by_head, by_head, by_head, table, P(), P(),
            columns, P("head"), by_head, P(), P(), P(),
        ),
        check_vma=False,
    )
```

```python
import functools
import jax
import jax.numpy as jnp
import numpy as np
from jax import lax
from jax.experimental import pallas as pl
from jax.experimental.pallas import tpu as pltpu
from jax.sharding import PartitionSpec as P

masked_score = -1e30
norm_eps = 1e-05
gelu_root = 0.7978845608028654
gelu_cubic = 0.044715
hidden_key = 1e6
F32 = jnp.float32
BF16 = jnp.bfloat16
MIB = 1024 * 1024
SMEM_SPEC = pl.BlockSpec(memory_space=pltpu.SMEM)


def dot_nt(a, b):
    return lax.dot_general(a, b, (((1,), (1,)), ((), ())), preferred_element_type=F32)


def dot_nn(a, b):
    return lax.dot_general(a, b, (((1,), (0,)), ((), ())), preferred_element_type=F32)


def dot_tn(a, b):
    return lax.dot_general(a, b, (((0,), (0,)), ((), ())), preferred_element_type=F32)


def position_rows(key_count, length, width):
    steps = key_count - 1 - np.arange(key_count + length, dtype=np.float64)
    freqs = 10000.0 ** (-np.arange(0, width, 2, dtype=np.float64) / width)
    angles = steps[:, None] * freqs[None, :]
    return np.concatenate([np.sin(angles), np.cos(angles)], axis=1).astype(jnp.bfloat16)


def whole(shape):
    return pl.BlockSpec(shape, lambda *_: (0,) * len(shape))


def call(kernel, name, ins, outs, scratch=(), grid=(), in_specs=None, out_specs=None, smem=(), limit=24, aliases=None):
    kept = pl.BlockSpec(memory_space=pltpu.VMEM)
    specs = [kept if grid == () else whole(x.shape) for x in ins]
    for i in smem:
        specs[i] = SMEM_SPEC
    for i, spec in (in_specs or {}).items():
        specs[i] = spec
    to = [kept if grid == () else whole(s) for s, _ in outs]
    for i, spec in (out_specs or {}).items():
        to[i] = spec
    return pl.pallas_call(
        kernel,
        grid=grid,
        in_specs=specs,
        out_specs=to,
        out_shape=[jax.ShapeDtypeStruct(s, t) for s, t in outs],
        scratch_shapes=list(scratch),
        input_output_aliases=aliases or {},
        compiler_params=pltpu.CompilerParams(vmem_limit_bytes=limit * MIB),
        cost_estimate=pl.CostEstimate(flops=0, bytes_accessed=0, transcendentals=0),
        name=name,
    )(*ins)


def at16(i, n):
    return pl.ds(pl.multiple_of(i, 16), n)


def row_sum(x):
    return jnp.sum(x, axis=0, keepdims=True)


def pack_kernel(*refs):
    start = 0
    for part in refs[:-1]:
        refs[-1][start : start + part.shape[0], :] = part[...]
        start += part.shape[0]


def pack(*ins):
    shape = (sum(x.shape[0] for x in ins), ins[0].shape[1])
    return call(pack_kernel, "pack", ins, [(shape, BF16)], limit=60)[0]


def prepare_kernel(
    own, own_picks, mem,
    present_ref, rank_ref, pick_ref, seg_ref, wb_ref, pb_ref, sb_ref, se_ref, table_ref, w_ref,
    rel_ref, col_ref, key_ref, bias_ref, embed_ref, row_ref,
):
    local, wide = w_ref.shape[0], rel_ref.shape[1]
    head_size = wb_ref.shape[1]
    length = rank_ref.shape[1]
    half = 2 * (own + own_picks)
    rel_ref[...] = jnp.zeros_like(rel_ref)
    rel_ref[:, :local] = dot_nt(table_ref[...], w_ref[...]).astype(BF16)

    bias_ref[...] = jnp.zeros_like(bias_ref)
    sources = (wb_ref[...], pb_ref[...], sb_ref[...], se_ref[0], se_ref[1])
    for i, source in enumerate(sources):
        source = source.astype(F32)
        for k in range(source.shape[0]):
            bias_ref[i : i + 1, k * head_size : (k + 1) * head_size] = source[k : k + 1, :]
    turned = bias_ref[...].T
    lane = lax.broadcasted_iota(jnp.int32, embed_ref.shape, 1)
    left = lane < wide
    lane = jnp.where(left, lane, lane - wide)
    same, other = turned[:, 3:4], turned[:, 4:5]
    a = jnp.where(left, same, other)
    b = jnp.where(left, other, same)
    is_zero = (lane == local) | (lane == local + 1)
    is_one = (lane == local + 2) | (lane == local + 3)
    embed_ref[...] = jnp.where(is_zero, a, jnp.where(is_one, b, 0.0)).astype(BF16)

    ranks = rank_ref[...].astype(F32)
    labels = seg_ref[...].astype(F32)
    row = lax.broadcasted_iota(jnp.int32, (8, length), 0)
    content_col = jnp.where(row == 0, ranks + 1.0, jnp.where(row == 1, labels, 0.0)).T
    key_ref[...] = content_col
    pick_row = jnp.broadcast_to(pick_ref[...].astype(F32), (8, pick_ref.shape[1]))
    picks = pick_row.T[:, 0:1]
    spot = lax.broadcasted_iota(jnp.int32, (picks.shape[0], length), 1).astype(F32)
    hit = spot == picks
    pick_rank = jnp.sum(jnp.where(hit, ranks, 0.0), axis=1, keepdims=True)
    pick_label = jnp.sum(jnp.where(hit, labels, 0.0), axis=1, keepdims=True)
    lane8 = lax.broadcasted_iota(jnp.int32, (picks.shape[0], 8), 1)
    shift = (length - 1.0) - picks
    pick_col = jnp.where(
        lane8 == 0, pick_rank, jnp.where(lane8 == 1, pick_label, jnp.where(lane8 == 2, shift, 0.0))
    )
    for c in range(2):
        for x in range(2):
            owner = 2 * x + c
            to = c * half + x * own
            col_ref[to : to + own, :] = content_col[owner * own : (owner + 1) * own, :]
            to = c * half + 2 * own + x * own_picks
            col_ref[to : to + own_picks, :] = pick_col[owner * own_picks : (owner + 1) * own_picks, :]
    memory_rank = jnp.where(present_ref[0] > 0, -1.0, hidden_key)
    row_ref[:, :mem] = jnp.full((8, mem), memory_rank, F32)
    row_ref[:, mem:] = jnp.broadcast_to(ranks, (8, length))


def prepare(small, table, w, own, own_picks, mem, wide):
    length = 4 * own
    outs = [
        ((table.shape[0], wide), BF16),
        ((4 * (own + own_picks), 8), F32),
        ((length, 8), F32),
        ((8, wide), F32),
        ((wide, 2 * wide), BF16),
        ((8, mem + length), F32),
    ]
    return call(
        functools.partial(prepare_kernel, own, own_picks, mem), "prepare", (*small, table, w), outs,
        smem=(0,), limit=60,
    )


def attend_forward_kernel(
    blocks, head_size, mem,
    ids_ref, c0_ref, c1_ref, c2_ref, c3_ref, m0_ref, m1_ref, m2_ref, m3_ref,
    wq_ref, wk_ref, wv_ref, rel_ref, col_in, key_ref, bias_ref, embed_ref, row_ref,
    p_ref, att_ref, col_ref, *refs,
):
    acc_ref, score_scr, rel_scr, place_scr, qf_ref, kc_ref, v_ref, stream_ref, joined_ref, sems = refs[5:]
    near = (qf_ref, kc_ref, v_ref, stream_ref, joined_ref)
    backs = [pltpu.make_async_copy(a, b, sems.at[i]) for i, (a, b) in enumerate(zip(near, refs[:5]))]
    h = pl.program_id(0)
    keys, wide = kc_ref.shape
    local = wq_ref.shape[0]
    length = keys - mem
    own, own_mem = length // 4, mem // 4
    own_picks = m0_ref.shape[0] - own_mem
    half = stream_ref.shape[0] // 2

    @pl.when(h == 0)
    def _():
        core, side = ids_ref[1], ids_ref[2]
        cores = (core, 1 - core, core, 1 - core)
        sides = (side, side, 1 - side, 1 - side)
        content = (c0_ref, c1_ref, c2_ref, c3_ref)
        others = (m0_ref, m1_ref, m2_ref, m3_ref)
        for i in range(4):
            owner = 2 * sides[i] + cores[i]
            rows = content[i][...]
            stream_ref[at16(cores[i] * half + sides[i] * own, own), :] = rows
            joined_ref[at16(mem + owner * own, own), :] = rows
            joined_ref[at16(owner * own_mem, own_mem), :] = others[i][:own_mem, :]
        for i in range(2):
            a = others[i][own_mem:, :].astype(F32)
            b = others[i + 2][own_mem:, :].astype(F32)
            first = jnp.where(side == 0, a, b)
            second = jnp.where(side == 0, b, a)
            both = jnp.concatenate([first, second], axis=0).astype(BF16)
            stream_ref[at16(cores[i] * half + 2 * own, 2 * own_picks), :] = both

        col_ref[...] = col_in[...]
        qf_ref[...] = jnp.zeros_like(qf_ref)
        qf_ref[:, :local] = dot_nt(stream_ref[...], wq_ref[...])
        v_ref[...] = jnp.zeros_like(v_ref)
        v_ref[:, :local] = dot_nt(joined_ref[...], wv_ref[...]).astype(BF16)
        key_label = jnp.concatenate([jnp.zeros((mem, 1), F32), key_ref[:, 1:2]], axis=0)
        lane = lax.broadcasted_iota(jnp.int32, (keys, wide), 1)
        is_zero = (lane == local) | (lane == local + 1)
        is_one = (lane == local + 2) | (lane == local + 3)
        kc_ref[...] = jnp.where(is_zero, 1.0 - key_label, jnp.where(is_one, key_label, 0.0)).astype(BF16)
        kc_ref[:, :local] = dot_nt(joined_ref[...], wk_ref[...]).astype(BF16)
        acc_ref[...] = jnp.zeros_like(acc_ref)
        for back in backs:
            back.start()

    lane = lax.broadcasted_iota(jnp.int32, (1, wide), 1)
    mine = (lane >= h * head_size) & (lane < (h + 1) * head_size)
    hi_lane = (lane == local) | (lane == local + 2)
    lo_lane = (lane == local + 1) | (lane == local + 3)
    qf = qf_ref[...]
    word = jnp.where(mine, (qf + bias_ref[0:1, :]).astype(BF16).astype(F32) * 0.125, 0.0)
    place = jnp.where(mine, qf + bias_ref[1:2, :], 0.0).astype(BF16) * 0.125
    label = jnp.where(mine, (qf + bias_ref[2:3, :]) * 0.125, 0.0)
    label_hi = label.astype(BF16)
    label_lo = (label - label_hi.astype(F32)).astype(BF16)
    both = dot_nn(label_hi, embed_ref[...]) + dot_nn(label_lo, embed_ref[...])
    pair = jnp.where(col_ref[:, 1:2] == 0, both[:, :wide], both[:, wide:])
    pair_hi = pair.astype(BF16).astype(F32)
    query = jnp.where(hi_lane, pair_hi, jnp.where(lo_lane, pair - pair_hi, word)).astype(BF16)
    score_scr[...] = dot_nt(query, kc_ref[...])
    place_scr[...] = place

    limit_row = row_ref[0:1, :]
    for start, size, position in blocks:
        place = place_scr[start : start + size, :]
        if position is not None:
            base = length - position - size
            width = keys + size
            rel_scr[:size, :width] = dot_nt(place, rel_ref[base : base + width, :])
        else:
            rel_scr[:size, :] = dot_nt(place, rel_ref[...])
        chunk = 32 if size % 32 == 0 else 16
        for low in range(0, size, chunk):
            blk = slice(start + low, start + low + chunk)
            if position is not None:
                rel = rel_scr[low : low + chunk, :width]
                rel = pltpu.roll(rel, width - (size - 1) + low, 1, stride=1, stride_axis=0)
            else:
                rel = rel_scr[low : low + chunk, :]
                shift = col_ref[blk, 2:3].astype(jnp.int32)
                bit = (length - 1).bit_length()
                while bit > 0:
                    bit -= 1
                    far = 1 << bit
                    left = pltpu.roll(rel, rel.shape[1] - far, 1)
                    rel = jnp.where(((shift >> bit) & 1) == 1, left, rel)
                    rel = rel[:, : -(-(keys + far - 1) // 128) * 128]
            scores = score_scr[blk, :] + rel[:, :keys]
            scores = jnp.where(limit_row < col_ref[blk, 0:1], scores, masked_score)
            top = jnp.max(scores, axis=-1, keepdims=True)
            powers = jnp.exp(scores - top)
            total = jnp.sum(powers, axis=-1, keepdims=True)
            p_ref[0, blk, :] = powers.astype(BF16)
            lane8 = lax.broadcasted_iota(jnp.int32, (chunk, 8), 1)
            col_ref[blk, :] = jnp.where(lane8 == 4 + h, 1.0 / total, col_ref[blk, :])
    lane8 = lax.broadcasted_iota(jnp.int32, col_ref.shape, 1)
    inverse = jnp.sum(jnp.where(lane8 == 4 + h, col_ref[...], 0.0), axis=1, keepdims=True)
    att = dot_nn(p_ref[0], v_ref[...]) * inverse
    acc_ref[...] = jnp.where(mine, att, acc_ref[...])

    @pl.when(h == pl.num_programs(0) - 1)
    def _():
        att_ref[:, :local] = acc_ref[:half, :local].astype(BF16)
        att_ref[:, local:] = acc_ref[half:, :local].astype(BF16)
        for back in backs:
            back.wait()


def attend_forward(blocks, ids, content, others, weights, rel, tables, heads, head_size, mem, rows):
    own, width = content[0].shape
    keys = 4 * own + mem
    wide = rel.shape[1]
    ins = (ids, *content, *others, *weights, rel, *tables)
    outs = [
        ((heads, rows, keys), BF16),
        ((rows // 2, 2 * heads * head_size), BF16),
        ((rows, 8), F32),
        ((rows, wide), F32),
        ((keys, wide), BF16),
        ((keys, wide), BF16),
        ((rows, width), BF16),
        ((keys, width), BF16),
    ]
    anywhere = pl.BlockSpec(memory_space=pl.ANY)
    return call(
        functools.partial(attend_forward_kernel, blocks, head_size, mem),
        "attend_forward", ins, outs,
        [
            pltpu.VMEM((rows, wide), F32),
            pltpu.VMEM((rows, keys), F32),
            pltpu.VMEM((own, rel.shape[0]), F32),
            pltpu.VMEM((rows, wide), BF16),
            *[pltpu.VMEM(shape, kind) for shape, kind in outs[3:]],
            pltpu.SemaphoreType.DMA((5,)),
        ],
        grid=(heads,), smem=(0,), limit=60,
        out_specs={0: pl.BlockSpec((1, rows, keys), lambda h: (h, 0, 0)), **{i: anywhere for i in range(3, 8)}},
    )


def second_half(packed):
    local = packed.shape[1] // 2
    return pltpu.roll(packed.astype(F32), local, 1)[:, :local].astype(BF16)


def attend_backward_kernel(
    h, heads, blocks, head_size, length, *refs,
):
    refs = list(refs)
    ids_ref, p_hbm = refs[:2]
    far, refs = refs[2:9], refs[9:]
    col_ref, bias_ref = refs[:2]
    refs = refs[2:]
    if h == 0:
        ag_ref, ago_ref, wo_ref, att_ref = refs[:4]
        refs = refs[4:]
    else:
        da_ref, dat_ref, dq_in, small_in = refs[:4]
        refs = refs[4:]
    if h == heads - 1:
        norm_ref, norm_core_ref, inner_ref = refs[:3]
        kgs, vgs = refs[3 : 2 + heads], refs[2 + heads : 1 + 2 * heads]
        weights_hbm = refs[1 + 2 * heads : 4 + 2 * heads]
        refs = refs[4 + 2 * heads :]
    dq_ref, small_ref, kg_ref, vg_ref, mine_ref, other_ref = refs[:6]
    refs = refs[6:]
    if h == 0:
        da_ref, dat_ref = refs[:2]
        refs = refs[2:]
    if h == heads - 1:
        row_mine, row_other, few_ref = refs[:3]
        refs = refs[3:]
    s_scr, rg_acc, qt_scr, all_ref, extra_scr, ag_scr = refs[:6]
    p_ref, near, sems = refs[6], refs[7:14], refs[14]
    chance_scr, word_scr, place_scr, wide_scr = refs[15:19]
    v_ref, kc_ref, rel_ref, qf_ref, joined_ref, stream_ref, table_ref = near
    copies = [pltpu.make_async_copy(p_hbm.at[h], p_ref, sems.at[7])]
    copies += [pltpu.make_async_copy(a, b, sems.at[i]) for i, (a, b) in enumerate(zip(far, near))]
    if h == heads - 1:
        weights, key_scr = refs[19:22], refs[22]
        copies += [
            pltpu.make_async_copy(a, b, sems.at[8 + i]) for i, (a, b) in enumerate(zip(weights_hbm, weights))
        ]
    for copy in copies:
        copy.start()
    keys, wide = kc_ref.shape
    total_rel = rel_ref.shape[0]
    local = da_ref.shape[1]
    at = slice(h * head_size, (h + 1) * head_size)
    side = ids_ref[3]
    part = head_size // 2

    if h == 0:
        half = ag_ref.shape[0]
        core = ids_ref[1]
        ag_scr[at16(core * half, half), :] = ag_ref[...]
        ag_scr[at16((1 - core) * half, half), :] = ago_ref[...]
        ag = ag_scr[...]
        grads = dot_nt(ag, wo_ref[...]).astype(BF16).astype(F32)
        turned = dot_nt(wo_ref[...], ag).astype(BF16).astype(F32)
        inverse = col_ref[...].T
        lane = lax.broadcasted_iota(jnp.int32, (1, local), 1)
        factor = jnp.zeros((grads.shape[0], 1), F32)
        for k in range(heads):
            of = slice(k * head_size, (k + 1) * head_size)
            here = (lane >= k * head_size) & (lane < (k + 1) * head_size)
            factor = jnp.where(here, col_ref[:, 4 + k : 5 + k], factor)
            dat_ref[of, :] = (turned[of, :] * inverse[4 + k : 5 + k, :]).astype(BF16)
        da_ref[...] = (grads * factor).astype(BF16)
        packed = att_ref[...]
        extra = dot_tn(packed[:, :local], ag[:half, :]) + dot_tn(second_half(packed), ag[half:, :])
        extra_scr[...] = extra.astype(BF16)

    lane = lax.broadcasted_iota(jnp.int32, (1, wide), 1)
    mine = (lane >= h * head_size) & (lane < (h + 1) * head_size)
    copies[0].wait()
    vg = dot_nn(dat_ref[at, :], p_ref[...]).astype(BF16)
    vg_ref[...] = vg
    for copy in copies[1:5]:
        copy.wait()
    rg_acc[...] = jnp.zeros_like(rg_acc)
    sums = [jnp.zeros((1, wide), F32) for _ in range(5)]
    chance_scr[...] = dot_nt(jnp.where(mine[:, :local], da_ref[...], 0), v_ref[:, :local])
    step = 32
    for start in range(0, p_ref.shape[0], step):
        blk = slice(start, start + step)
        soft = p_ref[blk, :].astype(F32)
        chance = chance_scr[blk, :]
        inner = jnp.sum(chance * soft, axis=-1, keepdims=True) * col_ref[blk, 4 + h : 5 + h]
        s_scr[blk, :] = (soft * (chance - inner)).astype(BF16)
    word_scr[...] = dot_nn(s_scr[...], kc_ref[...]) * 0.125
    for start, size, position in blocks:
        blk = slice(start, start + size)
        score = s_scr[blk, :]
        place = (qf_ref[blk, :] + bias_ref[1:2, :]).astype(BF16) * 0.125
        if position is not None:
            base = length - position - size
            width = keys + size
            turn = (
                lax.broadcasted_iota(jnp.int32, (size, size), 0)
                + lax.broadcasted_iota(jnp.int32, (size, size), 1)
                == size - 1
            ).astype(F32).astype(BF16)
            wider = jnp.concatenate([dot_nn(turn, score), jnp.zeros((size, width - keys), F32)], axis=1)
            wider = pltpu.roll(wider, 0, 1, stride=1, stride_axis=0).astype(BF16)
            placed = dot_nn(wider, rel_ref[base : base + width, :]) * 0.125
            high = placed.astype(BF16)
            low = (placed - high.astype(F32)).astype(BF16)
            place_scr[blk, :] = dot_nn(turn, high) + dot_nn(turn, low)
            place = dot_nn(turn, place)
        else:
            base = 0
            width = total_rel
            for low in range(0, size, 16):
                to = slice(start + low, start + low + 16)
                left = col_ref[to, 2:3].astype(jnp.int32)
                moved = s_scr[to, :].astype(F32)
                bit = 0
                while (1 << bit) < length:
                    need = -(-(keys + (2 << bit) - 1) // 128) * 128
                    if need > moved.shape[1]:
                        moved = jnp.concatenate(
                            [moved, jnp.zeros((16, need - moved.shape[1]), F32)], axis=1
                        )
                    moved = jnp.where(((left >> bit) & 1) == 1, pltpu.roll(moved, 1 << bit, 1), moved)
                    bit += 1
                wide_scr[low : low + 16, :] = moved.astype(BF16)
            wider = wide_scr[...]
            place_scr[blk, :] = dot_nn(wider, rel_ref[...]) * 0.125
            place = place.astype(F32)
        rg_acc[:, base : base + width] += dot_nn(place.T[at, :].astype(BF16), wider)
    step = 152
    for start in range(0, p_ref.shape[0], step):
        blk = slice(start, start + step)
        word, placed = word_scr[blk, :], place_scr[blk, :]
        row_label = col_ref[blk, 1:2]
        zero_key = word[:, local : local + 1]
        one_key = word[:, local + 2 : local + 3]
        same = jnp.where(row_label == 0, zero_key, one_key)
        other = jnp.where(row_label == 0, one_key, zero_key)
        label = same * bias_ref[3:4, :] + other * bias_ref[4:5, :]
        query_label = qf_ref[blk, :] + bias_ref[2:3, :]
        terms = (word, placed, label, query_label * same, query_label * other)
        for i, term in enumerate(terms):
            sums[i] = sums[i] + row_sum(term)
        word_scr[blk, :] = jnp.where(mine, word + placed + label, 0.0)
    dq = word_scr[...]
    if h == 0:
        dq_ref[...] = dq[:, :local].astype(BF16)
    else:
        dq_ref[...] = dq_in[...] + dq[:, :local].astype(BF16)
    qt_scr[...] = dq.T[at, :].astype(BF16)
    small_ref[...] = jnp.zeros_like(small_ref) if h == 0 else small_in[...]
    for i in range(5):
        old = jnp.zeros((1, wide), F32) if h == 0 else small_in[i : i + 1, :]
        small_ref[i : i + 1, :] = jnp.where(mine, sums[i], old)
    word_q = (qf_ref[...] + bias_ref[0:1, :]).astype(BF16).astype(F32) * 0.125
    kg = dot_nn(word_q.T[at, :].astype(BF16), s_scr[...]).astype(BF16)
    kg_ref[...] = kg
    for copy in copies[5:8]:
        copy.wait()
    all_ref[2] = dot_nn(vg, joined_ref[...]).astype(BF16)
    all_ref[0] = dot_nn(qt_scr[...], stream_ref[...]).astype(BF16)
    all_ref[1] = dot_nn(kg, joined_ref[...]).astype(BF16)
    all_ref[3] = dot_nn(rg_acc[...].astype(BF16), table_ref[...]).astype(BF16)
    if h == heads - 1:
        for copy in copies[8:]:
            copy.wait()
        half = row_mine.shape[0]
        core = ids_ref[1]
        own = key_scr.shape[0] // 4
        mem = keys - key_scr.shape[0]
        wq_ref, wk_ref, wv_ref = weights
        key_grad = jnp.concatenate([k[:, mem:].astype(F32) for k in (*kgs, kg_ref)], axis=0).T.astype(BF16)
        value_grad = jnp.concatenate([k[:, mem:].astype(F32) for k in (*vgs, vg_ref)], axis=0).T.astype(BF16)
        key_scr[...] = dot_nn(key_grad, wk_ref[...]) + dot_nn(value_grad, wv_ref[...])
        for step in range(2):
            c = core if step else 1 - core
            rows_part = dot_nn(dq_ref[at16(c * half, half), :], wq_ref[...])
            to = row_mine if step else row_other
            to[0:own, :] = (rows_part[:own] + key_scr[at16(c * own, own), :]).astype(BF16)
            to[own : 2 * own, :] = (rows_part[own : 2 * own] + key_scr[at16((2 + c) * own, own), :]).astype(BF16)
            to[2 * own :, :] = rows_part[2 * own :].astype(BF16)
        norm = norm_ref[...] + norm_core_ref[...]
        width = norm.shape[1]
        tail = jnp.concatenate([small_ref[...], jnp.zeros((8, width - wide), F32)], axis=1)
        row = lax.broadcasted_iota(jnp.int32, (8, width), 0)
        norm = jnp.where(row == 5, inner_ref[...], norm)
        few_ref[...] = jnp.concatenate([norm, tail], axis=0).astype(BF16)
    extra = extra_scr.shape[0] // 2
    for i in range(4):
        to = slice(i * part, (i + 1) * part)
        mine_ref[to, :] = all_ref[i, at16(side * part, part), :]
        other_ref[to, :] = all_ref[i, at16((1 - side) * part, part), :]
    if mine_ref.shape[0] > 4 * part:
        to = slice(4 * part, 4 * part + extra)
        mine_ref[to, :] = extra_scr[at16(side * extra, extra), :]
        other_ref[to, :] = extra_scr[at16((1 - side) * extra, extra), :]


def attend_backward(h, blocks, ids, p, far, shared, first, carried, final, head_size, length):
    heads, rows, keys = p.shape
    wide, total_rel = far[2].shape[1], far[2].shape[0]
    width = far[4].shape[1]
    local = heads * head_size
    last = h == heads - 1
    extra = local if h == 0 else 0
    part = (4 * head_size + extra) // 2
    ins = (ids, p, *far, *shared, *(first if h == 0 else carried), *(final if last else ()))
    outs = [
        ((rows, local), BF16),
        ((8, wide), F32),
        ((head_size, keys), BF16),
        ((head_size, keys), BF16),
        ((part, width), BF16),
        ((part, width), BF16),
    ]
    if h == 0:
        outs += [((rows, local), BF16), ((local, rows), BF16)]
    anywhere = pl.BlockSpec(memory_space=pl.ANY)
    in_specs = {i: anywhere for i in range(1, 2 + len(far))}
    scratch = []
    if last:
        outs += [((rows // 2, width), BF16)] * 2 + [((16, width), BF16)]
        in_specs.update({len(ins) - 1 - i: anywhere for i in range(3)})
        scratch = [pltpu.VMEM((local, width), BF16)] * 3 + [pltpu.VMEM((length, width), F32)]
    return call(
        functools.partial(attend_backward_kernel, h, heads, blocks, head_size, length),
        f"attend_backward_{h}", ins, outs,
        [
            pltpu.VMEM((rows, keys), BF16),
            pltpu.VMEM((head_size, total_rel), F32),
            pltpu.VMEM((head_size, rows), BF16),
            pltpu.VMEM((4, head_size, width), BF16),
            pltpu.VMEM((max(extra, 32), width), BF16),
            pltpu.VMEM((rows if h == 0 else 16, width), BF16),
            pltpu.VMEM((rows, keys), BF16),
            *[pltpu.VMEM(x.shape, x.dtype) for x in far],
            pltpu.SemaphoreType.DMA((11,)),
            pltpu.VMEM((rows, keys), F32),
            pltpu.VMEM((rows, wide), F32),
            pltpu.VMEM((rows, wide), F32),
            pltpu.VMEM((blocks[2][1], total_rel), BF16),
            *scratch,
        ],
        smem=(0,), limit=50, in_specs=in_specs,
    )


def norm_parts(x):
    center = x - jnp.mean(x, axis=-1, keepdims=True)
    scale = lax.rsqrt(jnp.mean(center * center, axis=-1, keepdims=True) + norm_eps)
    return center * scale, scale


def norm_back(grad, gain, unit, scale):
    along = grad * gain
    return scale * (
        along
        - jnp.mean(along, axis=-1, keepdims=True)
        - unit * jnp.mean(along * unit, axis=-1, keepdims=True)
    )


def stage_kernel(*refs):
    n = len(refs) // 2
    for a, b in zip(refs[:n], refs[n:]):
        b[...] = a[...]


def stage(*arrays):
    return call(stage_kernel, "stage", arrays, [(x.shape, x.dtype) for x in arrays], limit=10)


def feed_forward_kernel(
    ids_ref, a0_ref, a1_ref, a2_ref, a3_ref, w0_ref, w1_ref, w2_ref, w3_ref, stream_ref,
    gain_ref, shift_ref, wi_ref, bi_ref, wo_ref,
    hid_ref, act_ref, gp_ref, mixed_ref, mine_ref, other_ref,
):
    half = mine_ref.shape[0]
    local = w0_ref.shape[0]
    core = ids_ref[1]
    gain, shift = gain_ref[...].astype(F32), shift_ref[...].astype(F32)
    packed = [a[...].astype(F32) for a in (a0_ref, a1_ref, a2_ref, a3_ref)]
    turned = [pltpu.roll(a, local, 1)[:, :local] for a in packed]
    for step in range(2):
        rows = at16((core if step else 1 - core) * half, half)
        first = core == (0 if step else 1)
        att = [jnp.where(first, a[:, :local], b).astype(BF16) for a, b in zip(packed, turned)]
        out = dot_nn(att[0], w0_ref[...]) + dot_nn(att[1], w1_ref[...])
        out = out + dot_nn(att[2], w2_ref[:local, :]) + dot_nn(att[3], w3_ref[:local, :])
        mixed = stream_ref[rows, :].astype(F32) + out
        if step:
            mixed_ref[...] = mixed
        unit, _ = norm_parts(mixed)
        hidden = (unit * gain + shift).astype(BF16)
        hid_ref[rows, :] = hidden
        inner = dot_nn(hidden, wi_ref[...]) + bi_ref[...].astype(F32)
        square = inner * inner
        turn = jnp.tanh(gelu_root * (inner + gelu_cubic * square * inner))
        lift = 0.5 * (1.0 + turn)
        slope = lift + 0.5 * inner * (1.0 - turn * turn) * (gelu_root * (1.0 + 3.0 * gelu_cubic * square))
        active = (inner * lift).astype(BF16)
        act_ref[rows, :] = active
        gp_ref[rows, :] = slope.astype(BF16)
        part = dot_nn(active, wo_ref[...]).astype(BF16)
        if step:
            mine_ref[...] = part
        else:
            other_ref[...] = part


def feed_forward(ids, atts, wos, stream, gain, shift, wi, bi, wo):
    rows, width = stream.shape
    units = wi.shape[1]
    half = rows // 2
    ins = (ids, *atts, *wos, stream, gain, shift, wi, bi, wo)
    outs = [
        ((rows, width), BF16),
        ((rows, units), BF16),
        ((rows, units), BF16),
        ((half, width), F32),
        ((half, width), BF16),
        ((half, width), BF16),
    ]
    return call(feed_forward_kernel, "feed_forward", ins, outs, smem=(0,), limit=32)


def second_norm_kernel(
    ids_ref, a_ref, b_ref, mixed_ref, cot_ref, pcot_ref, late_ref, g1_ref, s1_ref, ob_ref, g2_ref, s2_ref,
    content_ref, pick_ref, og_ref, sg_ref, sums_ref, cot_scr, out_scr,
):
    own, picks = cot_ref.shape[0], pcot_ref.shape[0]
    side = ids_ref[2]
    skip = late_ref.shape[0] - own - picks
    cot_scr[at16(side * own, own), :] = cot_ref[...].astype(F32)
    cot_scr[at16((1 - side) * own, own), :] = late_ref[skip : skip + own, :].astype(F32)
    a = pcot_ref[...].astype(F32)
    b = late_ref[skip + own :, :].astype(F32)
    cot_scr[2 * own : 2 * own + picks, :] = jnp.where(side == 0, a, b)
    cot_scr[2 * own + picks :, :] = jnp.where(side == 0, b, a)
    gain = g2_ref[...].astype(F32)
    unit, _ = norm_parts(mixed_ref[...])
    hidden = unit * g1_ref[...].astype(F32) + s1_ref[...].astype(F32)
    total = a_ref[...].astype(F32) + b_ref[...].astype(F32)
    unit, scale = norm_parts(hidden + total + ob_ref[...].astype(F32))
    out_scr[...] = unit * gain + s2_ref[...].astype(F32)
    content_ref[...] = out_scr[at16(side * own, own), :].astype(BF16)
    pick_ref[...] = jnp.where(
        side == 0, out_scr[2 * own : 2 * own + picks, :], out_scr[2 * own + picks :, :]
    ).astype(BF16)
    cot = cot_scr[...]
    grad = norm_back(cot, gain, unit, scale)
    low = grad.astype(BF16)
    og_ref[...] = low
    sg_ref[...] = grad
    sums_ref[...] = jnp.zeros_like(sums_ref)
    sums_ref[0:1, :] = row_sum(low.astype(F32))
    sums_ref[1:2, :] = row_sum(cot * unit)
    sums_ref[2:3, :] = row_sum(cot)


def second_norm(ids, a, b, mixed, cot, pcot, late, vectors):
    ins = (ids, a, b, mixed, cot, pcot, late, *vectors)
    shape = a.shape
    outs = [(cot.shape, BF16), (pcot.shape, BF16), (shape, BF16), (shape, F32), ((8, shape[1]), F32)]
    return call(
        second_norm_kernel, "second_norm", ins, outs, [pltpu.VMEM(shape, F32)] * 2, smem=(0,), limit=24
    )


def feed_backward_kernel(
    ids_ref, mine_ref, other_ref, gp_ref, wi_ref, wo_ref, ig_ref, og_ref, bm_ref, bo_ref, sums_ref
):
    half = mine_ref.shape[0]
    core = ids_ref[1]
    total = jnp.zeros((1, gp_ref.shape[1]), F32)
    for step in range(2):
        rows = at16((core if step else 1 - core) * half, half)
        og = mine_ref[...] if step else other_ref[...]
        og_ref[rows, :] = og
        grad = (dot_nt(og, wo_ref[...]) * gp_ref[rows, :].astype(F32)).astype(BF16)
        ig_ref[rows, :] = grad
        total = total + row_sum(grad.astype(F32))
        part = dot_nt(grad, wi_ref[...]).astype(BF16)
        if step:
            bm_ref[...] = part
        else:
            bo_ref[...] = part
    sums_ref[...] = total


def feed_backward(ids, mine, other, gp, wi, wo):
    rows, units = gp.shape
    half, width = mine.shape
    ins = (ids, mine, other, gp, wi, wo)
    outs = [
        ((rows, units), BF16),
        ((rows, width), BF16),
        ((half, width), BF16),
        ((half, width), BF16),
        ((1, units), F32),
    ]
    return call(feed_backward_kernel, "feed_backward", ins, outs, smem=(0,), limit=24)


def first_norm_kernel(a_ref, b_ref, sg_ref, mixed_ref, gain_ref, sums_in, mg_ref, ag_ref, sums_ref):
    grad = sg_ref[...] + a_ref[...].astype(F32) + b_ref[...].astype(F32)
    unit, scale = norm_parts(mixed_ref[...])
    out = norm_back(grad, gain_ref[...].astype(F32), unit, scale)
    mg_ref[...] = out
    ag_ref[...] = out.astype(BF16)
    sums_ref[...] = sums_in[...]
    sums_ref[3:4, :] = row_sum(grad * unit)
    sums_ref[4:5, :] = row_sum(grad)


def first_norm(a, b, sg, mixed, gain, sums):
    ins = (a, b, sg, mixed, gain, sums)
    shape = a.shape
    outs = [(shape, F32), (shape, BF16), (sums.shape, F32)]
    return call(first_norm_kernel, "first_norm", ins, outs, limit=16)


def add_kernel(a_ref, b_ref, o_ref):
    o_ref[...] = (a_ref[...].astype(F32) + b_ref[...].astype(F32)).astype(BF16)


def add(a, b):
    return call(add_kernel, "add", (a, b), [(a.shape, BF16)], limit=8)[0]


def row_split_kernel(own, picks, ids_ref, a_ref, b_ref, mg_ref, keep_ref, keep_pick_ref, send_ref, scr):
    side = ids_ref[2]
    scr[...] = (a_ref[...].astype(F32) + b_ref[...].astype(F32)).astype(BF16).astype(F32)
    first, second = scr[2 * own : 2 * own + picks, :], scr[2 * own + picks :, :]
    send_ref[0:own, :] = scr[at16((1 - side) * own, own), :].astype(BF16)
    send_ref[own:, :] = jnp.where(side == 0, second, first).astype(BF16)
    keep_ref[...] = scr[at16(side * own, own), :] + mg_ref[at16(side * own, own), :]
    grad = jnp.where(side == 0, mg_ref[2 * own : 2 * own + picks, :], mg_ref[2 * own + picks :, :])
    keep_pick_ref[...] = jnp.where(side == 0, first, second) + grad


def row_split(own, picks, ids, a, b, mg):
    width = a.shape[1]
    outs = [((own, width), F32), ((picks, width), F32), ((own + picks, width), BF16)]
    return call(
        functools.partial(row_split_kernel, own, picks), "row_split", (ids, a, b, mg), outs,
        [pltpu.VMEM(a.shape, F32)], smem=(0,), limit=12,
    )


def row_finish_kernel(keep_ref, keep_pick_ref, got_ref, content_ref, pick_ref):
    own = keep_ref.shape[0]
    content_ref[...] = keep_ref[...] + got_ref[:own, :].astype(F32)
    pick_ref[...] = keep_pick_ref[...] + got_ref[own:, :].astype(F32)


def row_finish(keep, keep_pick, got):
    outs = [(keep.shape, F32), (keep_pick.shape, F32)]
    return call(row_finish_kernel, "row_finish", (keep, keep_pick, got), outs, limit=8)


def pair_grad_kernel(bit, ids_ref, a_ref, b_ref, mine_ref, other_ref):
    half = mine_ref.shape[0]
    side = ids_ref[3 + bit]
    for step in range(2):
        cols = pl.ds(pl.multiple_of((side if step else 1 - side) * half, 128), half)
        out = dot_tn(a_ref[:, cols], b_ref[...]).astype(BF16)
        if step:
            mine_ref[...] = out
        else:
            other_ref[...] = out


def pair_grads(ids, a, b, bit):
    outs = [((a.shape[1] // 2, b.shape[1]), BF16)] * 2
    return call(functools.partial(pair_grad_kernel, bit), "pair_grads", (ids, a, b), outs, smem=(0,), limit=16)


def batch_swap(x, bit):
    n = lax.axis_size("batch")
    return lax.ppermute(x, "batch", [(i, i ^ (1 << bit)) for i in range(n)])


def after(x, *others):
    return lax.optimization_barrier((x, *others))[0]


class BatchSum:
    def __init__(self, mine, other, turn=0):
        self.bits = lax.axis_size("batch").bit_length() - 1
        self.order = [(i + turn) % self.bits for i in range(self.bits)]
        self.step, self.x, self.first = 0, mine, other
        self.coming, self.start, self.tied = None, 0, False

    def next_step(self):
        last = self.bits - 1
        if self.coming is None:
            return "first", 0, self.order[0]
        if self.step == 2 * last:
            return None
        self.step += 1
        step = self.step
        if step < last:
            return "split", self.order[step], self.order[step]
        if step == last:
            return "add", 0, self.order[last]
        bit = self.order[2 * last - step]
        if step == last + 1:
            return "add", 0, bit
        return "spread", self.order[2 * last + 1 - step], bit

    def got(self):
        return lax.slice_in_dim(self.coming, self.start, self.start + self.x.shape[0], axis=0)

    def finished(self):
        return self.step == 2 * self.bits - 2

    def total(self):
        side = (lax.axis_index("batch") >> self.order[0]) & 1
        x, y = self.x, self.got()
        return jnp.where(side == 0, jnp.concatenate([x, y]), jnp.concatenate([y, x]))


class WholeSum(BatchSum):
    def __init__(self, rows):
        super().__init__(rows, rows)

    def next_step(self):
        if self.coming is None:
            return "first", 0, 0
        if self.finished():
            return None
        self.step += 1
        return "add", 0, self.step

    def finished(self):
        return self.step == self.bits - 1


def up16(n):
    return -(-n // 16) * 16


def step_kernel(jobs, sizes, ids_ref, *refs):
    ins, outs = refs[: len(refs) - len(sizes)], refs[len(refs) - len(sizes) :]
    for kind, bit, x_at, got_at, start, to, sent, place in jobs:
        x = ins[x_at][...].astype(F32)
        if kind != "first":
            n = x.shape[0]
            side = ids_ref[3 + bit]
            y = ins[got_at][start : start + up16(n), :].astype(F32)[:n, :]
            if kind == "spread":
                low, high = jnp.where(side == 0, x, y), jnp.where(side == 0, y, x)
                x = jnp.concatenate([low, high], axis=0)
            else:
                x = (x + y).astype(BF16).astype(F32)
            if kind == "split":
                low, high = x[: n // 2, :], x[n // 2 :, :]
                outs[to][...] = jnp.where(side == 0, low, high).astype(BF16)
                x = jnp.where(side == 0, high, low)
            elif to is not None:
                outs[to][...] = x.astype(BF16)
        if sent is not None:
            n = x.shape[0]
            if n % 16:
                x = jnp.concatenate([x, jnp.zeros((up16(n) - n, x.shape[1]), F32)], axis=0)
            outs[sent][place : place + up16(n), :] = x.astype(BF16)


def round_of(chains, ids, *others):
    todo = []
    for c in chains:
        step = c.next_step()
        if step is not None:
            kind, half_bit, bit = step
            n = c.first.shape[0] if kind == "first" else c.x.shape[0]
            n = {"split": n // 2, "spread": 2 * n}.get(kind, n)
            todo.append((c, kind, half_bit, bit, n))
    groups = {}
    for item in todo:
        groups.setdefault(item[3], []).append(item)
    plain = all(item[4] % 8 == 0 and item[0].x.shape[0] % 8 == 0 for item in todo)
    width = chains[0].x.shape[1]
    sends = {}
    if plain:
        jobs, ins, outs = [], [ids], []

        def source(x):
            ins.append(x)
            return len(ins) - 2

        results = []
        for bit, items in groups.items():
            shared = len(items) > 1
            sent, place = None, 0
            if shared or items[0][1] == "split":
                outs.append(sum(up16(item[4]) for item in items))
                sent = len(outs) - 1
            for c, kind, half_bit, _, n in items:
                job_sent = sent
                if kind == "first":
                    if shared:
                        jobs.append((kind, 0, source(c.first), 0, 0, None, sent, place))
                    results.append((c, None, bit, sent, place, c.first))
                else:
                    outs.append(n)
                    to = len(outs) - 1
                    jobs.append((kind, half_bit, source(c.x), source(c.coming), c.start, to, sent, place))
                    results.append((c, to, bit, sent, place, None))
                place += up16(n)
        made = ()
        if jobs:
            shapes = [((n, width), BF16) for n in outs]
            made = call(functools.partial(step_kernel, jobs, outs), "step", ins, shapes, smem=(0,), limit=14)
        for c, to, bit, sent, place, first in results:
            if to is not None:
                c.x = made[to]
            c.start = place
            sends[bit] = made[sent] if sent is not None else (first if to is None else c.x)
    else:
        me = lax.axis_index("batch")
        for c, kind, half_bit, bit, n in todo:
            x = c.first
            if kind != "first":
                side = (me >> half_bit) & 1
                y = c.got()
                if kind == "spread":
                    c.x = jnp.where(side == 0, jnp.concatenate([c.x, y]), jnp.concatenate([y, c.x]))
                else:
                    c.x = c.x + y
                x = c.x
            if kind == "split":
                c.x = lax.dynamic_slice_in_dim(x, side * n, n, 0)
                x = lax.dynamic_slice_in_dim(x, (1 - side) * n, n, 0)
            c.start = 0
            if bit in sends:
                c.start = up16(sends[bit].shape[0])
                gap = jnp.zeros((c.start - sends[bit].shape[0], width), BF16)
                x = jnp.concatenate([sends[bit], gap, x])
            sends[bit] = x
    settled = [c for c in chains if c.finished() and not c.tied and all(c is not item[0] for item in todo)]
    bits = list(sends)
    tied = lax.optimization_barrier((*[sends[b] for b in bits], *[c.coming for c in settled], *others))
    for c, x in zip(settled, tied[len(bits) :]):
        c.coming, c.tied = x, True
    arrived = {b: batch_swap(x, b) for b, x in zip(bits, tied)}
    for c, _, _, bit, _ in todo:
        c.coming = arrived[bit]
    return tied[len(bits) + len(settled) :]


def finish_few_kernel(heads, head_size, start, a_ref, b_ref, wb, pb, sb, se, vec, small):
    small[...] = a_ref[...].astype(F32) + b_ref[start : start + 16, :].astype(F32)
    vec[...] = small[0:8, :]
    for h in range(heads):
        at = slice(h * head_size, (h + 1) * head_size)
        for i, to in enumerate((wb, pb, sb)):
            to[h : h + 1, :] = small[8 + i : 9 + i, at]
        for c in range(2):
            se[c, h : h + 1, :] = small[11 + c : 12 + c, at]


def finish_few(chain, heads, head_size):
    width = chain.x.shape[1]
    outs = [((heads, head_size), F32)] * 3 + [((2, heads, head_size), F32), ((8, width), F32)]
    return call(
        functools.partial(finish_few_kernel, heads, head_size, chain.start), "finish_few",
        (chain.x, chain.coming), outs, [pltpu.VMEM((16, width), F32)], limit=8,
    )


def place_head(pairs, start, head_size, side, scr, row):
    part = head_size // 2
    for i in range(4):
        for s in range(2):
            first = i * part + (start if s else 0)
            place = side if s == 0 else 1 - side
            scr[i, at16(row + place * part, part), :] = pairs[s][first : first + part, :].astype(F32)


def finish_kernel(heads, head_size, starts, ids_ref, *refs):
    n = heads - 1
    pairs, outs, scr, sems = refs[: 2 * n], refs[2 * n : 2 * n + 5], refs[2 * n + 5], refs[2 * n + 6]
    side = ids_ref[3]
    part = head_size // 2
    for h in range(n):
        place_head(pairs[2 * h : 2 * h + 2], starts[h], head_size, side, scr, h * head_size)
    backs = [
        pltpu.make_async_copy(scr.at[i], to.at[0 : n * head_size], sems.at[i]) for i, to in enumerate(outs[:4])
    ]
    for back in backs:
        back.start()
    half = heads * part
    for s in range(2):
        place = side if s == 0 else 1 - side
        start = 4 * part + (starts[0] if s else 0)
        outs[4][at16(place * half, half), :] = pairs[s][start : start + half, :].astype(F32)
    for back in backs:
        back.wait()


def finish_last_kernel(heads, head_size, start, ids_ref, a_ref, b_ref, *refs):
    outs, scr, sems = refs[4:8], refs[8], refs[9]
    place_head((a_ref, b_ref), start, head_size, ids_ref[3], scr, 0)
    backs = [
        pltpu.make_async_copy(scr.at[i], to.at[(heads - 1) * head_size : heads * head_size], sems.at[i])
        for i, to in enumerate(outs)
    ]
    for back in backs:
        back.start()
    for back in backs:
        back.wait()


def finish(ids, chains, heads, head_size):
    width = chains[0].x.shape[1]
    local = heads * head_size
    anywhere = pl.BlockSpec(memory_space=pl.ANY)
    pairs = [half for c in chains[:-1] for half in (c.x, c.coming)]
    shape = ((local, width), F32)
    *four, o = call(
        functools.partial(finish_kernel, heads, head_size, [c.start for c in chains[:-1]]), "finish",
        (ids, *pairs), [shape] * 5,
        [pltpu.VMEM((4, local - head_size, width), F32), pltpu.SemaphoreType.DMA((4,))],
        smem=(0,), limit=16, out_specs={i: anywhere for i in range(4)},
    )
    last = chains[-1]
    four = call(
        functools.partial(finish_last_kernel, heads, head_size, last.start), "finish_last",
        (ids, last.x, last.coming, *four), [shape] * 4,
        [pltpu.VMEM((4, head_size, width), F32), pltpu.SemaphoreType.DMA((4,))],
        smem=(0,), limit=8, in_specs={i: anywhere for i in range(3, 7)},
        out_specs={i: anywhere for i in range(4)}, aliases={i + 3: i for i in range(4)},
    )
    return (*four, o)


def on_device(
    content, query_stream, memory, has_memory, order_rank, targets, segments,
    query_weight, key_weight, value_weight, output_weight, relative_weight,
    word_bias, position_bias, segment_bias, segment_embed, first_gain, first_shift,
    inner_weight, inner_bias, outer_weight, outer_bias, second_gain, second_shift,
    content_cotangent, query_cotangent,
):
    parts = lax.axis_size("head")
    me = lax.axis_index("head")
    core_perm = [(i, i ^ 1) for i in range(parts)]
    x_perm = [(i, i ^ 2) for i in range(parts)]

    def swap_core(x):
        return lax.ppermute(x, "head", core_perm)

    def swap_x(x):
        return lax.ppermute(x, "head", x_perm)

    own, width = content.shape[1:]
    own_picks, own_memory = query_stream.shape[1], memory.shape[1]
    length, mem = own * parts, own_memory * parts
    keys = mem + length
    heads, head_size = word_bias.shape
    local = heads * head_size
    wide = local + head_size
    half = 2 * (own + own_picks)
    rows = 2 * half
    bits = lax.axis_size("batch").bit_length() - 1
    group = lax.axis_index("batch")
    ids = jnp.stack([me, me % 2, me // 2, *[(group >> i) & 1 for i in range(bits)]]).astype(jnp.int32)
    blocks = (
        (0, own, 0),
        (own, own, 2 * own),
        (2 * own, 2 * own_picks, None),
        (half, own, own),
        (half + own, own, 3 * own),
        (half + 2 * own, 2 * own_picks, None),
    )

    turned = (query_weight.T, key_weight.T, value_weight.T)
    con = content[0]
    con_x = swap_x(con)
    rest = pack(memory[0], query_stream[0])
    rest_x = swap_x(rest)
    con_core, rest_core = swap_core(con), swap_core(rest)
    table = jnp.asarray(position_rows(keys, length, width))
    small_ins = (
        has_memory, order_rank, targets, segments, word_bias, position_bias, segment_bias, segment_embed
    )
    rel, *tables = prepare(small_ins, table, relative_weight.T, own, own_picks, mem, wide)
    late = pack(output_weight, content_cotangent[0], after(query_cotangent[0], rest))
    con_x, rest_x, ids = lax.optimization_barrier((con_x, rest_x, ids, rel, late))[:3]
    con_diag, rest_diag = swap_core(con_x), swap_core(rest_x)
    late_x = swap_x(after(late, con_x))
    wo_core = swap_core(output_weight)
    p, att, col, qf, kc, v, stream, joined = attend_forward(
        blocks, ids, (con, con_core, con_x, con_diag), (rest, rest_core, rest_x, rest_diag), turned, rel, tables,
        heads, head_size, mem, rows,
    )
    bias = tables[2]
    att_x = swap_x(att)
    att_core = swap_core(att)
    late_diag = swap_core(after(late_x, att))
    wi, wo = stage(after(inner_weight, att), after(outer_weight, att))
    att_x = after(att_x, wi)
    att_diag = swap_core(att_x)

    def vector(x):
        return x.reshape(1, -1)

    hid, act, gp, mixed, part_mine, part_other = feed_forward(
        ids, (att, att_core, att_x, att_diag), (output_weight, wo_core, late_x, late_diag), stream,
        vector(first_gain), vector(first_shift), wi, vector(inner_bias), wo,
    )
    part_core = swap_core(part_other)
    chip_part = add(part_mine, part_core)
    vectors = [vector(x) for x in (first_gain, first_shift, outer_bias, second_gain, second_shift)]
    content_out, query_out, og_half, sg_half, sums = second_norm(
        ids, chip_part, swap_x(chip_part), mixed, content_cotangent[0], query_cotangent[0], late_x, vectors
    )
    ig, og, back_mine, back_other, inner_sums = feed_backward(
        ids, og_half, swap_core(og_half), gp, wi, wo
    )
    back_core = swap_core(back_other)
    outer_pair = pair_grads(ids, act, og, 0)
    chip_back = add(after(back_mine, outer_pair[0]), back_core)
    back_x = swap_x(chip_back)
    outer_chain = BatchSum(outer_pair[0], after(outer_pair[1], chip_back))
    round_of([outer_chain], ids)
    inner_chain = BatchSum(*pair_grads(ids, hid, after(ig, chip_back), 1), 1)
    ff_chains = [outer_chain, inner_chain]
    round_of([inner_chain], ids)
    mg_half, ag_half, sums = first_norm(chip_back, back_x, sg_half, mixed, vector(first_gain), sums)
    ag_other = swap_core(ag_half)
    sums_core = swap_core(sums)

    far = (v, kc, rel, qf, joined, stream, table)
    chains, kgs, vgs = list(ff_chains), [], []
    carried = None
    (tied,) = round_of([outer_chain], after(ids, ag_half), ids)
    (tied,) = round_of([inner_chain], tied, tied)
    for h in range(heads):
        outs = attend_backward(
            h, blocks, tied, p, far, (col, bias), (ag_half, ag_other, output_weight, att), carried,
            (sums, sums_core, inner_sums, *kgs, *vgs, *turned), head_size, length,
        )
        dq, small, kg, vg, mine, other = outs[:6]
        if h == 0:
            grads_in = outs[6:]
        carried = (*grads_in, dq, small)
        kgs.append(kg)
        vgs.append(vg)
        chains.append(BatchSum(mine, other))
        if h < heads - 1:
            (tied,) = round_of(chains, after(ids, dq), ids)
    row_mine, row_other, few = outs[6:]
    few_chain = WholeSum(few)
    heads_chains = chains[2:]
    chains.append(few_chain)
    (row_other,) = round_of(chains, after(ids, dq), row_other)
    keep, keep_pick, send = row_split(own, own_picks, ids, row_mine, swap_core(row_other), mg_half)
    (send,) = round_of(chains, ids, send)
    got = swap_x(send)
    totals = []
    few_sums = None
    while not heads_chains[-1].finished():
        carried = [got] if isinstance(got, jax.Array) else list(got)
        if not totals and all(c.finished() for c in ff_chains):
            totals = [c.total().astype(F32) for c in ff_chains]
        mixed_out = round_of(chains, ids, *carried, *totals)
        totals = list(mixed_out[len(carried) :])
        got = mixed_out[: len(carried)]
        if few_chain.finished() and few_sums is None and few_chain.tied:
            few_sums = finish_few(few_chain, heads, head_size)
        if len(got) == 1:
            got = row_finish(keep, keep_pick, got[0])
    content_grad, query_grad = got
    outer_sum, inner_sum = totals
    if few_sums is None:
        few_sums = finish_few(few_chain, heads, head_size)
    wb, pb, sb, se, vec = few_sums
    q, k, v_, r, o = finish(ids, heads_chains, heads, head_size)
    return (
        content_out[None],
        query_out[None],
        content_grad[None],
        query_grad[None],
        q.T, k.T, v_.T, o, r.T, wb, pb, sb, se,
        vec[3],
        vec[4],
        inner_sum,
        vec[5],
        outer_sum,
        vec[0],
        vec[1],
        vec[2],
    )


def solution(mesh):
    rows = P("batch", "head", None)
    ids = P("batch", None)
    columns = P(None, "head")
    by_head = P("head", None)
    table = P(None, "head", None)
    return jax.shard_map(
        on_device,
        mesh=mesh,
        in_specs=(
            rows, rows, rows, P("batch"), ids, ids, ids,
            columns, columns, columns, by_head, columns,
            by_head, by_head, by_head, table, P(), P(),
            columns, P("head"), by_head, P(), P(), P(), rows, rows,
        ),
        out_specs=(
            rows, rows, rows, rows,
            columns, columns, columns, by_head, columns,
            by_head, by_head, by_head, table, P(), P(),
            columns, P("head"), by_head, P(), P(), P(),
        ),
        check_vma=False,
    )
```

```python
import functools
import jax
import jax.numpy as jnp
import numpy as np
from jax import lax
from jax.experimental import pallas as pl
from jax.experimental.pallas import tpu as pltpu
from jax.sharding import PartitionSpec as P

masked_score = -1e30
norm_eps = 1e-05
gelu_root = 0.7978845608028654
gelu_cubic = 0.044715
hidden_key = 1e6
F32 = jnp.float32
BF16 = jnp.bfloat16
MIB = 1024 * 1024
SMEM_SPEC = pl.BlockSpec(memory_space=pltpu.SMEM)


def dot_nt(a, b):
    return lax.dot_general(a, b, (((1,), (1,)), ((), ())), preferred_element_type=F32)


def dot_nn(a, b):
    return lax.dot_general(a, b, (((1,), (0,)), ((), ())), preferred_element_type=F32)


def dot_tn(a, b):
    return lax.dot_general(a, b, (((0,), (0,)), ((), ())), preferred_element_type=F32)


def position_rows(key_count, length, width):
    steps = key_count - 1 - np.arange(key_count + length, dtype=np.float64)
    freqs = 10000.0 ** (-np.arange(0, width, 2, dtype=np.float64) / width)
    angles = steps[:, None] * freqs[None, :]
    return np.concatenate([np.sin(angles), np.cos(angles)], axis=1).astype(jnp.bfloat16)


def whole(shape):
    return pl.BlockSpec(shape, lambda *_: (0,) * len(shape))


def call(kernel, name, ins, outs, scratch=(), grid=(), in_specs=None, out_specs=None, smem=(), limit=24, aliases=None):
    kept = pl.BlockSpec(memory_space=pltpu.VMEM)
    specs = [kept if grid == () else whole(x.shape) for x in ins]
    for i in smem:
        specs[i] = SMEM_SPEC
    for i, spec in (in_specs or {}).items():
        specs[i] = spec
    to = [kept if grid == () else whole(s) for s, _ in outs]
    for i, spec in (out_specs or {}).items():
        to[i] = spec
    return pl.pallas_call(
        kernel,
        grid=grid,
        in_specs=specs,
        out_specs=to,
        out_shape=[jax.ShapeDtypeStruct(s, t) for s, t in outs],
        scratch_shapes=list(scratch),
        input_output_aliases=aliases or {},
        compiler_params=pltpu.CompilerParams(vmem_limit_bytes=limit * MIB),
        cost_estimate=pl.CostEstimate(flops=0, bytes_accessed=0, transcendentals=0),
        name=name,
    )(*ins)


def at16(i, n):
    return pl.ds(pl.multiple_of(i, 16), n)


def row_sum(x):
    return jnp.sum(x, axis=0, keepdims=True)


def pack_kernel(*refs):
    start = 0
    for part in refs[:-1]:
        refs[-1][start : start + part.shape[0], :] = part[...]
        start += part.shape[0]


def pack(*ins):
    shape = (sum(x.shape[0] for x in ins), ins[0].shape[1])
    return call(pack_kernel, "pack", ins, [(shape, BF16)], limit=60)[0]


def prepare_kernel(
    own, own_picks, mem,
    present_ref, rank_ref, pick_ref, seg_ref, wb_ref, pb_ref, sb_ref, se_ref, table_ref, w_ref,
    rel_ref, col_ref, key_ref, bias_ref, embed_ref, row_ref,
):
    local, wide = w_ref.shape[0], rel_ref.shape[1]
    head_size = wb_ref.shape[1]
    length = rank_ref.shape[1]
    half = 2 * (own + own_picks)
    rel_ref[...] = jnp.zeros_like(rel_ref)
    rel_ref[:, :local] = dot_nt(table_ref[...], w_ref[...]).astype(BF16)

    bias_ref[...] = jnp.zeros_like(bias_ref)
    sources = (wb_ref[...], pb_ref[...], sb_ref[...], se_ref[:, 0, :], se_ref[:, 1, :])
    for i, source in enumerate(sources):
        source = source.astype(F32)
        for k in range(source.shape[0]):
            bias_ref[i : i + 1, k * head_size : (k + 1) * head_size] = source[k : k + 1, :]
    turned = bias_ref[...].T
    lane = lax.broadcasted_iota(jnp.int32, embed_ref.shape, 1)
    left = lane < wide
    lane = jnp.where(left, lane, lane - wide)
    same, other = turned[:, 3:4], turned[:, 4:5]
    a = jnp.where(left, same, other)
    b = jnp.where(left, other, same)
    is_zero = (lane == local) | (lane == local + 1)
    is_one = (lane == local + 2) | (lane == local + 3)
    embed_ref[...] = jnp.where(is_zero, a, jnp.where(is_one, b, 0.0)).astype(BF16)

    ranks = rank_ref[...].astype(F32)
    labels = seg_ref[...].astype(F32)
    row = lax.broadcasted_iota(jnp.int32, (8, length), 0)
    content_col = jnp.where(row == 0, ranks + 1.0, jnp.where(row == 1, labels, 0.0)).T
    key_ref[...] = content_col
    pick_row = jnp.broadcast_to(pick_ref[...].astype(F32), (8, pick_ref.shape[1]))
    picks = pick_row.T[:, 0:1]
    spot = lax.broadcasted_iota(jnp.int32, (picks.shape[0], length), 1).astype(F32)
    hit = spot == picks
    pick_rank = jnp.sum(jnp.where(hit, ranks, 0.0), axis=1, keepdims=True)
    pick_label = jnp.sum(jnp.where(hit, labels, 0.0), axis=1, keepdims=True)
    lane8 = lax.broadcasted_iota(jnp.int32, (picks.shape[0], 8), 1)
    shift = (length - 1.0) - picks
    pick_col = jnp.where(
        lane8 == 0, pick_rank, jnp.where(lane8 == 1, pick_label, jnp.where(lane8 == 2, shift, 0.0))
    )
    for c in range(2):
        for x in range(2):
            owner = 2 * x + c
            to = c * half + x * own
            col_ref[to : to + own, :] = content_col[owner * own : (owner + 1) * own, :]
            to = c * half + 2 * own + x * own_picks
            col_ref[to : to + own_picks, :] = pick_col[owner * own_picks : (owner + 1) * own_picks, :]
    memory_rank = jnp.where(present_ref[0] > 0, -1.0, hidden_key)
    row_ref[:, :mem] = jnp.full((8, mem), memory_rank, F32)
    row_ref[:, mem:] = jnp.broadcast_to(ranks, (8, length))


def prepare(small, table, w, own, own_picks, mem, wide):
    length = 4 * own
    outs = [
        ((table.shape[0], wide), BF16),
        ((4 * (own + own_picks), 8), F32),
        ((length, 8), F32),
        ((8, wide), F32),
        ((wide, 2 * wide), BF16),
        ((8, mem + length), F32),
    ]
    return call(
        functools.partial(prepare_kernel, own, own_picks, mem), "prepare", (*small, table, w), outs,
        smem=(0,), limit=60,
    )


def attend_forward_kernel(
    blocks, head_size, mem,
    ids_ref, c0_ref, c1_ref, c2_ref, c3_ref, m0_ref, m1_ref, m2_ref, m3_ref,
    wq_ref, wk_ref, wv_ref, rel_ref, col_in, key_ref, bias_ref, embed_ref, row_ref,
    p_ref, att_ref, col_ref, *refs,
):
    acc_ref, score_scr, rel_scr, place_scr, qf_ref, kc_ref, v_ref, stream_ref, joined_ref, sems = refs[5:]
    near = (qf_ref, kc_ref, v_ref, stream_ref, joined_ref)
    backs = [pltpu.make_async_copy(a, b, sems.at[i]) for i, (a, b) in enumerate(zip(near, refs[:5]))]
    h = pl.program_id(0)
    keys, wide = kc_ref.shape
    local = wq_ref.shape[0]
    length = keys - mem
    own, own_mem = length // 4, mem // 4
    own_picks = m0_ref.shape[0] - own_mem
    half = stream_ref.shape[0] // 2

    @pl.when(h == 0)
    def _():
        core, side = ids_ref[1], ids_ref[2]
        cores = (core, 1 - core, core, 1 - core)
        sides = (side, side, 1 - side, 1 - side)
        content = (c0_ref, c1_ref, c2_ref, c3_ref)
        others = (m0_ref, m1_ref, m2_ref, m3_ref)
        for i in range(4):
            owner = 2 * sides[i] + cores[i]
            rows = content[i][...]
            stream_ref[at16(cores[i] * half + sides[i] * own, own), :] = rows
            joined_ref[at16(mem + owner * own, own), :] = rows
            joined_ref[at16(owner * own_mem, own_mem), :] = others[i][:own_mem, :]
        for i in range(2):
            a = others[i][own_mem:, :].astype(F32)
            b = others[i + 2][own_mem:, :].astype(F32)
            first = jnp.where(side == 0, a, b)
            second = jnp.where(side == 0, b, a)
            both = jnp.concatenate([first, second], axis=0).astype(BF16)
            stream_ref[at16(cores[i] * half + 2 * own, 2 * own_picks), :] = both

        col_ref[...] = col_in[...]
        qf_ref[...] = jnp.zeros_like(qf_ref)
        qf_ref[:, :local] = dot_nt(stream_ref[...], wq_ref[...])
        v_ref[...] = jnp.zeros_like(v_ref)
        v_ref[:, :local] = dot_nt(joined_ref[...], wv_ref[...]).astype(BF16)
        key_label = jnp.concatenate([jnp.zeros((mem, 1), F32), key_ref[:, 1:2]], axis=0)
        lane = lax.broadcasted_iota(jnp.int32, (keys, wide), 1)
        is_zero = (lane == local) | (lane == local + 1)
        is_one = (lane == local + 2) | (lane == local + 3)
        kc_ref[...] = jnp.where(is_zero, 1.0 - key_label, jnp.where(is_one, key_label, 0.0)).astype(BF16)
        kc_ref[:, :local] = dot_nt(joined_ref[...], wk_ref[...]).astype(BF16)
        acc_ref[...] = jnp.zeros_like(acc_ref)
        for back in backs:
            back.start()

    lane = lax.broadcasted_iota(jnp.int32, (1, wide), 1)
    mine = (lane >= h * head_size) & (lane < (h + 1) * head_size)
    hi_lane = (lane == local) | (lane == local + 2)
    lo_lane = (lane == local + 1) | (lane == local + 3)
    qf = qf_ref[...]
    word = jnp.where(mine, (qf + bias_ref[0:1, :]).astype(BF16).astype(F32) * 0.125, 0.0)
    place = jnp.where(mine, qf + bias_ref[1:2, :], 0.0).astype(BF16) * 0.125
    label = jnp.where(mine, (qf + bias_ref[2:3, :]) * 0.125, 0.0)
    label_hi = label.astype(BF16)
    label_lo = (label - label_hi.astype(F32)).astype(BF16)
    both = dot_nn(label_hi, embed_ref[...]) + dot_nn(label_lo, embed_ref[...])
    pair = jnp.where(col_ref[:, 1:2] == 0, both[:, :wide], both[:, wide:])
    pair_hi = pair.astype(BF16).astype(F32)
    query = jnp.where(hi_lane, pair_hi, jnp.where(lo_lane, pair - pair_hi, word)).astype(BF16)
    score_scr[...] = dot_nt(query, kc_ref[...])
    place_scr[...] = place

    limit_row = row_ref[0:1, :]
    for start, size, position in blocks:
        place = place_scr[start : start + size, :]
        if position is not None:
            base = length - position - size
            width = keys + size
            rel_scr[:size, :width] = dot_nt(place, rel_ref[base : base + width, :])
        else:
            rel_scr[:size, :] = dot_nt(place, rel_ref[...])
        chunk = 32 if size % 32 == 0 else 16
        for low in range(0, size, chunk):
            blk = slice(start + low, start + low + chunk)
            if position is not None:
                rel = rel_scr[low : low + chunk, :width]
                rel = pltpu.roll(rel, width - (size - 1) + low, 1, stride=1, stride_axis=0)
            else:
                rel = rel_scr[low : low + chunk, :]
                shift = col_ref[blk, 2:3].astype(jnp.int32)
                bit = (length - 1).bit_length()
                while bit > 0:
                    bit -= 1
                    far = 1 << bit
                    left = pltpu.roll(rel, rel.shape[1] - far, 1)
                    rel = jnp.where(((shift >> bit) & 1) == 1, left, rel)
                    rel = rel[:, : -(-(keys + far - 1) // 128) * 128]
            scores = score_scr[blk, :] + rel[:, :keys]
            scores = jnp.where(limit_row < col_ref[blk, 0:1], scores, masked_score)
            top = jnp.max(scores, axis=-1, keepdims=True)
            powers = jnp.exp(scores - top)
            total = jnp.sum(powers, axis=-1, keepdims=True)
            p_ref[0, blk, :] = powers.astype(BF16)
            lane8 = lax.broadcasted_iota(jnp.int32, (chunk, 8), 1)
            col_ref[blk, :] = jnp.where(lane8 == 4 + h, 1.0 / total, col_ref[blk, :])
    lane8 = lax.broadcasted_iota(jnp.int32, col_ref.shape, 1)
    inverse = jnp.sum(jnp.where(lane8 == 4 + h, col_ref[...], 0.0), axis=1, keepdims=True)
    att = dot_nn(p_ref[0], v_ref[...]) * inverse
    acc_ref[...] = jnp.where(mine, att, acc_ref[...])

    @pl.when(h == pl.num_programs(0) - 1)
    def _():
        att_ref[:, :local] = acc_ref[:half, :local].astype(BF16)
        att_ref[:, local:] = acc_ref[half:, :local].astype(BF16)
        for back in backs:
            back.wait()


def attend_forward(blocks, ids, content, others, weights, rel, tables, heads, head_size, mem, rows):
    own, width = content[0].shape
    keys = 4 * own + mem
    wide = rel.shape[1]
    ins = (ids, *content, *others, *weights, rel, *tables)
    outs = [
        ((heads, rows, keys), BF16),
        ((rows // 2, 2 * heads * head_size), BF16),
        ((rows, 8), F32),
        ((rows, wide), F32),
        ((keys, wide), BF16),
        ((keys, wide), BF16),
        ((rows, width), BF16),
        ((keys, width), BF16),
    ]
    anywhere = pl.BlockSpec(memory_space=pl.ANY)
    return call(
        functools.partial(attend_forward_kernel, blocks, head_size, mem),
        "attend_forward", ins, outs,
        [
            pltpu.VMEM((rows, wide), F32),
            pltpu.VMEM((rows, keys), F32),
            pltpu.VMEM((own, rel.shape[0]), F32),
            pltpu.VMEM((rows, wide), BF16),
            *[pltpu.VMEM(shape, kind) for shape, kind in outs[3:]],
            pltpu.SemaphoreType.DMA((5,)),
        ],
        grid=(heads,), smem=(0,), limit=60,
        out_specs={0: pl.BlockSpec((1, rows, keys), lambda h: (h, 0, 0)), **{i: anywhere for i in range(3, 8)}},
    )


def second_half(packed):
    local = packed.shape[1] // 2
    return pltpu.roll(packed.astype(F32), local, 1)[:, :local].astype(BF16)


def attend_backward_kernel(
    h, heads, blocks, head_size, length, *refs,
):
    refs = list(refs)
    ids_ref, p_hbm = refs[:2]
    far, refs = refs[2:9], refs[9:]
    col_ref, bias_ref = refs[:2]
    refs = refs[2:]
    if h == 0:
        ag_ref, ago_ref, wo_ref, att_ref = refs[:4]
        refs = refs[4:]
    else:
        da_ref, dat_ref, dq_in, small_in = refs[:4]
        refs = refs[4:]
    if h == heads - 1:
        norm_ref, norm_core_ref, inner_ref = refs[:3]
        kgs, vgs = refs[3 : 2 + heads], refs[2 + heads : 1 + 2 * heads]
        weights_hbm = refs[1 + 2 * heads : 4 + 2 * heads]
        refs = refs[4 + 2 * heads :]
    dq_ref, small_ref, kg_ref, vg_ref, mine_ref, other_ref = refs[:6]
    refs = refs[6:]
    if h == 0:
        da_ref, dat_ref = refs[:2]
        refs = refs[2:]
    if h == heads - 1:
        row_mine, row_other, few_ref = refs[:3]
        refs = refs[3:]
    s_scr, rg_acc, qt_scr, all_ref, extra_scr, ag_scr = refs[:6]
    p_ref, near, sems = refs[6], refs[7:14], refs[14]
    chance_scr, word_scr, place_scr, wide_scr = refs[15:19]
    v_ref, kc_ref, rel_ref, qf_ref, joined_ref, stream_ref, table_ref = near
    copies = [pltpu.make_async_copy(p_hbm.at[h], p_ref, sems.at[7])]
    copies += [pltpu.make_async_copy(a, b, sems.at[i]) for i, (a, b) in enumerate(zip(far, near))]
    if h == heads - 1:
        weights, key_scr = refs[19:22], refs[22]
        copies += [
            pltpu.make_async_copy(a, b, sems.at[8 + i]) for i, (a, b) in enumerate(zip(weights_hbm, weights))
        ]
    for copy in copies:
        copy.start()
    keys, wide = kc_ref.shape
    total_rel = rel_ref.shape[0]
    local = da_ref.shape[1]
    at = slice(h * head_size, (h + 1) * head_size)
    side = ids_ref[3]
    part = head_size // 2

    if h == 0:
        half = ag_ref.shape[0]
        core = ids_ref[1]
        ag_scr[at16(core * half, half), :] = ag_ref[...]
        ag_scr[at16((1 - core) * half, half), :] = ago_ref[...]
        ag = ag_scr[...]
        grads = dot_nt(ag, wo_ref[...]).astype(BF16).astype(F32)
        turned = dot_nt(wo_ref[...], ag).astype(BF16).astype(F32)
        inverse = col_ref[...].T
        lane = lax.broadcasted_iota(jnp.int32, (1, local), 1)
        factor = jnp.zeros((grads.shape[0], 1), F32)
        for k in range(heads):
            of = slice(k * head_size, (k + 1) * head_size)
            here = (lane >= k * head_size) & (lane < (k + 1) * head_size)
            factor = jnp.where(here, col_ref[:, 4 + k : 5 + k], factor)
            dat_ref[of, :] = (turned[of, :] * inverse[4 + k : 5 + k, :]).astype(BF16)
        da_ref[...] = (grads * factor).astype(BF16)
        packed = att_ref[...]
        extra = dot_tn(packed[:, :local], ag[:half, :]) + dot_tn(second_half(packed), ag[half:, :])
        extra_scr[...] = extra.astype(BF16)

    lane = lax.broadcasted_iota(jnp.int32, (1, wide), 1)
    mine = (lane >= h * head_size) & (lane < (h + 1) * head_size)
    copies[0].wait()
    vg = dot_nn(dat_ref[at, :], p_ref[...]).astype(BF16)
    vg_ref[...] = vg
    for copy in copies[1:5]:
        copy.wait()
    rg_acc[...] = jnp.zeros_like(rg_acc)
    sums = [jnp.zeros((1, wide), F32) for _ in range(5)]
    chance_scr[...] = dot_nt(jnp.where(mine[:, :local], da_ref[...], 0), v_ref[:, :local])
    step = 32
    for start in range(0, p_ref.shape[0], step):
        blk = slice(start, start + step)
        soft = p_ref[blk, :].astype(F32)
        chance = chance_scr[blk, :]
        inner = jnp.sum(chance * soft, axis=-1, keepdims=True) * col_ref[blk, 4 + h : 5 + h]
        s_scr[blk, :] = (soft * (chance - inner)).astype(BF16)
    word_scr[...] = dot_nn(s_scr[...], kc_ref[...]) * 0.125
    for start, size, position in blocks:
        blk = slice(start, start + size)
        score = s_scr[blk, :]
        place = (qf_ref[blk, :] + bias_ref[1:2, :]).astype(BF16) * 0.125
        if position is not None:
            base = length - position - size
            width = keys + size
            turn = (
                lax.broadcasted_iota(jnp.int32, (size, size), 0)
                + lax.broadcasted_iota(jnp.int32, (size, size), 1)
                == size - 1
            ).astype(F32).astype(BF16)
            wider = jnp.concatenate([dot_nn(turn, score), jnp.zeros((size, width - keys), F32)], axis=1)
            wider = pltpu.roll(wider, 0, 1, stride=1, stride_axis=0).astype(BF16)
            placed = dot_nn(wider, rel_ref[base : base + width, :]) * 0.125
            high = placed.astype(BF16)
            low = (placed - high.astype(F32)).astype(BF16)
            place_scr[blk, :] = dot_nn(turn, high) + dot_nn(turn, low)
            place = dot_nn(turn, place)
        else:
            base = 0
            width = total_rel
            for low in range(0, size, 16):
                to = slice(start + low, start + low + 16)
                left = col_ref[to, 2:3].astype(jnp.int32)
                moved = s_scr[to, :].astype(F32)
                bit = 0
                while (1 << bit) < length:
                    need = -(-(keys + (2 << bit) - 1) // 128) * 128
                    if need > moved.shape[1]:
                        moved = jnp.concatenate(
                            [moved, jnp.zeros((16, need - moved.shape[1]), F32)], axis=1
                        )
                    moved = jnp.where(((left >> bit) & 1) == 1, pltpu.roll(moved, 1 << bit, 1), moved)
                    bit += 1
                wide_scr[low : low + 16, :] = moved.astype(BF16)
            wider = wide_scr[...]
            place_scr[blk, :] = dot_nn(wider, rel_ref[...]) * 0.125
            place = place.astype(F32)
        rg_acc[:, base : base + width] += dot_nn(place.T[at, :].astype(BF16), wider)
    step = 152
    for start in range(0, p_ref.shape[0], step):
        blk = slice(start, start + step)
        word, placed = word_scr[blk, :], place_scr[blk, :]
        row_label = col_ref[blk, 1:2]
        zero_key = word[:, local : local + 1]
        one_key = word[:, local + 2 : local + 3]
        same = jnp.where(row_label == 0, zero_key, one_key)
        other = jnp.where(row_label == 0, one_key, zero_key)
        label = same * bias_ref[3:4, :] + other * bias_ref[4:5, :]
        query_label = qf_ref[blk, :] + bias_ref[2:3, :]
        terms = (word, placed, label, query_label * same, query_label * other)
        for i, term in enumerate(terms):
            sums[i] = sums[i] + row_sum(term)
        word_scr[blk, :] = jnp.where(mine, word + placed + label, 0.0)
    dq = word_scr[...]
    if h == 0:
        dq_ref[...] = dq[:, :local].astype(BF16)
    else:
        dq_ref[...] = dq_in[...] + dq[:, :local].astype(BF16)
    qt_scr[...] = dq.T[at, :].astype(BF16)
    small_ref[...] = jnp.zeros_like(small_ref) if h == 0 else small_in[...]
    for i in range(5):
        old = jnp.zeros((1, wide), F32) if h == 0 else small_in[i : i + 1, :]
        small_ref[i : i + 1, :] = jnp.where(mine, sums[i], old)
    word_q = (qf_ref[...] + bias_ref[0:1, :]).astype(BF16).astype(F32) * 0.125
    kg = dot_nn(word_q.T[at, :].astype(BF16), s_scr[...]).astype(BF16)
    kg_ref[...] = kg
    for copy in copies[5:8]:
        copy.wait()
    all_ref[2] = dot_nn(vg, joined_ref[...]).astype(BF16)
    all_ref[0] = dot_nn(qt_scr[...], stream_ref[...]).astype(BF16)
    all_ref[1] = dot_nn(kg, joined_ref[...]).astype(BF16)
    all_ref[3] = dot_nn(rg_acc[...].astype(BF16), table_ref[...]).astype(BF16)
    if h == heads - 1:
        for copy in copies[8:]:
            copy.wait()
        half = row_mine.shape[0]
        core = ids_ref[1]
        own = key_scr.shape[0] // 4
        mem = keys - key_scr.shape[0]
        wq_ref, wk_ref, wv_ref = weights
        key_grad = jnp.concatenate([k[:, mem:].astype(F32) for k in (*kgs, kg_ref)], axis=0).T.astype(BF16)
        value_grad = jnp.concatenate([k[:, mem:].astype(F32) for k in (*vgs, vg_ref)], axis=0).T.astype(BF16)
        key_scr[...] = dot_nn(key_grad, wk_ref[...]) + dot_nn(value_grad, wv_ref[...])
        for step in range(2):
            c = core if step else 1 - core
            rows_part = dot_nn(dq_ref[at16(c * half, half), :], wq_ref[...])
            to = row_mine if step else row_other
            to[0:own, :] = (rows_part[:own] + key_scr[at16(c * own, own), :]).astype(BF16)
            to[own : 2 * own, :] = (rows_part[own : 2 * own] + key_scr[at16((2 + c) * own, own), :]).astype(BF16)
            to[2 * own :, :] = rows_part[2 * own :].astype(BF16)
        norm = norm_ref[...] + norm_core_ref[...]
        width = norm.shape[1]
        tail = jnp.concatenate([small_ref[...], jnp.zeros((8, width - wide), F32)], axis=1)
        row = lax.broadcasted_iota(jnp.int32, (8, width), 0)
        norm = jnp.where(row == 5, inner_ref[...], norm)
        few_ref[...] = jnp.concatenate([norm, tail], axis=0).astype(BF16)
    extra = extra_scr.shape[0] // 2
    for i in range(4):
        to = slice(i * part, (i + 1) * part)
        mine_ref[to, :] = all_ref[i, at16(side * part, part), :]
        other_ref[to, :] = all_ref[i, at16((1 - side) * part, part), :]
    if mine_ref.shape[0] > 4 * part:
        to = slice(4 * part, 4 * part + extra)
        mine_ref[to, :] = extra_scr[at16(side * extra, extra), :]
        other_ref[to, :] = extra_scr[at16((1 - side) * extra, extra), :]


def attend_backward(h, blocks, ids, p, far, shared, first, carried, final, head_size, length):
    heads, rows, keys = p.shape
    wide, total_rel = far[2].shape[1], far[2].shape[0]
    width = far[4].shape[1]
    local = heads * head_size
    last = h == heads - 1
    extra = local if h == 0 else 0
    part = (4 * head_size + extra) // 2
    ins = (ids, p, *far, *shared, *(first if h == 0 else carried), *(final if last else ()))
    outs = [
        ((rows, local), BF16),
        ((8, wide), F32),
        ((head_size, keys), BF16),
        ((head_size, keys), BF16),
        ((part, width), BF16),
        ((part, width), BF16),
    ]
    if h == 0:
        outs += [((rows, local), BF16), ((local, rows), BF16)]
    anywhere = pl.BlockSpec(memory_space=pl.ANY)
    in_specs = {i: anywhere for i in range(1, 2 + len(far))}
    scratch = []
    if last:
        outs += [((rows // 2, width), BF16)] * 2 + [((16, width), BF16)]
        in_specs.update({len(ins) - 1 - i: anywhere for i in range(3)})
        scratch = [pltpu.VMEM((local, width), BF16)] * 3 + [pltpu.VMEM((length, width), F32)]
    return call(
        functools.partial(attend_backward_kernel, h, heads, blocks, head_size, length),
        f"attend_backward_{h}", ins, outs,
        [
            pltpu.VMEM((rows, keys), BF16),
            pltpu.VMEM((head_size, total_rel), F32),
            pltpu.VMEM((head_size, rows), BF16),
            pltpu.VMEM((4, head_size, width), BF16),
            pltpu.VMEM((max(extra, 32), width), BF16),
            pltpu.VMEM((rows if h == 0 else 16, width), BF16),
            pltpu.VMEM((rows, keys), BF16),
            *[pltpu.VMEM(x.shape, x.dtype) for x in far],
            pltpu.SemaphoreType.DMA((11,)),
            pltpu.VMEM((rows, keys), F32),
            pltpu.VMEM((rows, wide), F32),
            pltpu.VMEM((rows, wide), F32),
            pltpu.VMEM((blocks[2][1], total_rel), BF16),
            *scratch,
        ],
        smem=(0,), limit=50, in_specs=in_specs,
    )


def norm_parts(x):
    center = x - jnp.mean(x, axis=-1, keepdims=True)
    scale = lax.rsqrt(jnp.mean(center * center, axis=-1, keepdims=True) + norm_eps)
    return center * scale, scale


def norm_back(grad, gain, unit, scale):
    along = grad * gain
    return scale * (
        along
        - jnp.mean(along, axis=-1, keepdims=True)
        - unit * jnp.mean(along * unit, axis=-1, keepdims=True)
    )


def stage_kernel(*refs):
    n = len(refs) // 2
    for a, b in zip(refs[:n], refs[n:]):
        b[...] = a[...]


def stage(*arrays):
    return call(stage_kernel, "stage", arrays, [(x.shape, x.dtype) for x in arrays], limit=10)


def feed_forward_kernel(
    ids_ref, a0_ref, a1_ref, a2_ref, a3_ref, w0_ref, w1_ref, w2_ref, w3_ref, stream_ref,
    gain_ref, shift_ref, wi_ref, bi_ref, wo_ref,
    hid_ref, act_ref, gp_ref, mixed_ref, mine_ref, other_ref,
):
    half = mine_ref.shape[0]
    local = w0_ref.shape[0]
    core = ids_ref[1]
    gain, shift = gain_ref[...].astype(F32), shift_ref[...].astype(F32)
    packed = [a[...].astype(F32) for a in (a0_ref, a1_ref, a2_ref, a3_ref)]
    turned = [pltpu.roll(a, local, 1)[:, :local] for a in packed]
    for step in range(2):
        rows = at16((core if step else 1 - core) * half, half)
        first = core == (0 if step else 1)
        att = [jnp.where(first, a[:, :local], b).astype(BF16) for a, b in zip(packed, turned)]
        out = dot_nn(att[0], w0_ref[...]) + dot_nn(att[1], w1_ref[...])
        out = out + dot_nn(att[2], w2_ref[:local, :]) + dot_nn(att[3], w3_ref[:local, :])
        mixed = stream_ref[rows, :].astype(F32) + out
        if step:
            mixed_ref[...] = mixed
        unit, _ = norm_parts(mixed)
        hidden = (unit * gain + shift).astype(BF16)
        hid_ref[rows, :] = hidden
        inner = dot_nn(hidden, wi_ref[...]) + bi_ref[...].astype(F32)
        square = inner * inner
        turn = jnp.tanh(gelu_root * (inner + gelu_cubic * square * inner))
        lift = 0.5 * (1.0 + turn)
        slope = lift + 0.5 * inner * (1.0 - turn * turn) * (gelu_root * (1.0 + 3.0 * gelu_cubic * square))
        active = (inner * lift).astype(BF16)
        act_ref[rows, :] = active
        gp_ref[rows, :] = slope.astype(BF16)
        part = dot_nn(active, wo_ref[...]).astype(BF16)
        if step:
            mine_ref[...] = part
        else:
            other_ref[...] = part


def feed_forward(ids, atts, wos, stream, gain, shift, wi, bi, wo):
    rows, width = stream.shape
    units = wi.shape[1]
    half = rows // 2
    ins = (ids, *atts, *wos, stream, gain, shift, wi, bi, wo)
    outs = [
        ((rows, width), BF16),
        ((rows, units), BF16),
        ((rows, units), BF16),
        ((half, width), F32),
        ((half, width), BF16),
        ((half, width), BF16),
    ]
    return call(feed_forward_kernel, "feed_forward", ins, outs, smem=(0,), limit=32)


def before_norm_kernel(
    ids_ref, mixed_ref, cot_ref, pcot_ref, late_ref, g1_ref, s1_ref, ob_ref, base_ref, cots_ref
):
    own, picks = cot_ref.shape[0], pcot_ref.shape[0]
    side = ids_ref[2]
    skip = late_ref.shape[0] - own - picks
    cots_ref[at16(side * own, own), :] = cot_ref[...].astype(F32)
    cots_ref[at16((1 - side) * own, own), :] = late_ref[skip : skip + own, :].astype(F32)
    a = pcot_ref[...].astype(F32)
    b = late_ref[skip + own :, :].astype(F32)
    cots_ref[2 * own : 2 * own + picks, :] = jnp.where(side == 0, a, b)
    cots_ref[2 * own + picks :, :] = jnp.where(side == 0, b, a)
    unit, _ = norm_parts(mixed_ref[...])
    base_ref[...] = unit * g1_ref[...].astype(F32) + s1_ref[...].astype(F32) + ob_ref[...].astype(F32)


def before_norm(ids, mixed, cot, pcot, late, vectors):
    outs = [(mixed.shape, F32)] * 2
    ins = (ids, mixed, cot, pcot, late, *vectors)
    return call(before_norm_kernel, "before_norm", ins, outs, smem=(0,), limit=12)


def second_norm_kernel(
    own, picks, ids_ref, a_ref, b_ref, base_ref, cots_ref, g2_ref, s2_ref,
    content_ref, pick_ref, og_ref, sg_ref, sums_ref, out_scr,
):
    side = ids_ref[2]
    gain = g2_ref[...].astype(F32)
    total = a_ref[...].astype(F32) + b_ref[...].astype(F32)
    unit, scale = norm_parts(base_ref[...] + total)
    out_scr[...] = unit * gain + s2_ref[...].astype(F32)
    content_ref[...] = out_scr[at16(side * own, own), :].astype(BF16)
    pick_ref[...] = jnp.where(
        side == 0, out_scr[2 * own : 2 * own + picks, :], out_scr[2 * own + picks :, :]
    ).astype(BF16)
    cot = cots_ref[...]
    grad = norm_back(cot, gain, unit, scale)
    low = grad.astype(BF16)
    og_ref[...] = low
    sg_ref[...] = grad
    sums_ref[...] = jnp.zeros_like(sums_ref)
    sums_ref[0:1, :] = row_sum(low.astype(F32))
    sums_ref[1:2, :] = row_sum(cot * unit)
    sums_ref[2:3, :] = row_sum(cot)


def second_norm(ids, a, b, base, cots, own, picks, gain, shift):
    ins = (ids, a, b, base, cots, gain, shift)
    shape, width = a.shape, a.shape[1]
    outs = [((own, width), BF16), ((picks, width), BF16), (shape, BF16), (shape, F32), ((8, width), F32)]
    return call(
        functools.partial(second_norm_kernel, own, picks), "second_norm", ins, outs,
        [pltpu.VMEM(shape, F32)], smem=(0,), limit=20,
    )


def feed_backward_kernel(
    ids_ref, mine_ref, other_ref, gp_ref, wi_ref, wo_ref, ig_ref, og_ref, bm_ref, bo_ref, sums_ref
):
    half = mine_ref.shape[0]
    core = ids_ref[1]
    total = jnp.zeros((1, gp_ref.shape[1]), F32)
    for step in range(2):
        rows = at16((core if step else 1 - core) * half, half)
        og = mine_ref[...] if step else other_ref[...]
        og_ref[rows, :] = og
        grad = (dot_nt(og, wo_ref[...]) * gp_ref[rows, :].astype(F32)).astype(BF16)
        ig_ref[rows, :] = grad
        total = total + row_sum(grad.astype(F32))
        part = dot_nt(grad, wi_ref[...]).astype(BF16)
        if step:
            bm_ref[...] = part
        else:
            bo_ref[...] = part
    sums_ref[...] = total


def feed_backward(ids, mine, other, gp, wi, wo):
    rows, units = gp.shape
    half, width = mine.shape
    ins = (ids, mine, other, gp, wi, wo)
    outs = [
        ((rows, units), BF16),
        ((rows, width), BF16),
        ((half, width), BF16),
        ((half, width), BF16),
        ((1, units), F32),
    ]
    return call(feed_backward_kernel, "feed_backward", ins, outs, smem=(0,), limit=24)


def first_norm_kernel(a_ref, b_ref, sg_ref, mixed_ref, gain_ref, sums_in, mg_ref, ag_ref, sums_ref):
    grad = sg_ref[...] + a_ref[...].astype(F32) + b_ref[...].astype(F32)
    unit, scale = norm_parts(mixed_ref[...])
    out = norm_back(grad, gain_ref[...].astype(F32), unit, scale)
    mg_ref[...] = out
    ag_ref[...] = out.astype(BF16)
    sums_ref[...] = sums_in[...]
    sums_ref[3:4, :] = row_sum(grad * unit)
    sums_ref[4:5, :] = row_sum(grad)


def first_norm(a, b, sg, mixed, gain, sums):
    ins = (a, b, sg, mixed, gain, sums)
    shape = a.shape
    outs = [(shape, F32), (shape, BF16), (sums.shape, F32)]
    return call(first_norm_kernel, "first_norm", ins, outs, limit=16)


def add_kernel(a_ref, b_ref, o_ref):
    o_ref[...] = (a_ref[...].astype(F32) + b_ref[...].astype(F32)).astype(BF16)


def add(a, b):
    return call(add_kernel, "add", (a, b), [(a.shape, BF16)], limit=8)[0]


def row_split_kernel(own, picks, ids_ref, a_ref, b_ref, mg_ref, keep_ref, keep_pick_ref, send_ref, scr):
    side = ids_ref[2]
    scr[...] = (a_ref[...].astype(F32) + b_ref[...].astype(F32)).astype(BF16).astype(F32)
    first, second = scr[2 * own : 2 * own + picks, :], scr[2 * own + picks :, :]
    send_ref[0:own, :] = scr[at16((1 - side) * own, own), :].astype(BF16)
    send_ref[own:, :] = jnp.where(side == 0, second, first).astype(BF16)
    keep_ref[...] = scr[at16(side * own, own), :] + mg_ref[at16(side * own, own), :]
    grad = jnp.where(side == 0, mg_ref[2 * own : 2 * own + picks, :], mg_ref[2 * own + picks :, :])
    keep_pick_ref[...] = jnp.where(side == 0, first, second) + grad


def row_split(own, picks, ids, a, b, mg):
    width = a.shape[1]
    outs = [((own, width), F32), ((picks, width), F32), ((own + picks, width), BF16)]
    return call(
        functools.partial(row_split_kernel, own, picks), "row_split", (ids, a, b, mg), outs,
        [pltpu.VMEM(a.shape, F32)], smem=(0,), limit=12,
    )


def row_finish_kernel(keep_ref, keep_pick_ref, got_ref, content_ref, pick_ref):
    own = keep_ref.shape[0]
    content_ref[...] = keep_ref[...] + got_ref[:own, :].astype(F32)
    pick_ref[...] = keep_pick_ref[...] + got_ref[own:, :].astype(F32)


def row_finish(keep, keep_pick, got):
    outs = [(keep.shape, F32), (keep_pick.shape, F32)]
    return call(row_finish_kernel, "row_finish", (keep, keep_pick, got), outs, limit=8)


def pair_grad_kernel(bit, ids_ref, a_ref, b_ref, mine_ref, other_ref):
    half = mine_ref.shape[0]
    side = ids_ref[3 + bit]
    for step in range(2):
        cols = pl.ds(pl.multiple_of((side if step else 1 - side) * half, 128), half)
        out = dot_tn(a_ref[:, cols], b_ref[...]).astype(BF16)
        if step:
            mine_ref[...] = out
        else:
            other_ref[...] = out


def pair_grads(ids, a, b, bit):
    outs = [((a.shape[1] // 2, b.shape[1]), BF16)] * 2
    return call(functools.partial(pair_grad_kernel, bit), "pair_grads", (ids, a, b), outs, smem=(0,), limit=16)


def batch_swap(x, bit):
    n = lax.axis_size("batch")
    return lax.ppermute(x, "batch", [(i, i ^ (1 << bit)) for i in range(n)])


def after(x, *others):
    return lax.optimization_barrier((x, *others))[0]


class BatchSum:
    def __init__(self, mine, other, order=(0, 1, 2)):
        self.bits = lax.axis_size("batch").bit_length() - 1
        self.order = [*order, *range(len(order), self.bits)]
        self.step, self.x, self.first = 0, mine, other
        self.coming, self.start, self.tied = None, 0, False

    def next_step(self):
        last = self.bits - 1
        if self.coming is None:
            return "first", 0, self.order[0]
        if self.step == 2 * last:
            return None
        self.step += 1
        step = self.step
        if step < last:
            return "split", self.order[step], self.order[step]
        if step == last:
            return "add", 0, self.order[last]
        bit = self.order[2 * last - step]
        if step == last + 1:
            return "add", 0, bit
        return "spread", self.order[2 * last + 1 - step], bit

    def got(self):
        return lax.slice_in_dim(self.coming, self.start, self.start + self.x.shape[0], axis=0)

    def finished(self):
        return self.step == 2 * self.bits - 2

    def total(self):
        side = (lax.axis_index("batch") >> self.order[0]) & 1
        x, y = self.x, self.got()
        return jnp.where(side == 0, jnp.concatenate([x, y]), jnp.concatenate([y, x]))


class WholeSum(BatchSum):
    def __init__(self, rows):
        super().__init__(rows, rows)

    def next_step(self):
        if self.coming is None:
            return "first", 0, 0
        if self.finished():
            return None
        self.step += 1
        return "add", 0, self.step

    def finished(self):
        return self.step == self.bits - 1


def up16(n):
    return -(-n // 16) * 16


def step_kernel(jobs, sizes, ids_ref, *refs):
    ins, outs = refs[: len(refs) - len(sizes)], refs[len(refs) - len(sizes) :]
    for kind, bit, x_at, got_at, start, to, sent, place in jobs:
        x = ins[x_at][...].astype(F32)
        if kind != "first":
            n = x.shape[0]
            side = ids_ref[3 + bit]
            y = ins[got_at][start : start + up16(n), :].astype(F32)[:n, :]
            if kind == "spread":
                low, high = jnp.where(side == 0, x, y), jnp.where(side == 0, y, x)
                x = jnp.concatenate([low, high], axis=0)
            else:
                x = (x + y).astype(BF16).astype(F32)
            if kind == "split":
                low, high = x[: n // 2, :], x[n // 2 :, :]
                outs[to][...] = jnp.where(side == 0, low, high).astype(BF16)
                x = jnp.where(side == 0, high, low)
            elif to is not None:
                outs[to][...] = x.astype(BF16)
        if sent is not None:
            n = x.shape[0]
            if n % 16:
                x = jnp.concatenate([x, jnp.zeros((up16(n) - n, x.shape[1]), F32)], axis=0)
            outs[sent][place : place + up16(n), :] = x.astype(BF16)


def round_of(chains, ids, *others):
    todo = []
    for c in chains:
        step = c.next_step()
        if step is not None:
            kind, half_bit, bit = step
            n = c.first.shape[0] if kind == "first" else c.x.shape[0]
            n = {"split": n // 2, "spread": 2 * n}.get(kind, n)
            todo.append((c, kind, half_bit, bit, n))
    groups = {}
    for item in todo:
        groups.setdefault(item[3], []).append(item)
    plain = all(item[4] % 8 == 0 and item[0].x.shape[0] % 8 == 0 for item in todo)
    width = chains[0].x.shape[1]
    sends = {}
    if plain:
        jobs, ins, outs = [], [ids], []

        def source(x):
            ins.append(x)
            return len(ins) - 2

        results = []
        for bit, items in groups.items():
            shared = len(items) > 1
            sent, place = None, 0
            if shared or items[0][1] == "split":
                outs.append(sum(up16(item[4]) for item in items))
                sent = len(outs) - 1
            for c, kind, half_bit, _, n in items:
                job_sent = sent
                if kind == "first":
                    if shared:
                        jobs.append((kind, 0, source(c.first), 0, 0, None, sent, place))
                    results.append((c, None, bit, sent, place, c.first))
                else:
                    outs.append(n)
                    to = len(outs) - 1
                    jobs.append((kind, half_bit, source(c.x), source(c.coming), c.start, to, sent, place))
                    results.append((c, to, bit, sent, place, None))
                place += up16(n)
        made = ()
        if jobs:
            shapes = [((n, width), BF16) for n in outs]
            made = call(functools.partial(step_kernel, jobs, outs), "step", ins, shapes, smem=(0,), limit=14)
        for c, to, bit, sent, place, first in results:
            if to is not None:
                c.x = made[to]
            c.start = place
            sends[bit] = made[sent] if sent is not None else (first if to is None else c.x)
    else:
        me = lax.axis_index("batch")
        for c, kind, half_bit, bit, n in todo:
            x = c.first
            if kind != "first":
                side = (me >> half_bit) & 1
                y = c.got()
                if kind == "spread":
                    c.x = jnp.where(side == 0, jnp.concatenate([c.x, y]), jnp.concatenate([y, c.x]))
                else:
                    c.x = c.x + y
                x = c.x
            if kind == "split":
                c.x = lax.dynamic_slice_in_dim(x, side * n, n, 0)
                x = lax.dynamic_slice_in_dim(x, (1 - side) * n, n, 0)
            c.start = 0
            if bit in sends:
                c.start = up16(sends[bit].shape[0])
                gap = jnp.zeros((c.start - sends[bit].shape[0], width), BF16)
                x = jnp.concatenate([sends[bit], gap, x])
            sends[bit] = x
    settled = [c for c in chains if c.finished() and not c.tied and all(c is not item[0] for item in todo)]
    bits = list(sends)
    tied = lax.optimization_barrier((*[sends[b] for b in bits], *[c.coming for c in settled], *others))
    for c, x in zip(settled, tied[len(bits) :]):
        c.coming, c.tied = x, True
    arrived = {b: batch_swap(x, b) for b, x in zip(bits, tied)}
    for c, _, _, bit, _ in todo:
        c.coming = arrived[bit]
    return tied[len(bits) + len(settled) :]


def finish_few_kernel(heads, head_size, start, a_ref, b_ref, wb, pb, sb, se, vec, small):
    small[...] = a_ref[...].astype(F32) + b_ref[start : start + 16, :].astype(F32)
    vec[...] = small[0:8, :]
    for h in range(heads):
        at = slice(h * head_size, (h + 1) * head_size)
        for i, to in enumerate((wb, pb, sb)):
            to[h : h + 1, :] = small[8 + i : 9 + i, at]
        for c in range(2):
            se[h, c : c + 1, :] = small[11 + c : 12 + c, at]


def finish_few(chain, heads, head_size):
    width = chain.x.shape[1]
    outs = [((heads, head_size), F32)] * 3 + [((heads, 2, head_size), F32), ((8, width), F32)]
    return call(
        functools.partial(finish_few_kernel, heads, head_size, chain.start), "finish_few",
        (chain.x, chain.coming), outs, [pltpu.VMEM((16, width), F32)], limit=8,
    )


def place_head(pairs, start, head_size, side, scr, row):
    part = head_size // 2
    for i in range(4):
        for s in range(2):
            first = i * part + (start if s else 0)
            place = side if s == 0 else 1 - side
            scr[i, at16(row + place * part, part), :] = pairs[s][first : first + part, :].astype(F32)


def finish_kernel(heads, head_size, starts, ids_ref, *refs):
    n = heads - 1
    pairs, outs, scr, sems = refs[: 2 * n], refs[2 * n : 2 * n + 5], refs[2 * n + 5], refs[2 * n + 6]
    side = ids_ref[3]
    part = head_size // 2
    for h in range(n):
        place_head(pairs[2 * h : 2 * h + 2], starts[h], head_size, side, scr, h * head_size)
    backs = [
        pltpu.make_async_copy(scr.at[i], to.at[0 : n * head_size], sems.at[i]) for i, to in enumerate(outs[:4])
    ]
    for back in backs:
        back.start()
    half = heads * part
    for s in range(2):
        place = side if s == 0 else 1 - side
        start = 4 * part + (starts[0] if s else 0)
        outs[4][at16(place * half, half), :] = pairs[s][start : start + half, :].astype(F32)
    for back in backs:
        back.wait()


def finish_last_kernel(heads, head_size, start, ids_ref, a_ref, b_ref, *refs):
    outs, scr, sems = refs[4:8], refs[8], refs[9]
    place_head((a_ref, b_ref), start, head_size, ids_ref[3], scr, 0)
    backs = [
        pltpu.make_async_copy(scr.at[i], to.at[(heads - 1) * head_size : heads * head_size], sems.at[i])
        for i, to in enumerate(outs)
    ]
    for back in backs:
        back.start()
    for back in backs:
        back.wait()


def finish(ids, chains, heads, head_size):
    width = chains[0].x.shape[1]
    local = heads * head_size
    anywhere = pl.BlockSpec(memory_space=pl.ANY)
    pairs = [half for c in chains[:-1] for half in (c.x, c.coming)]
    shape = ((local, width), F32)
    *four, o = call(
        functools.partial(finish_kernel, heads, head_size, [c.start for c in chains[:-1]]), "finish",
        (ids, *pairs), [shape] * 5,
        [pltpu.VMEM((4, local - head_size, width), F32), pltpu.SemaphoreType.DMA((4,))],
        smem=(0,), limit=16, out_specs={i: anywhere for i in range(4)},
    )
    last = chains[-1]
    four = call(
        functools.partial(finish_last_kernel, heads, head_size, last.start), "finish_last",
        (ids, last.x, last.coming, *four), [shape] * 4,
        [pltpu.VMEM((4, head_size, width), F32), pltpu.SemaphoreType.DMA((4,))],
        smem=(0,), limit=8, in_specs={i: anywhere for i in range(3, 7)},
        out_specs={i: anywhere for i in range(4)}, aliases={i + 3: i for i in range(4)},
    )
    return (*four, o)


def on_device(
    content, query_stream, memory, has_memory, order_rank, targets, segments,
    query_weight, key_weight, value_weight, output_weight, relative_weight,
    word_bias, position_bias, segment_bias, segment_embed, first_gain, first_shift,
    inner_weight, inner_bias, outer_weight, outer_bias, second_gain, second_shift,
    content_cotangent, query_cotangent,
):
    parts = lax.axis_size("head")
    me = lax.axis_index("head")
    core_perm = [(i, i ^ 1) for i in range(parts)]
    x_perm = [(i, i ^ 2) for i in range(parts)]

    def swap_core(x):
        return lax.ppermute(x, "head", core_perm)

    def swap_x(x):
        return lax.ppermute(x, "head", x_perm)

    own, width = content.shape[1:]
    own_picks, own_memory = query_stream.shape[1], memory.shape[1]
    length, mem = own * parts, own_memory * parts
    keys = mem + length
    heads, head_size = word_bias.shape
    local = heads * head_size
    wide = local + head_size
    half = 2 * (own + own_picks)
    rows = 2 * half
    bits = lax.axis_size("batch").bit_length() - 1
    group = lax.axis_index("batch")
    ids = jnp.stack([me, me % 2, me // 2, *[(group >> i) & 1 for i in range(bits)]]).astype(jnp.int32)
    blocks = (
        (0, own, 0),
        (own, own, 2 * own),
        (2 * own, 2 * own_picks, None),
        (half, own, own),
        (half + own, own, 3 * own),
        (half + 2 * own, 2 * own_picks, None),
    )

    turned = (query_weight.T, key_weight.T, value_weight.T)
    con = content[0]
    con_x = swap_x(con)
    rest = pack(memory[0], query_stream[0])
    rest_x = swap_x(rest)
    con_core, rest_core = swap_core(con), swap_core(rest)
    table = jnp.asarray(position_rows(keys, length, width))
    small_ins = (
        has_memory, order_rank, targets, segments, word_bias, position_bias, segment_bias,
        jnp.swapaxes(segment_embed, 0, 1),
    )
    rel, *tables = prepare(small_ins, table, relative_weight.T, own, own_picks, mem, wide)
    late = pack(output_weight, content_cotangent[0], after(query_cotangent[0], rest))
    con_x, rest_x, ids = lax.optimization_barrier((con_x, rest_x, ids, rel, late))[:3]
    con_diag, rest_diag = swap_core(con_x), swap_core(rest_x)
    late_x = swap_x(after(late, con_x))
    wo_core = swap_core(output_weight)
    p, att, col, qf, kc, v, stream, joined = attend_forward(
        blocks, ids, (con, con_core, con_x, con_diag), (rest, rest_core, rest_x, rest_diag), turned, rel, tables,
        heads, head_size, mem, rows,
    )
    bias = tables[2]
    att_x = swap_x(att)
    att_core = swap_core(att)
    late_diag = swap_core(after(late_x, att))
    wi, wo = stage(after(inner_weight, att), after(outer_weight, att))
    att_x = after(att_x, wi)
    att_diag = swap_core(att_x)

    def vector(x):
        return x.reshape(1, -1)

    hid, act, gp, mixed, part_mine, part_other = feed_forward(
        ids, (att, att_core, att_x, att_diag), (output_weight, wo_core, late_x, late_diag), stream,
        vector(first_gain), vector(first_shift), wi, vector(inner_bias), wo,
    )
    part_core = swap_core(part_other)
    chip_part = add(part_mine, part_core)
    vectors = [vector(x) for x in (first_gain, first_shift, outer_bias)]
    base, cots = before_norm(ids, mixed, content_cotangent[0], query_cotangent[0], late_x, vectors)
    content_out, query_out, og_half, sg_half, sums = second_norm(
        ids, chip_part, swap_x(chip_part), base, cots, own, own_picks, vector(second_gain), vector(second_shift)
    )
    ig, og, back_mine, back_other, inner_sums = feed_backward(
        ids, og_half, swap_core(og_half), gp, wi, wo
    )
    back_core = swap_core(back_other)
    outer_pair = pair_grads(ids, act, og, 0)
    chip_back = add(after(back_mine, outer_pair[0]), back_core)
    back_x = swap_x(chip_back)
    outer_chain = BatchSum(outer_pair[0], after(outer_pair[1], chip_back), (0, 2, 1))
    round_of([outer_chain], ids)
    inner_chain = BatchSum(*pair_grads(ids, hid, after(ig, chip_back), 1), (1, 0, 2))
    ff_chains = [outer_chain, inner_chain]
    round_of([inner_chain], ids)
    mg_half, ag_half, sums = first_norm(chip_back, back_x, sg_half, mixed, vector(first_gain), sums)
    ag_other = swap_core(ag_half)
    sums_core = swap_core(sums)

    far = (v, kc, rel, qf, joined, stream, table)
    chains, kgs, vgs = list(ff_chains), [], []
    carried = None
    (tied,) = round_of([outer_chain], after(ids, ag_half), ids)
    (tied,) = round_of([inner_chain], tied, tied)
    for h in range(heads):
        outs = attend_backward(
            h, blocks, tied, p, far, (col, bias), (ag_half, ag_other, output_weight, att), carried,
            (sums, sums_core, inner_sums, *kgs, *vgs, *turned), head_size, length,
        )
        dq, small, kg, vg, mine, other = outs[:6]
        if h == 0:
            grads_in = outs[6:]
        carried = (*grads_in, dq, small)
        kgs.append(kg)
        vgs.append(vg)
        chains.append(BatchSum(mine, other))
        if h < heads - 1:
            (tied,) = round_of(chains, after(ids, dq), ids)
    row_mine, row_other, few = outs[6:]
    few_chain = WholeSum(few)
    heads_chains = chains[2:]
    chains.append(few_chain)
    (row_other,) = round_of(chains, after(ids, dq), row_other)
    keep, keep_pick, send = row_split(own, own_picks, ids, row_mine, swap_core(row_other), mg_half)
    (send,) = round_of(chains, ids, send)
    got = swap_x(send)
    totals = []
    few_sums = None
    while not heads_chains[-1].finished():
        carried = [got] if isinstance(got, jax.Array) else list(got)
        if not totals and all(c.finished() for c in ff_chains):
            totals = [c.total().astype(F32) for c in ff_chains]
        mixed_out = round_of(chains, ids, *carried, *totals)
        totals = list(mixed_out[len(carried) :])
        got = mixed_out[: len(carried)]
        if few_chain.finished() and few_sums is None and few_chain.tied:
            few_sums = finish_few(few_chain, heads, head_size)
        if len(got) == 1:
            got = row_finish(keep, keep_pick, got[0])
    content_grad, query_grad = got
    outer_sum, inner_sum = totals
    if few_sums is None:
        few_sums = finish_few(few_chain, heads, head_size)
    wb, pb, sb, se, vec = few_sums
    se = jnp.swapaxes(se, 0, 1)
    q, k, v_, r, o = finish(ids, heads_chains, heads, head_size)
    return (
        content_out[None],
        query_out[None],
        content_grad[None],
        query_grad[None],
        q.T, k.T, v_.T, o, r.T, wb, pb, sb, se,
        vec[3],
        vec[4],
        inner_sum,
        vec[5],
        outer_sum,
        vec[0],
        vec[1],
        vec[2],
    )


def solution(mesh):
    rows = P("batch", "head", None)
    ids = P("batch", None)
    columns = P(None, "head")
    by_head = P("head", None)
    table = P(None, "head", None)
    return jax.shard_map(
        on_device,
        mesh=mesh,
        in_specs=(
            rows, rows, rows, P("batch"), ids, ids, ids,
            columns, columns, columns, by_head, columns,
            by_head, by_head, by_head, table, P(), P(),
            columns, P("head"), by_head, P(), P(), P(), rows, rows,
        ),
        out_specs=(
            rows, rows, rows, rows,
            columns, columns, columns, by_head, columns,
            by_head, by_head, by_head, table, P(), P(),
            columns, P("head"), by_head, P(), P(), P(),
        ),
        check_vma=False,
    )
```
